32 devices in a mesh: gx: 8 (over y, x, core), gy: 4 (over z).
Axes of the slice: x: 2, y: 2, z: 4, core: 2. Of those that a mesh axis runs over, the one named last changes fastest.
Arguments:
- right_side: bfloat16 [8, 4, 896, 128], P('gx', 'gy')
- schur_offdiag: bfloat16 [8, 4, 896, 896], P('gx', 'gy'), may hold values from -0.125 to 0.125
- schur_diag: float32 [8, 4, 896], P('gx', 'gy'), may hold values from 1.5 to 3
- trace_offdiag: bfloat16 [8, 4, 896, 896], P('gx', 'gy'), may hold values from -0.0390625 to 0.0390625
- trace_diag: float32 [8, 4, 896], P('gx', 'gy'), may hold values from 0.3 to 0.7
- couplings: bfloat16 [8, 4, 4, 128, 128], P('gx', 'gy'), may hold values from -0.375 to 0.375
- margin_rows: int32 [8, 4, 4, 128], P('gx', 'gy'), may hold values from 0 to 895, as said below
- deflation: bfloat16 [8, 4, 8, 896], P('gx', 'gy'), may hold values from -0.59765625 to 0.59765625
- coarse_inverse: float32 [256, 256], P(('gx', 'gy'))
- coarse_map: int32 [256], replicated, may hold values from 0 to 255, each once
Outputs:
- solution: float32 [8, 4, 896, 128], P('gx', 'gy')
- residual: float32 [8, 4, 896, 128], P('gx', 'gy')
The draws below stay inside these ranges and needn't reach their ends.
Inputs may be any that keep to these rules, and one draw needn't show every extreme that they name: `margin_rows`: the 512 rows of one subdomain's four lists are all distinct. `coarse_map`: every coarse number appears once.
All inputs are finite; a program needn't handle non-finite values.
Results may differ from the reference program's by a relative error of at most 0.022.
Values may be sent and summed in bfloat16 or wider, within the bound.
A program may use at most 64 MiB of HBM per device.

```python
import math
import jax
import jax.numpy as jnp
from jax import lax

ROWS = 896
OV = 128
K = 8
SRC = 128
ITERS = 3
SUBX = 8
SUBY = 4
NC = 256


def draw_right_side(key, part):
    key_vals = jax.random.fold_in(key, 11)
    key_rows = jax.random.fold_in(key, 12)
    key_cols = jax.random.fold_in(key, 13)
    row_scale = jnp.exp(jax.random.uniform(key_rows, (SUBX, SUBY, ROWS, 1), jnp.float32, jnp.log(0.3), jnp.log(3.0)))
    col_scale = jnp.exp(jax.random.uniform(key_cols, (1, 1, 1, SRC), jnp.float32, jnp.log(0.3), jnp.log(3.0)))
    values = jax.random.truncated_normal(key_vals, -4.0, 4.0, (SUBX, SUBY, ROWS, SRC), jnp.float32)
    return (values * row_scale * col_scale).astype(jnp.bfloat16)


def draw_margin_rows(key, part):
    keys = jax.random.split(jax.random.fold_in(key, 21), SUBX * SUBY)
    lists = jax.vmap(lambda single: jax.random.permutation(single, ROWS)[:4 * OV])(keys)
    return lists.reshape(SUBX, SUBY, 4, OV).astype(jnp.int32)


def draw_coarse_inverse(key, part):
    key_vals = jax.random.fold_in(key, 31)
    noise = jax.random.normal(key_vals, (NC, NC), jnp.float32)
    return jnp.eye(NC, dtype=jnp.float32) + noise * (1.0 / NC ** 0.5)


def block_scale(stream_key, dims, cuts, least, high):
    factor_of, own = 1.0, jax.random.fold_in(stream_key, 6)
    for axis_at, shards_of in cuts:
        draws = jnp.exp(jax.random.uniform(jax.random.fold_in(own, axis_at), (shards_of,), jnp.float32, least / len(cuts), high / len(cuts)))
        factor_of = factor_of * jnp.repeat(draws, dims[axis_at] // shards_of).reshape([-1 if axis == axis_at else 1 for axis in range(len(dims))])
    return factor_of


def normal_values(key, dims, spread, reach, cuts=(), kind=jnp.bfloat16):
    gain = block_scale(key, dims, cuts, -0.22, 0.18) if cuts else 1.0
    entries = jax.random.normal(key, dims, jnp.float32) * spread * gain
    return jnp.minimum(jnp.maximum(entries, -reach), reach).astype(kind)


def setup_inputs(seed: int = 0) -> dict:
    arg_keys = jax.random.split(jax.random.key(seed), 11)
    right_side = draw_right_side(jax.random.fold_in(arg_keys[10], 71), 0)
    schur_offdiag = normal_values(arg_keys[1], (SUBX, SUBY, ROWS, ROWS), (3 * ROWS) ** -0.5, 0.125, ((0, 8), (1, 4)))
    schur_diag = jnp.clip(jnp.exp(math.log(3.0) - 0.6931472 * jax.random.uniform(arg_keys[2], (SUBX, SUBY, ROWS), jnp.float32) ** block_scale(arg_keys[2], (SUBX, SUBY, ROWS), ((0, 8), (1, 4)), -0.2, 0.2)), 1.5, 3.0)
    trace_offdiag = normal_values(arg_keys[3], (SUBX, SUBY, ROWS, ROWS), (30 * ROWS) ** -0.5, 0.0390625, ((0, 8), (1, 4)))
    trace_diag = jnp.clip(jnp.exp(math.log(0.7) - 0.8472978 * jax.random.uniform(arg_keys[4], (SUBX, SUBY, ROWS), jnp.float32) ** block_scale(arg_keys[4], (SUBX, SUBY, ROWS), ((0, 8), (1, 4)), -0.2, 0.2)), 0.3, 0.7)
    couplings = normal_values(arg_keys[5], (SUBX, SUBY, 4, OV, OV), (2 * OV) ** -0.5, 0.375, ((0, 8), (1, 4)))
    margin_rows = draw_margin_rows(jax.random.fold_in(arg_keys[10], 71), 0)
    deflation = normal_values(arg_keys[7], (SUBX, SUBY, K, ROWS), 0.1, 0.59765625, ((0, 8), (1, 4)))
    coarse_inverse = draw_coarse_inverse(jax.random.fold_in(arg_keys[10], 71), 0)
    coarse_map = jax.random.permutation(arg_keys[9], NC).astype(jnp.int32)
    return dict(right_side=right_side, schur_offdiag=schur_offdiag, schur_diag=schur_diag, trace_offdiag=trace_offdiag, trace_diag=trace_diag, couplings=couplings, margin_rows=margin_rows, deflation=deflation, coarse_inverse=coarse_inverse, coarse_map=coarse_map)


def shift_grid(arr, axis, offset):
    count = arr.shape[axis]
    zeros = jnp.zeros_like(lax.slice_in_dim(arr, 0, 1, axis=axis))
    if offset == 1:
        return jnp.concatenate([zeros, lax.slice_in_dim(arr, 0, count - 1, axis=axis)], axis=axis)
    return jnp.concatenate([lax.slice_in_dim(arr, 1, count, axis=axis), zeros], axis=axis)


def local_products(mats, fields):
    shape = fields.shape
    flat_mats = mats.reshape((-1,) + mats.shape[2:])
    flat_fields = fields.reshape((-1,) + shape[2:])
    out = lax.map(lambda pair: jnp.dot(pair[0], pair[1], preferred_element_type=jnp.float32), (flat_mats, flat_fields))
    return out.reshape(shape)


def pick_rows(field, rows):
    return field[rows]


def add_rows(result, rows, values):
    return result.at[rows.reshape(-1)].add(-values.reshape(-1, values.shape[-1]))


def reference(right_side, schur_offdiag, schur_diag, trace_offdiag, trace_diag, couplings, margin_rows, deflation, coarse_inverse, coarse_map):
    blocks_wide = couplings.astype(jnp.float32)
    vectors = deflation.astype(jnp.float32)
    coarse_cols = jnp.take(coarse_inverse, coarse_map, axis=1)

    def apply_schur(field):
        rounded = lax.optimization_barrier(field.astype(jnp.bfloat16))
        result = schur_diag[..., None] * rounded.astype(jnp.float32) + local_products(schur_offdiag, rounded)
        sent_rows = jax.vmap(jax.vmap(pick_rows))(rounded, margin_rows)
        received = jnp.stack([shift_grid(sent_rows[:, :, 1], 0, 1), shift_grid(sent_rows[:, :, 0], 0, -1),
                              shift_grid(sent_rows[:, :, 3], 1, 1), shift_grid(sent_rows[:, :, 2], 1, -1)], axis=2)
        coupled = jnp.einsum("xydab,xydbs->xydas", blocks_wide, received.astype(jnp.float32))
        return jax.vmap(jax.vmap(add_rows))(result, margin_rows, coupled)

    def apply_prec(field):
        rounded = lax.optimization_barrier(field.astype(jnp.bfloat16))
        result = trace_diag[..., None] * rounded.astype(jnp.float32) + local_products(trace_offdiag, rounded)
        coarse = jnp.einsum("xykr,xyrs->xyks", vectors, rounded.astype(jnp.float32))
        stacked = coarse.reshape(-1, coarse.shape[-1])
        solved = jnp.dot(coarse_cols, stacked, precision=lax.Precision.HIGHEST).reshape(coarse.shape)
        return result + jnp.einsum("xykr,xyks->xyrs", vectors, solved, precision=lax.Precision.HIGHEST)

    rhs_wide = right_side.astype(jnp.float32)
    solution = jnp.zeros(right_side.shape, jnp.float32)
    direction = apply_prec(rhs_wide)
    for iteration in range(ITERS):
        image = apply_schur(direction)
        mapped = apply_prec(image)
        numer = jnp.sum(mapped * direction, axis=(0, 1, 2))
        denom = jnp.sum(mapped * mapped, axis=(0, 1, 2))
        alpha = numer / denom
        solution = solution + alpha * direction
        direction = direction - alpha * mapped
    residual = rhs_wide - apply_schur(solution)
    return solution, residual
```

```python
import functools

import jax
import jax.numpy as jnp
from jax import lax
from jax.experimental import pallas as pl
from jax.experimental.pallas import tpu as pltpu
from jax.sharding import PartitionSpec as P

ITERS = 3


def from_behind(value, axis, steps):
    count = lax.axis_size(axis)
    leading, last = (max(0, -steps), min(count, count - steps))
    return lax.ppermute(value, axis, [(source, source + steps) for source in range(leading, last)])


def pass_columns(rows, offset):
    return from_behind(rows, "gx", offset)


def pass_lines(rows, offset):
    return from_behind(rows, "gy", offset)


def shards(
    right_side,
    schur_offdiag,
    schur_diag,
    trace_offdiag,
    trace_diag,
    couplings,
    margin_rows,
    deflation,
    coarse_inverse,
    coarse_map,
):
    rhs_wide = right_side[0, 0].astype(jnp.float32)
    schur_mat = schur_offdiag[0, 0]
    schur_scale = schur_diag[0, 0][:, None]
    trace_mat = trace_offdiag[0, 0]
    trace_scale = trace_diag[0, 0][:, None]
    coupling_blocks = couplings[0, 0]
    rows_lists = margin_rows[0, 0]
    flat_rows = rows_lists.reshape(-1)
    vectors = deflation[0, 0]
    vectors_wide = vectors.astype(jnp.float32).T
    coarse_cols = jnp.take(coarse_inverse, coarse_map, axis=1)

    def apply_schur(field):
        rounded = lax.optimization_barrier(field.astype(jnp.bfloat16))
        result = schur_scale * rounded.astype(jnp.float32) + jnp.dot(
            schur_mat, rounded, preferred_element_type=jnp.float32
        )
        sent_rows = rounded[rows_lists]
        received = jnp.stack(
            [
                pass_columns(sent_rows[1], 1),
                pass_columns(sent_rows[0], -1),
                pass_lines(sent_rows[3], 1),
                pass_lines(sent_rows[2], -1),
            ]
        )
        coupled = jnp.einsum(
            "dab,dbs->das", coupling_blocks, received, preferred_element_type=jnp.float32
        )
        return result.at[flat_rows].add(-coupled.reshape(-1, coupled.shape[-1]))

    def apply_prec(field):
        rounded = lax.optimization_barrier(field.astype(jnp.bfloat16))
        result = trace_scale * rounded.astype(jnp.float32) + jnp.dot(
            trace_mat, rounded, preferred_element_type=jnp.float32
        )
        coarse = jnp.dot(vectors, rounded, preferred_element_type=jnp.float32)
        stacked = lax.all_gather(coarse, ("gx", "gy"), axis=0, tiled=True)
        solved = jnp.dot(coarse_cols, stacked, precision=lax.Precision.HIGHEST)
        return result + jnp.dot(vectors_wide, solved, precision=lax.Precision.HIGHEST)

    solution = jnp.zeros(rhs_wide.shape, jnp.float32)
    direction = apply_prec(rhs_wide)
    for iteration in range(ITERS):
        image = apply_schur(direction)
        mapped = apply_prec(image)
        numer, denom = lax.psum(
            (jnp.sum(mapped * direction, axis=0), jnp.sum(mapped * mapped, axis=0)), ("gx", "gy")
        )
        alpha = numer / denom
        solution = solution + alpha * direction
        direction = direction - alpha * mapped
    residual = rhs_wide - apply_schur(solution)
    return (solution[None, None], residual[None, None])


MESH = pl.DeviceIdType.MESH
REPLICATED_COARSE = 512


def wide_dot(left, right):
    return jnp.dot(left, right, precision=lax.Precision.HIGHEST, preferred_element_type=jnp.float32)


def dot16(left, right):
    return jnp.dot(left, right, preferred_element_type=jnp.float32)


def pieces(value):
    high = value.astype(jnp.bfloat16)
    rest = value - high.astype(jnp.float32)
    middle = rest.astype(jnp.bfloat16)
    low = (rest - middle.astype(jnp.float32)).astype(jnp.bfloat16)
    return high, middle, low


def exact_dot(left, value):
    cols = value.shape[1]
    out = dot16(left, jnp.concatenate(pieces(value), axis=1))
    return out[:, :cols] + (out[:, cols : 2 * cols] + out[:, 2 * cols :])


def kernel(
    gx,
    gy,
    rhs_ref,
    schur_ref,
    sdiag_ref,
    trace_ref,
    tdiag_ref,
    coup_ref,
    rows_ref,
    defl_ref,
    cinv_ref,
    cmap_ref,
    x_ref,
    res_ref,
    sb_ref,
    pick_ref,
    v_ref,
    sd_ref,
    td_ref,
    d_ref,
    dh_ref,
    xh_ref,
    e_ref,
    solved_ref,
    dt_ref,
    dht_ref,
    cp_ref,
    gram_ref,
    a_buf,
    b_buf,
    extra,
    halo,
    halo_d,
    halo_d_out,
    halo_out,
    a_send,
    a_recv,
    b_send,
    b_recv,
    ea_send,
    ea_recv,
    eb_send,
    eb_recv,
    h_send,
    h_recv,
    hd_send,
    hd_recv,
):
    f32, bf16 = jnp.float32, jnp.bfloat16
    rows, src = rhs_ref.shape
    ov = rows_ref.shape[1]
    k = defl_ref.shape[0]
    nc = cinv_ref.shape[1]
    me_x, me_y = lax.axis_index("gx"), lax.axis_index("gy")
    place = me_x * gy + me_y
    iters = ITERS

    along_x = [lax.rem(me_x + step, gx) for step in range(1, gx)]
    along_y = [lax.rem(me_y + step, gy) for step in range(1, gy)]
    near = [
        (me_x > 0, (jnp.maximum(me_x - 1, 0), me_y)),
        (me_x < gx - 1, (jnp.minimum(me_x + 1, gx - 1), me_y)),
        (me_y > 0, (me_x, jnp.maximum(me_y - 1, 0))),
        (me_y < gy - 1, (me_x, jnp.minimum(me_y + 1, gy - 1))),
    ]

    halo[...] = jnp.zeros_like(halo)
    halo_d[...] = jnp.zeros_like(halo_d)

    barrier = pltpu.get_barrier_semaphore()
    for other in along_x:
        pl.semaphore_signal(barrier, inc=1, device_id=(other, me_y), device_id_type=MESH)
    for other in along_y:
        pl.semaphore_signal(barrier, inc=1, device_id=(me_x, other), device_id_type=MESH)

    def remote(source, target, send, recv, device):
        return pltpu.make_async_remote_copy(
            src_ref=source, dst_ref=target, send_sem=send, recv_sem=recv, device_id=device, device_id_type=MESH
        )

    defl = defl_ref[...]
    defl_wide = defl.astype(f32)
    tiled = jnp.concatenate([defl_wide] * (nc // k), axis=0).astype(bf16)
    gram = lax.dot_general(defl, tiled, (((1,), (1,)), ((), ())), preferred_element_type=f32)
    column = lax.broadcasted_iota(jnp.int32, (k, nc), 1)
    own = (column >= place * k) & (column < place * k + k)
    extra[me_x, me_y, 0:k, :] = cinv_ref[...]
    extra[me_x, me_y, k : 2 * k, :] = jnp.where(own, gram, 0.0)

    pl.semaphore_wait(barrier, gx + gy - 2)

    extra_a = [
        remote(extra.at[me_x, me_y], extra.at[me_x, me_y], ea_send.at[i], ea_recv.at[i], (me_x, other))
        for i, other in enumerate(along_y)
    ]
    for copy in extra_a:
        copy.start()

    def column_of(ref):
        return jnp.transpose(jnp.broadcast_to(ref[...], (src, rows)))

    td_ref[...] = column_of(tdiag_ref)
    sd_ref[...] = column_of(sdiag_ref)

    def local_prec(rounded):
        q = td_ref[...] * rounded.astype(f32) + dot16(trace_ref[...], rounded)
        return q, dot16(defl, rounded)

    def start_sums(t, q, coarse, sums):
        a_buf[t, me_y, 0:k, :] = coarse
        a_buf[t, me_y, k : 2 * k, :] = exact_dot(defl, q)
        a_buf[t, me_y, 2 * k : 3 * k, :] = sums

    def a_copies(t):
        return [
            remote(a_buf.at[t, me_y], a_buf.at[t, me_y], a_send.at[t, i], a_recv.at[t, i], (me_x, other))
            for i, other in enumerate(along_y)
        ]

    def b_copies(t):
        return [
            remote(b_buf.at[t, me_x], b_buf.at[t, me_x], b_send.at[t, i], b_recv.at[t, i], (other, me_y))
            for i, other in enumerate(along_x)
        ]

    def halo_copies(t):
        return [
            remote(halo_out.at[t, d], halo.at[t, d ^ 1], h_send.at[t, d], h_recv.at[t, d ^ 1], near[d][1])
            for d in range(4)
        ]

    def halo_waits(t):
        return [
            remote(halo_out.at[t, d], halo.at[t, d], h_send.at[t, d], h_recv.at[t, d], near[d][1])
            for d in range(4)
        ]

    def exchange(t, q, coarse, sums, with_halo):
        start_sums(t, q, coarse, sums)
        first = a_copies(t)
        for copy in first:
            copy.start()

        def send_halo():
            picked = exact_dot(pick_ref[...], q)
            for d in range(4):
                halo_out[t, d, :, :] = picked[d * ov : (d + 1) * ov]
            for d, copy in enumerate(halo_copies(t)):
                pl.when(near[d][0])(copy.start)

        if with_halo is True:
            send_halo()
        else:
            pl.when(with_halo)(send_halo)
        for copy in first:
            copy.wait()
        total = jnp.zeros((k, src), f32)
        for b in range(gy):
            b_buf[t, me_x, b * k : (b + 1) * k, :] = a_buf[t, b, 0:k, :]
            b_buf[t, me_x, (gy + b) * k : (gy + b + 1) * k, :] = a_buf[t, b, k : 2 * k, :]
            total = total + a_buf[t, b, 2 * k : 3 * k, :]
        b_buf[t, me_x, 2 * gy * k :, :] = total
        second = b_copies(t)
        for copy in second:
            copy.start()
        return second

    def gathered(t):
        coarse_all = jnp.concatenate([b_buf[t, a, 0 : gy * k, :] for a in range(gx)], axis=0)
        dq_all = jnp.concatenate([b_buf[t, a, gy * k : 2 * gy * k, :] for a in range(gx)], axis=0)
        total = b_buf[t, 0, 2 * gy * k :, :]
        for a in range(1, gx):
            total = total + b_buf[t, a, 2 * gy * k :, :]
        return coarse_all, dq_all, total

    def solve(coarse_all, dq_all):
        solved = wide_dot(cp_ref[...], coarse_all)
        solved_ref[...] = solved
        return solved, dq_all + wide_dot(gram_ref[...], solved)

    def solved_of(device):
        at = (device[0] * gy + device[1]) * k
        return jnp.concatenate(pieces(solved_ref[pl.ds(pl.multiple_of(at, k), k), :]), axis=0)

    def halo_mapped(t):
        for d, copy in enumerate(halo_waits(t)):
            pl.when(near[d][0])(copy.wait)
        return [
            halo[t, d, :, :] + dot16(dht_ref[d, :, :], solved_of(near[d][1])) for d in range(4)
        ]

    for d in range(4):
        wanted = jnp.transpose(jnp.broadcast_to(rows_ref[d : d + 1, :].astype(f32), (ov, ov)))
        wanted = jnp.concatenate([wanted] * (rows // ov), axis=1).astype(jnp.int32)
        hot = wanted == lax.broadcasted_iota(jnp.int32, (ov, rows), 1)
        pick_ref[d * ov : (d + 1) * ov, :] = jnp.where(hot, 1.0, 0.0).astype(bf16)

    q0, coarse0 = local_prec(rhs_ref[...])
    pending = exchange(0, q0, coarse0, jnp.zeros((k, src), f32), True)
    for copy in extra_a:
        copy.wait()
    extra_b = [
        remote(extra.at[me_x], extra.at[me_x], eb_send.at[i], eb_recv.at[i], (other, me_y))
        for i, other in enumerate(along_x)
    ]
    for copy in extra_b:
        copy.start()

    for d in range(4):
        halo_d_out[d, :, :] = lax.dot_general(
            defl, pick_ref[d * ov : (d + 1) * ov, :], (((1,), (1,)), ((), ())), preferred_element_type=f32
        )
        copy = remote(halo_d_out.at[d], halo_d.at[d ^ 1], hd_send.at[d], hd_recv.at[d ^ 1], near[d][1])
        pl.when(near[d][0])(copy.start)

    sb_ref[:, 0:rows] = schur_ref[...]
    for d in range(4):
        hot = rows_ref[d : d + 1, :] == lax.broadcasted_iota(jnp.int32, (rows, ov), 0)
        spread = dot16(jnp.where(hot, -1.0, 0.0).astype(bf16), coup_ref[d, :, :])
        sb_ref[:, rows + d * ov : rows + (d + 1) * ov] = spread.astype(bf16)
    dt_ref[...] = jnp.transpose(jnp.concatenate([defl_wide] * 3, axis=0)).astype(bf16)
    for d in range(4):
        arrival = remote(halo_d_out.at[d], halo_d.at[d], hd_send.at[d], hd_recv.at[d], near[d][1])
        pl.when(near[d][0])(arrival.wait)
        dht_ref[d, :, :] = jnp.transpose(jnp.concatenate([halo_d[d, :, :]] * 3, axis=0)).astype(bf16)

    for copy in extra_b:
        copy.wait()
    inverse = jnp.concatenate([extra[a, b, 0:k, :] for a in range(gx) for b in range(gy)], axis=0)
    gram_ref[...] = jnp.concatenate([extra[a, b, k : 2 * k, :] for a in range(gx) for b in range(gy)], axis=0)
    order = cmap_ref[...] == lax.broadcasted_iota(jnp.int32, (nc, nc), 0)
    cp_ref[...] = wide_dot(inverse, jnp.where(order, 1.0, 0.0))

    for copy in pending:
        copy.wait()
    coarse_all, dq_all, _ = gathered(0)
    solved, projected = solve(coarse_all, dq_all)
    e_ref[...] = projected
    d_ref[...] = q0 + dot16(dt_ref[...], solved_of((me_x, me_y)))
    dh_ref[...] = jnp.concatenate(halo_mapped(0), axis=0)
    x_ref[...] = jnp.zeros_like(x_ref)
    xh_ref[...] = jnp.zeros_like(xh_ref)

    def schur(field_ref, margin_ref):
        v_ref[0:rows, :] = field_ref[...].astype(bf16)
        v_ref[rows:, :] = margin_ref[...].astype(bf16)
        return sd_ref[...] * v_ref[0:rows, :].astype(f32) + dot16(sb_ref[...], v_ref[...])

    def iteration(step, carry):
        t = step + 1
        more = t < iters
        q, coarse = local_prec(schur(d_ref, dh_ref).astype(bf16))
        sums = jnp.concatenate(
            [
                jnp.sum(q * d_ref[...], axis=0, keepdims=True),
                jnp.sum(q * q, axis=0, keepdims=True),
                jnp.zeros((k - 2, src), f32),
            ],
            axis=0,
        )
        for copy in exchange(t, q, coarse, sums, more):
            copy.wait()
        coarse_all, dq_all, total = gathered(t)
        solved, projected = solve(coarse_all, dq_all)
        numer = total[0:1] + jnp.sum(solved * e_ref[...], axis=0, keepdims=True)
        denom = total[1:2] + jnp.sum(solved * (dq_all + projected), axis=0, keepdims=True)
        alpha = numer / denom
        x_ref[...] += alpha * d_ref[...]
        xh_ref[...] += alpha * dh_ref[...]

        @pl.when(more)
        def _():
            d_ref[...] -= alpha * (q + dot16(dt_ref[...], solved_of((me_x, me_y))))
            e_ref[...] -= alpha * projected
            dh_ref[...] -= alpha * jnp.concatenate(halo_mapped(t), axis=0)

        return carry

    lax.fori_loop(0, iters, iteration, 0)
    res_ref[...] = rhs_ref[...].astype(f32) - schur(x_ref, xh_ref)


def one_kernel(gx, gy, *args):
    right_side, schur, sdiag, trace, tdiag, couplings, margin, deflation, inverse, coarse_map = args
    rows, src = right_side.shape[2:]
    ov = margin.shape[3]
    k = deflation.shape[2]
    nc = inverse.shape[1]
    f32, bf16 = jnp.float32, jnp.bfloat16
    rounds = ITERS + 1
    vmem, dma = pltpu.VMEM, pltpu.SemaphoreType.DMA
    x, residual = pl.pallas_call(
        functools.partial(kernel, gx, gy),
        out_shape=[jax.ShapeDtypeStruct((rows, src), f32)] * 2,
        in_specs=[pl.BlockSpec(memory_space=pltpu.VMEM)] * 10,
        out_specs=[pl.BlockSpec(memory_space=pltpu.VMEM)] * 2,
        scratch_shapes=[
            vmem((rows, rows + 4 * ov), bf16),
            vmem((4 * ov, rows), bf16),
            vmem((rows + 4 * ov, src), bf16),
            vmem((rows, src), f32),
            vmem((rows, src), f32),
            vmem((rows, src), f32),
            vmem((4 * ov, src), f32),
            vmem((4 * ov, src), f32),
            vmem((nc, src), f32),
            vmem((nc, src), f32),
            vmem((rows, 3 * k), bf16),
            vmem((4, ov, 3 * k), bf16),
            vmem((nc, nc), f32),
            vmem((nc, nc), f32),
            vmem((rounds, gy, 3 * k, src), f32),
            vmem((rounds, gx, (2 * gy + 1) * k, src), f32),
            vmem((gx, gy, 2 * k, nc), f32),
            vmem((rounds, 4, ov, src), f32),
            vmem((4, k, ov), f32),
            vmem((4, k, ov), f32),
            vmem((rounds, 4, ov, src), f32),
            dma((rounds, gy - 1)),
            dma((rounds, gy - 1)),
            dma((rounds, gx - 1)),
            dma((rounds, gx - 1)),
            dma((gy - 1,)),
            dma((gy - 1,)),
            dma((gx - 1,)),
            dma((gx - 1,)),
            dma((rounds, 4)),
            dma((rounds, 4)),
            dma((4,)),
            dma((4,)),
        ],
        compiler_params=pltpu.CompilerParams(
            collective_id=0, has_side_effects=True, vmem_limit_bytes=48 * 1024 * 1024
        ),
        cost_estimate=pl.CostEstimate(flops=4_000_000_000, bytes_accessed=6_000_000, transcendentals=0),
    )(
        right_side[0, 0],
        schur[0, 0],
        sdiag[0],
        trace[0, 0],
        tdiag[0],
        couplings[0, 0],
        margin[0, 0],
        deflation[0, 0],
        inverse,
        coarse_map[None],
    )
    return x[None, None], residual[None, None]


def plan(gx, gy, *args):
    if args[8].shape[1] <= REPLICATED_COARSE:
        return one_kernel(gx, gy, *args)
    return shards(*args)


def solution(mesh):
    return jax.shard_map(
        functools.partial(plan, mesh.shape["gx"], mesh.shape["gy"]),
        mesh=mesh,
        in_specs=(
            P("gx", "gy", None, None),
            P("gx", "gy", None, None),
            P("gx", "gy", None),
            P("gx", "gy", None, None),
            P("gx", "gy", None),
            P("gx", "gy", None, None, None),
            P("gx", "gy", None, None),
            P("gx", "gy", None, None),
            P(("gx", "gy"), None),
            P(),
        ),
        out_specs=(P("gx", "gy", None, None), P("gx", "gy", None, None)),
        check_vma=False,
    )
```

```python
import functools

import jax
import jax.numpy as jnp
from jax import lax
from jax.experimental import pallas as pl
from jax.experimental.pallas import tpu as pltpu
from jax.sharding import PartitionSpec as P

ITERS = 3


def from_behind(value, axis, steps):
    count = lax.axis_size(axis)
    leading, last = (max(0, -steps), min(count, count - steps))
    return lax.ppermute(value, axis, [(source, source + steps) for source in range(leading, last)])


def pass_columns(rows, offset):
    return from_behind(rows, "gx", offset)


def pass_lines(rows, offset):
    return from_behind(rows, "gy", offset)


def shards(
    right_side,
    schur_offdiag,
    schur_diag,
    trace_offdiag,
    trace_diag,
    couplings,
    margin_rows,
    deflation,
    coarse_inverse,
    coarse_map,
):
    rhs_wide = right_side[0, 0].astype(jnp.float32)
    schur_mat = schur_offdiag[0, 0]
    schur_scale = schur_diag[0, 0][:, None]
    trace_mat = trace_offdiag[0, 0]
    trace_scale = trace_diag[0, 0][:, None]
    coupling_blocks = couplings[0, 0]
    rows_lists = margin_rows[0, 0]
    flat_rows = rows_lists.reshape(-1)
    vectors = deflation[0, 0]
    vectors_wide = vectors.astype(jnp.float32).T
    coarse_cols = jnp.take(coarse_inverse, coarse_map, axis=1)

    def apply_schur(field):
        rounded = lax.optimization_barrier(field.astype(jnp.bfloat16))
        result = schur_scale * rounded.astype(jnp.float32) + jnp.dot(
            schur_mat, rounded, preferred_element_type=jnp.float32
        )
        sent_rows = rounded[rows_lists]
        received = jnp.stack(
            [
                pass_columns(sent_rows[1], 1),
                pass_columns(sent_rows[0], -1),
                pass_lines(sent_rows[3], 1),
                pass_lines(sent_rows[2], -1),
            ]
        )
        coupled = jnp.einsum(
            "dab,dbs->das", coupling_blocks, received, preferred_element_type=jnp.float32
        )
        return result.at[flat_rows].add(-coupled.reshape(-1, coupled.shape[-1]))

    def apply_prec(field):
        rounded = lax.optimization_barrier(field.astype(jnp.bfloat16))
        result = trace_scale * rounded.astype(jnp.float32) + jnp.dot(
            trace_mat, rounded, preferred_element_type=jnp.float32
        )
        coarse = jnp.dot(vectors, rounded, preferred_element_type=jnp.float32)
        stacked = lax.all_gather(coarse, ("gx", "gy"), axis=0, tiled=True)
        solved = jnp.dot(coarse_cols, stacked, precision=lax.Precision.HIGHEST)
        return result + jnp.dot(vectors_wide, solved, precision=lax.Precision.HIGHEST)

    solution = jnp.zeros(rhs_wide.shape, jnp.float32)
    direction = apply_prec(rhs_wide)
    for iteration in range(ITERS):
        image = apply_schur(direction)
        mapped = apply_prec(image)
        numer, denom = lax.psum(
            (jnp.sum(mapped * direction, axis=0), jnp.sum(mapped * mapped, axis=0)), ("gx", "gy")
        )
        alpha = numer / denom
        solution = solution + alpha * direction
        direction = direction - alpha * mapped
    residual = rhs_wide - apply_schur(solution)
    return (solution[None, None], residual[None, None])


MESH = pl.DeviceIdType.MESH
REPLICATED_COARSE = 512


def wide_dot(left, right):
    return jnp.dot(left, right, precision=lax.Precision.HIGHEST, preferred_element_type=jnp.float32)


def dot16(left, right):
    return jnp.dot(left, right, preferred_element_type=jnp.float32)


def pieces(value):
    high = value.astype(jnp.bfloat16)
    rest = value - high.astype(jnp.float32)
    middle = rest.astype(jnp.bfloat16)
    low = (rest - middle.astype(jnp.float32)).astype(jnp.bfloat16)
    return high, middle, low


def exact_dot(left, value):
    cols = value.shape[1]
    out = dot16(left, jnp.concatenate(pieces(value), axis=1))
    return out[:, :cols] + (out[:, cols : 2 * cols] + out[:, 2 * cols :])


def six(value, left):
    high, middle, low = pieces(value)
    if left:
        return jnp.concatenate([high, high, high, middle, middle, low], axis=1)
    return jnp.concatenate([high, middle, low, high, middle, high], axis=0)


def kernel(
    gx,
    gy,
    rhs_hbm,
    schur_hbm,
    sdiag_hbm,
    trace_hbm,
    tdiag_hbm,
    coup_hbm,
    rows_hbm,
    defl_hbm,
    cinv_hbm,
    cmap_hbm,
    x_ref,
    res_ref,
    rhs_ref,
    sdiag_ref,
    trace_ref,
    tdiag_ref,
    coup_ref,
    rows_ref,
    defl_ref,
    cmap_ref,
    load_sem,
    sb_ref,
    pick_ref,
    v_ref,
    sd_ref,
    td_ref,
    d_ref,
    dh_ref,
    xh_ref,
    e_ref,
    solved_ref,
    dt_ref,
    dht_ref,
    both_ref,
    small_ref,
    main,
    sum_a,
    sum_b,
    extra,
    halo,
    halo_d,
    halo_d_out,
    halo_out,
    a_send,
    a_recv,
    b_send,
    b_recv,
    sa_send,
    sa_recv,
    sb_send,
    sb_recv,
    ea_send,
    ea_recv,
    eb_send,
    eb_recv,
    h_send,
    h_recv,
    hd_send,
    hd_recv,
):
    f32, bf16 = jnp.float32, jnp.bfloat16
    rows, src = rhs_ref.shape
    ov = rows_ref.shape[1]
    k = defl_ref.shape[0]
    nc = cmap_ref.shape[1]
    me_x, me_y = lax.axis_index("gx"), lax.axis_index("gy")
    iters = ITERS

    def load(i, source, target):
        copy = pltpu.make_async_copy(source, target, load_sem.at[i])
        copy.start()
        return copy

    load_defl = load(0, defl_hbm, defl_ref)
    load_cinv = load(1, cinv_hbm, extra.at[me_x, me_y, :, pl.ds(0, nc)])
    load_tdiag = load(2, tdiag_hbm, tdiag_ref)
    load_rhs = load(3, rhs_hbm, rhs_ref)
    load_trace = load(4, trace_hbm, trace_ref)
    load_rows = load(5, rows_hbm, rows_ref)
    load_cmap = load(6, cmap_hbm, cmap_ref)
    load_sdiag = load(7, sdiag_hbm, sdiag_ref)
    load_coup = load(8, coup_hbm, coup_ref)
    load_schur = load(9, schur_hbm, sb_ref.at[:, pl.ds(0, rows)])

    along_x = [lax.rem(me_x + step, gx) for step in range(1, gx)]
    along_y = [lax.rem(me_y + step, gy) for step in range(1, gy)]
    near = [
        (me_x > 0, (jnp.maximum(me_x - 1, 0), me_y)),
        (me_x < gx - 1, (jnp.minimum(me_x + 1, gx - 1), me_y)),
        (me_y > 0, (me_x, jnp.maximum(me_y - 1, 0))),
        (me_y < gy - 1, (me_x, jnp.minimum(me_y + 1, gy - 1))),
    ]

    for d in range(4):

        @pl.when(jnp.logical_not(near[d][0]))
        def _():
            halo[:, d, :, :] = jnp.zeros((iters, ov, src), f32)
            halo_d[d, :, :] = jnp.zeros((k, ov), f32)

    barrier = pltpu.get_barrier_semaphore()
    for other in along_x:
        pl.semaphore_signal(barrier, inc=1, device_id=(other, me_y), device_id_type=MESH)
    for other in along_y:
        pl.semaphore_signal(barrier, inc=1, device_id=(me_x, other), device_id_type=MESH)

    def remote(source, target, send, recv, device):
        return pltpu.make_async_remote_copy(
            src_ref=source, dst_ref=target, send_sem=send, recv_sem=recv, device_id=device, device_id_type=MESH
        )

    def to_lines(ref, send, recv):
        return [remote(ref, ref, send.at[i], recv.at[i], (me_x, other)) for i, other in enumerate(along_y)]

    def to_columns(ref, send, recv):
        return [remote(ref, ref, send.at[i], recv.at[i], (other, me_y)) for i, other in enumerate(along_x)]

    def start(copies):
        for copy in copies:
            copy.start()

    def wait(copies):
        for copy in copies:
            copy.wait()

    load_defl.wait()
    defl = defl_ref[...]
    defl_wide = defl.astype(f32)
    padded = jnp.concatenate([defl_wide, jnp.zeros((src - k, rows), f32)], axis=0).astype(bf16)
    extra[me_x, me_y, :, nc:] = lax.dot_general(
        defl, padded, (((1,), (1,)), ((), ())), preferred_element_type=f32
    )
    load_cinv.wait()
    pl.semaphore_wait(barrier, gx + gy - 2)

    extra_a = to_lines(extra.at[me_x, me_y], ea_send, ea_recv)
    start(extra_a)

    load_tdiag.wait()
    load_trace.wait()
    with_trace = defl_wide * tdiag_ref[...] + dot16(defl, trace_ref[...])
    small_ref[...] = jnp.concatenate(
        [defl_wide] + [piece.astype(f32) for piece in pieces(with_trace)], axis=0
    ).astype(bf16)

    def coarse_copies(t):
        return (
            to_lines(main.at[t, me_x, me_y], a_send.at[t], a_recv.at[t]),
            to_columns(main.at[t, me_x], b_send.at[t], b_recv.at[t]),
        )

    def start_coarse(t, rounded):
        out = dot16(small_ref[...], rounded)
        main[t, me_x, me_y, 0:k, :] = out[0:k]
        main[t, me_x, me_y, k : 2 * k, :] = out[k : 2 * k] + (out[2 * k : 3 * k] + out[3 * k : 4 * k])
        start(coarse_copies(t)[0])

    def forward_coarse(t):
        first, second = coarse_copies(t)
        wait(first)
        start(second)

    def local_prec(rounded):
        return td_ref[...] * rounded.astype(f32) + dot16(trace_ref[...], rounded)

    def halo_copies(t, arriving):
        return [
            remote(
                halo_out.at[t, d],
                halo.at[t, d if arriving else d ^ 1],
                h_send.at[t, d],
                h_recv.at[t, d if arriving else d ^ 1],
                near[d][1],
            )
            for d in range(4)
        ]

    def send_halo(t, q):
        picked = exact_dot(pick_ref[...], q)
        for d in range(4):
            halo_out[t, d, :, :] = picked[d * ov : (d + 1) * ov]
        for d, copy in enumerate(halo_copies(t, False)):
            pl.when(near[d][0])(copy.start)

    def solve(t):
        wait(coarse_copies(t)[1])
        coarse_all = jnp.concatenate([main[t, a, b, 0:k, :] for a in range(gx) for b in range(gy)], axis=0)
        dq_all = jnp.concatenate([main[t, a, b, k : 2 * k, :] for a in range(gx) for b in range(gy)], axis=0)
        both = dot16(both_ref[...], six(coarse_all, False))
        solved_ref[...] = both[0:nc]
        return both[0:nc], dq_all, dq_all + both[nc:]

    def solved_of(device):
        at = (device[0] * gy + device[1]) * k
        return jnp.concatenate(pieces(solved_ref[pl.ds(pl.multiple_of(at, k), k), :]), axis=0)

    def halo_mapped(t):
        for d, copy in enumerate(halo_copies(t, True)):
            pl.when(near[d][0])(copy.wait)
        return jnp.concatenate(
            [halo[t, d, :, :] + dot16(dht_ref[d, :, :], solved_of(near[d][1])) for d in range(4)], axis=0
        )

    load_rhs.wait()
    start_coarse(0, rhs_ref[...])

    load_rows.wait()
    for d in range(4):
        wanted = jnp.transpose(jnp.broadcast_to(rows_ref[d : d + 1, :].astype(f32), (ov, ov)))
        wanted = jnp.concatenate([wanted] * (rows // ov), axis=1).astype(jnp.int32)
        hot = wanted == lax.broadcasted_iota(jnp.int32, (ov, rows), 1)
        pick_ref[d * ov : (d + 1) * ov, :] = jnp.where(hot, 1.0, 0.0).astype(bf16)
    for d in range(4):
        halo_d_out[d, :, :] = lax.dot_general(
            defl, pick_ref[d * ov : (d + 1) * ov, :], (((1,), (1,)), ((), ())), preferred_element_type=f32
        )
        copy = remote(halo_d_out.at[d], halo_d.at[d ^ 1], hd_send.at[d], hd_recv.at[d ^ 1], near[d][1])
        pl.when(near[d][0])(copy.start)

    forward_coarse(0)
    wait(extra_a)
    extra_b = to_columns(extra.at[me_x], eb_send, eb_recv)
    start(extra_b)

    def column_of(ref):
        return jnp.transpose(jnp.broadcast_to(ref[...], (src, rows)))

    td_ref[...] = column_of(tdiag_ref)
    q0 = local_prec(rhs_ref[...])
    send_halo(0, q0)

    load_sdiag.wait()
    sd_ref[...] = column_of(sdiag_ref)
    load_coup.wait()
    for d in range(4):
        hot = rows_ref[d : d + 1, :] == lax.broadcasted_iota(jnp.int32, (rows, ov), 0)
        spread = dot16(jnp.where(hot, -1.0, 0.0).astype(bf16), coup_ref[d, :, :])
        sb_ref[:, rows + d * ov : rows + (d + 1) * ov] = spread.astype(bf16)
    dt_ref[...] = jnp.transpose(jnp.concatenate([defl_wide] * 3, axis=0)).astype(bf16)
    for d in range(4):
        arrival = remote(halo_d_out.at[d], halo_d.at[d], hd_send.at[d], hd_recv.at[d], near[d][1])
        pl.when(near[d][0])(arrival.wait)
        dht_ref[d, :, :] = jnp.transpose(jnp.concatenate([halo_d[d, :, :]] * 3, axis=0)).astype(bf16)
    load_cmap.wait()
    order = cmap_ref[...] == lax.broadcasted_iota(jnp.int32, (nc, nc), 0)
    order = jnp.where(order, 1.0, 0.0).astype(bf16)

    wait(extra_b)
    blocks = [(a, b) for a in range(gx) for b in range(gy)]
    inverse = jnp.concatenate([extra[a, b, :, 0:nc] for a, b in blocks], axis=0)
    inverse = sum(dot16(piece, order) for piece in reversed(pieces(inverse)))
    gram = jnp.concatenate([extra[a, b, :, nc:] for a, b in blocks], axis=0)
    row = lax.broadcasted_iota(jnp.int32, (src, nc), 0)
    column = lax.broadcasted_iota(jnp.int32, (src, nc), 1)
    repeat = jnp.where(row == column % k, 1.0, 0.0).astype(bf16)
    gram = sum(dot16(piece, repeat) for piece in reversed(pieces(gram)))
    row = lax.broadcasted_iota(jnp.int32, (nc, nc), 0)
    column = lax.broadcasted_iota(jnp.int32, (nc, nc), 1)
    gram = jnp.where(row // k == column // k, gram, 0.0)
    both_ref[0:nc, :] = six(inverse, True)
    both_ref[nc:, :] = six(wide_dot(gram, inverse), True)

    solved, _, projected = solve(0)
    e_ref[...] = projected
    d_ref[...] = q0 + dot16(dt_ref[...], solved_of((me_x, me_y)))
    dh_ref[...] = halo_mapped(0)
    x_ref[...] = jnp.zeros_like(x_ref)
    xh_ref[...] = jnp.zeros_like(xh_ref)
    load_schur.wait()

    def schur(field_ref, margin_ref):
        v_ref[0:rows, :] = field_ref[...].astype(bf16)
        v_ref[rows:, :] = margin_ref[...].astype(bf16)
        return sd_ref[...] * v_ref[0:rows, :].astype(f32) + dot16(sb_ref[...], v_ref[...])

    def iteration(step, carry):
        t = step + 1
        more = t < iters
        rounded = schur(d_ref, dh_ref).astype(bf16)
        start_coarse(t, rounded)
        q = local_prec(rounded)
        sum_a[t, me_y, :, :] = jnp.concatenate(
            [
                jnp.sum(q * d_ref[...], axis=0, keepdims=True),
                jnp.sum(q * q, axis=0, keepdims=True),
                jnp.zeros((k - 2, src), f32),
            ],
            axis=0,
        )
        first = to_lines(sum_a.at[t, me_y], sa_send.at[t], sa_recv.at[t])
        start(first)
        forward_coarse(t)
        wait(first)
        total = sum_a[t, 0, :, :]
        for b in range(1, gy):
            total = total + sum_a[t, b, :, :]
        sum_b[t, me_x, :, :] = total
        second = to_columns(sum_b.at[t, me_x], sb_send.at[t], sb_recv.at[t])
        start(second)
        pl.when(more)(lambda: send_halo(t, q))
        solved, dq_all, projected = solve(t)
        numer = jnp.sum(solved * e_ref[...], axis=0, keepdims=True)
        denom = jnp.sum(solved * (dq_all + projected), axis=0, keepdims=True)
        wait(second)
        total = sum_b[t, 0, :, :]
        for a in range(1, gx):
            total = total + sum_b[t, a, :, :]
        alpha = (total[0:1] + numer) / (total[1:2] + denom)
        x_ref[...] += alpha * d_ref[...]
        xh_ref[...] += alpha * dh_ref[...]

        @pl.when(more)
        def _():
            d_ref[...] -= alpha * (q + dot16(dt_ref[...], solved_of((me_x, me_y))))
            e_ref[...] -= alpha * projected
            dh_ref[...] -= alpha * halo_mapped(t)

        return carry

    lax.fori_loop(0, iters, iteration, 0)
    res_ref[...] = rhs_ref[...].astype(f32) - schur(x_ref, xh_ref)


def one_kernel(gx, gy, *args):
    right_side, schur, sdiag, trace, tdiag, couplings, margin, deflation, inverse, coarse_map = args
    rows, src = right_side.shape[2:]
    ov = margin.shape[3]
    k = deflation.shape[2]
    nc = inverse.shape[1]
    f32, bf16 = jnp.float32, jnp.bfloat16
    rounds = ITERS + 1
    vmem, dma = pltpu.VMEM, pltpu.SemaphoreType.DMA
    x, residual = pl.pallas_call(
        functools.partial(kernel, gx, gy),
        out_shape=[jax.ShapeDtypeStruct((rows, src), f32)] * 2,
        in_specs=[pl.BlockSpec(memory_space=pl.ANY)] * 10,
        out_specs=[pl.BlockSpec(memory_space=pltpu.VMEM)] * 2,
        scratch_shapes=[
            vmem((rows, src), bf16),
            vmem((1, rows), f32),
            vmem((rows, rows), bf16),
            vmem((1, rows), f32),
            vmem((4, ov, ov), bf16),
            vmem((4, ov), jnp.int32),
            vmem((k, rows), bf16),
            vmem((1, nc), jnp.int32),
            dma((10,)),
            vmem((rows, rows + 4 * ov), bf16),
            vmem((4 * ov, rows), bf16),
            vmem((rows + 4 * ov, src), bf16),
            vmem((rows, src), f32),
            vmem((rows, src), f32),
            vmem((rows, src), f32),
            vmem((4 * ov, src), f32),
            vmem((4 * ov, src), f32),
            vmem((nc, src), f32),
            vmem((nc, src), f32),
            vmem((rows, 3 * k), bf16),
            vmem((4, ov, 3 * k), bf16),
            vmem((2 * nc, 6 * nc), bf16),
            vmem((4 * k, rows), bf16),
            vmem((rounds, gx, gy, 2 * k, src), f32),
            vmem((rounds, gy, k, src), f32),
            vmem((rounds, gx, k, src), f32),
            vmem((gx, gy, k, nc + src), f32),
            vmem((ITERS, 4, ov, src), f32),
            vmem((4, k, ov), f32),
            vmem((4, k, ov), f32),
            vmem((ITERS, 4, ov, src), f32),
            dma((rounds, gy - 1)),
            dma((rounds, gy - 1)),
            dma((rounds, gx - 1)),
            dma((rounds, gx - 1)),
            dma((rounds, gy - 1)),
            dma((rounds, gy - 1)),
            dma((rounds, gx - 1)),
            dma((rounds, gx - 1)),
            dma((gy - 1,)),
            dma((gy - 1,)),
            dma((gx - 1,)),
            dma((gx - 1,)),
            dma((ITERS, 4)),
            dma((ITERS, 4)),
            dma((4,)),
            dma((4,)),
        ],
        compiler_params=pltpu.CompilerParams(
            collective_id=0, has_side_effects=True, vmem_limit_bytes=60 * 1024 * 1024
        ),
        cost_estimate=pl.CostEstimate(flops=4_000_000_000, bytes_accessed=6_000_000, transcendentals=0),
    )(
        right_side[0, 0],
        schur[0, 0],
        sdiag[0],
        trace[0, 0],
        tdiag[0],
        couplings[0, 0],
        margin[0, 0],
        deflation[0, 0],
        inverse,
        coarse_map[None],
    )
    return x[None, None], residual[None, None]


def plan(gx, gy, *args):
    if args[8].shape[1] <= REPLICATED_COARSE:
        return one_kernel(gx, gy, *args)
    return shards(*args)


def solution(mesh):
    return jax.shard_map(
        functools.partial(plan, mesh.shape["gx"], mesh.shape["gy"]),
        mesh=mesh,
        in_specs=(
            P("gx", "gy", None, None),
            P("gx", "gy", None, None),
            P("gx", "gy", None),
            P("gx", "gy", None, None),
            P("gx", "gy", None),
            P("gx", "gy", None, None, None),
            P("gx", "gy", None, None),
            P("gx", "gy", None, None),
            P(("gx", "gy"), None),
            P(),
        ),
        out_specs=(P("gx", "gy", None, None), P("gx", "gy", None, None)),
        check_vma=False,
    )
```

```python
import functools

import jax
import jax.numpy as jnp
from jax import lax
from jax.experimental import pallas as pl
from jax.experimental.pallas import tpu as pltpu
from jax.sharding import PartitionSpec as P

ITERS = 3


def from_behind(value, axis, steps):
    count = lax.axis_size(axis)
    leading, last = (max(0, -steps), min(count, count - steps))
    return lax.ppermute(value, axis, [(source, source + steps) for source in range(leading, last)])


def pass_columns(rows, offset):
    return from_behind(rows, "gx", offset)


def pass_lines(rows, offset):
    return from_behind(rows, "gy", offset)


def shards(
    right_side,
    schur_offdiag,
    schur_diag,
    trace_offdiag,
    trace_diag,
    couplings,
    margin_rows,
    deflation,
    coarse_inverse,
    coarse_map,
):
    rhs_wide = right_side[0, 0].astype(jnp.float32)
    schur_mat = schur_offdiag[0, 0]
    schur_scale = schur_diag[0, 0][:, None]
    trace_mat = trace_offdiag[0, 0]
    trace_scale = trace_diag[0, 0][:, None]
    coupling_blocks = couplings[0, 0]
    rows_lists = margin_rows[0, 0]
    flat_rows = rows_lists.reshape(-1)
    vectors = deflation[0, 0]
    vectors_wide = vectors.astype(jnp.float32).T
    coarse_cols = jnp.take(coarse_inverse, coarse_map, axis=1)

    def apply_schur(field):
        rounded = lax.optimization_barrier(field.astype(jnp.bfloat16))
        result = schur_scale * rounded.astype(jnp.float32) + jnp.dot(
            schur_mat, rounded, preferred_element_type=jnp.float32
        )
        sent_rows = rounded[rows_lists]
        received = jnp.stack(
            [
                pass_columns(sent_rows[1], 1),
                pass_columns(sent_rows[0], -1),
                pass_lines(sent_rows[3], 1),
                pass_lines(sent_rows[2], -1),
            ]
        )
        coupled = jnp.einsum(
            "dab,dbs->das", coupling_blocks, received, preferred_element_type=jnp.float32
        )
        return result.at[flat_rows].add(-coupled.reshape(-1, coupled.shape[-1]))

    def apply_prec(field):
        rounded = lax.optimization_barrier(field.astype(jnp.bfloat16))
        result = trace_scale * rounded.astype(jnp.float32) + jnp.dot(
            trace_mat, rounded, preferred_element_type=jnp.float32
        )
        coarse = jnp.dot(vectors, rounded, preferred_element_type=jnp.float32)
        stacked = lax.all_gather(coarse, ("gx", "gy"), axis=0, tiled=True)
        solved = jnp.dot(coarse_cols, stacked, precision=lax.Precision.HIGHEST)
        return result + jnp.dot(vectors_wide, solved, precision=lax.Precision.HIGHEST)

    solution = jnp.zeros(rhs_wide.shape, jnp.float32)
    direction = apply_prec(rhs_wide)
    for iteration in range(ITERS):
        image = apply_schur(direction)
        mapped = apply_prec(image)
        numer, denom = lax.psum(
            (jnp.sum(mapped * direction, axis=0), jnp.sum(mapped * mapped, axis=0)), ("gx", "gy")
        )
        alpha = numer / denom
        solution = solution + alpha * direction
        direction = direction - alpha * mapped
    residual = rhs_wide - apply_schur(solution)
    return (solution[None, None], residual[None, None])


MESH = pl.DeviceIdType.MESH
REPLICATED_COARSE = 512


def wide_dot(left, right):
    return jnp.dot(left, right, precision=lax.Precision.HIGHEST, preferred_element_type=jnp.float32)


def dot16(left, right):
    return jnp.dot(left, right, preferred_element_type=jnp.float32)


def pieces(value):
    high = value.astype(jnp.bfloat16)
    rest = value - high.astype(jnp.float32)
    middle = rest.astype(jnp.bfloat16)
    low = (rest - middle.astype(jnp.float32)).astype(jnp.bfloat16)
    return high, middle, low


def exact_dot(left, value):
    cols = value.shape[1]
    out = dot16(left, jnp.concatenate(pieces(value), axis=1))
    return out[:, :cols] + (out[:, cols : 2 * cols] + out[:, 2 * cols :])


def six(value, left):
    high, middle, low = pieces(value)
    if left:
        return jnp.concatenate([high, high, high, middle, middle, low], axis=1)
    return jnp.concatenate([high, middle, low, high, middle, high], axis=0)


def kernel(
    gx,
    gy,
    rhs_hbm,
    schur_hbm,
    sdiag_hbm,
    trace_hbm,
    tdiag_hbm,
    coup_hbm,
    rows_hbm,
    defl_hbm,
    cinv_hbm,
    cmap_hbm,
    x_ref,
    res_ref,
    rhs_ref,
    sdiag_ref,
    trace_ref,
    tdiag_ref,
    coup_ref,
    rows_ref,
    defl_ref,
    cmap_ref,
    load_sem,
    sb_ref,
    pick_ref,
    v_ref,
    sd_ref,
    td_ref,
    d_ref,
    dh_ref,
    xh_ref,
    e_ref,
    solved_ref,
    dt_ref,
    dht_ref,
    both_ref,
    small_ref,
    main,
    sum_a,
    sum_b,
    extra,
    halo,
    halo_d,
    halo_d_out,
    halo_out,
    a_send,
    a_recv,
    b_send,
    b_recv,
    sa_send,
    sa_recv,
    sb_send,
    sb_recv,
    ea_send,
    ea_recv,
    eb_send,
    eb_recv,
    h_send,
    h_recv,
    hd_send,
    hd_recv,
):
    f32, bf16 = jnp.float32, jnp.bfloat16
    rows, src = rhs_ref.shape
    ov = rows_ref.shape[1]
    k = defl_ref.shape[0]
    nc = cmap_ref.shape[1]
    me_x, me_y = lax.axis_index("gx"), lax.axis_index("gy")
    iters = ITERS

    def load(i, source, target):
        copy = pltpu.make_async_copy(source, target, load_sem.at[i])
        copy.start()
        return copy

    load_defl = load(0, defl_hbm, defl_ref)
    load_cinv = load(1, cinv_hbm, extra.at[me_x, me_y, :, pl.ds(0, nc)])
    load_tdiag = load(2, tdiag_hbm, tdiag_ref)
    load_rhs = load(3, rhs_hbm, rhs_ref)
    load_trace = load(4, trace_hbm, trace_ref)
    load_rows = load(5, rows_hbm, rows_ref)
    load_cmap = load(6, cmap_hbm, cmap_ref)
    load_sdiag = load(7, sdiag_hbm, sdiag_ref)
    load_coup = load(8, coup_hbm, coup_ref)
    load_schur = load(9, schur_hbm, sb_ref.at[:, pl.ds(0, rows)])

    along_x = [lax.rem(me_x + step, gx) for step in range(1, gx)]
    along_y = [lax.rem(me_y + step, gy) for step in range(1, gy)]
    near = [
        (me_x > 0, (jnp.maximum(me_x - 1, 0), me_y)),
        (me_x < gx - 1, (jnp.minimum(me_x + 1, gx - 1), me_y)),
        (me_y > 0, (me_x, jnp.maximum(me_y - 1, 0))),
        (me_y < gy - 1, (me_x, jnp.minimum(me_y + 1, gy - 1))),
    ]

    for d in range(4):

        @pl.when(jnp.logical_not(near[d][0]))
        def _():
            halo[:, d, :, :] = jnp.zeros((iters, ov, src), f32)
            halo_d[d, :, :] = jnp.zeros((k, ov), f32)

    barrier = pltpu.get_barrier_semaphore()
    for other in along_x:
        pl.semaphore_signal(barrier, inc=1, device_id=(other, me_y), device_id_type=MESH)
    for other in along_y:
        pl.semaphore_signal(barrier, inc=1, device_id=(me_x, other), device_id_type=MESH)

    def remote(source, target, send, recv, device):
        return pltpu.make_async_remote_copy(
            src_ref=source, dst_ref=target, send_sem=send, recv_sem=recv, device_id=device, device_id_type=MESH
        )

    def to_lines(ref, send, recv):
        return [remote(ref, ref, send.at[i], recv.at[i], (me_x, other)) for i, other in enumerate(along_y)]

    def to_columns(ref, send, recv):
        return [remote(ref, ref, send.at[i], recv.at[i], (other, me_y)) for i, other in enumerate(along_x)]

    sibling = me_x + 1 - 2 * lax.rem(me_x, 2)
    ahead = [lax.rem(me_x + 2 * step, gx) for step in range(1, gx // 2)]
    behind = [lax.rem(me_x + gx - 2 * step, gx) for step in range(1, gx // 2)]

    def to_chips(ref, send, recv):
        return [
            remote(ref.at[me_x], ref.at[me_x], send.at[i], recv.at[i], (other, me_y)) for i, other in enumerate(ahead)
        ]

    def to_sibling(ref, send, recv):
        last = gx // 2 - 1
        return [
            remote(ref.at[x], ref.at[x], send.at[last + i], recv.at[last + i], (sibling, me_y))
            for i, x in enumerate([me_x] + behind)
        ]

    def spread(ref, send, recv):
        start(to_chips(ref, send, recv))
        to_sibling(ref, send, recv)[0].start()

    def collect(ref, send, recv):
        own, *passed = to_sibling(ref, send, recv)
        for arrival, copy in zip(to_chips(ref, send, recv), passed):
            arrival.wait()
            copy.start()
        wait([own] + passed)

    def start(copies):
        for copy in copies:
            copy.start()

    def wait(copies):
        for copy in copies:
            copy.wait()

    load_defl.wait()
    defl = defl_ref[...]
    defl_wide = defl.astype(f32)
    padded = jnp.concatenate([defl_wide, jnp.zeros((src - k, rows), f32)], axis=0).astype(bf16)
    extra[me_x, me_y, :, nc:] = lax.dot_general(
        defl, padded, (((1,), (1,)), ((), ())), preferred_element_type=f32
    )
    load_cinv.wait()
    pl.semaphore_wait(barrier, gx + gy - 2)

    extra_a = to_lines(extra.at[me_x, me_y], ea_send, ea_recv)
    start(extra_a)

    load_tdiag.wait()
    load_trace.wait()
    with_trace = defl_wide * tdiag_ref[...] + dot16(defl, trace_ref[...])
    small_ref[...] = jnp.concatenate(
        [defl_wide] + [piece.astype(f32) for piece in pieces(with_trace)], axis=0
    ).astype(bf16)

    def coarse_lines(t):
        return to_lines(main.at[t, me_x, me_y], a_send.at[t], a_recv.at[t])

    def start_coarse(t, rounded):
        out = dot16(small_ref[...], rounded)
        main[t, me_x, me_y, 0:k, :] = out[0:k]
        main[t, me_x, me_y, k : 2 * k, :] = out[k : 2 * k] + (out[2 * k : 3 * k] + out[3 * k : 4 * k])
        start(coarse_lines(t))

    def forward_coarse(t):
        wait(coarse_lines(t))
        spread(main.at[t], b_send.at[t], b_recv.at[t])

    def local_prec(rounded):
        return td_ref[...] * rounded.astype(f32) + dot16(trace_ref[...], rounded)

    def halo_copies(t, arriving):
        return [
            remote(
                halo_out.at[t, d],
                halo.at[t, d if arriving else d ^ 1],
                h_send.at[t, d],
                h_recv.at[t, d if arriving else d ^ 1],
                near[d][1],
            )
            for d in range(4)
        ]

    def send_halo(t, q):
        picked = exact_dot(pick_ref[...], q)
        for d in range(4):
            halo_out[t, d, :, :] = picked[d * ov : (d + 1) * ov]
        for d, copy in enumerate(halo_copies(t, False)):
            pl.when(near[d][0])(copy.start)

    def solve(t):
        collect(main.at[t], b_send.at[t], b_recv.at[t])
        coarse_all = jnp.concatenate([main[t, a, b, 0:k, :] for a in range(gx) for b in range(gy)], axis=0)
        dq_all = jnp.concatenate([main[t, a, b, k : 2 * k, :] for a in range(gx) for b in range(gy)], axis=0)
        both = dot16(both_ref[...], six(coarse_all, False))
        solved_ref[...] = both[0:nc]
        return both[0:nc], dq_all, dq_all + both[nc:]

    def solved_of(device):
        at = (device[0] * gy + device[1]) * k
        return jnp.concatenate(pieces(solved_ref[pl.ds(pl.multiple_of(at, k), k), :]), axis=0)

    def halo_mapped(t):
        for d, copy in enumerate(halo_copies(t, True)):
            pl.when(near[d][0])(copy.wait)
        return jnp.concatenate(
            [halo[t, d, :, :] + dot16(dht_ref[d, :, :], solved_of(near[d][1])) for d in range(4)], axis=0
        )

    load_rhs.wait()
    start_coarse(0, rhs_ref[...])

    load_rows.wait()
    for d in range(4):
        wanted = jnp.transpose(jnp.broadcast_to(rows_ref[d : d + 1, :].astype(f32), (ov, ov)))
        wanted = jnp.concatenate([wanted] * (rows // ov), axis=1).astype(jnp.int32)
        hot = wanted == lax.broadcasted_iota(jnp.int32, (ov, rows), 1)
        pick_ref[d * ov : (d + 1) * ov, :] = jnp.where(hot, 1.0, 0.0).astype(bf16)
    for d in range(4):
        halo_d_out[d, :, :] = lax.dot_general(
            defl, pick_ref[d * ov : (d + 1) * ov, :], (((1,), (1,)), ((), ())), preferred_element_type=f32
        )
        copy = remote(halo_d_out.at[d], halo_d.at[d ^ 1], hd_send.at[d], hd_recv.at[d ^ 1], near[d][1])
        pl.when(near[d][0])(copy.start)

    forward_coarse(0)
    wait(extra_a)
    spread(extra, eb_send, eb_recv)

    def column_of(ref):
        return jnp.transpose(jnp.broadcast_to(ref[...], (src, rows)))

    td_ref[...] = column_of(tdiag_ref)
    q0 = local_prec(rhs_ref[...])
    send_halo(0, q0)

    load_sdiag.wait()
    sd_ref[...] = column_of(sdiag_ref)
    load_coup.wait()
    for d in range(4):
        hot = rows_ref[d : d + 1, :] == lax.broadcasted_iota(jnp.int32, (rows, ov), 0)
        scattered = dot16(jnp.where(hot, -1.0, 0.0).astype(bf16), coup_ref[d, :, :])
        sb_ref[:, rows + d * ov : rows + (d + 1) * ov] = scattered.astype(bf16)
    dt_ref[...] = jnp.transpose(jnp.concatenate([defl_wide] * 3, axis=0)).astype(bf16)
    for d in range(4):
        arrival = remote(halo_d_out.at[d], halo_d.at[d], hd_send.at[d], hd_recv.at[d], near[d][1])
        pl.when(near[d][0])(arrival.wait)
        dht_ref[d, :, :] = jnp.transpose(jnp.concatenate([halo_d[d, :, :]] * 3, axis=0)).astype(bf16)
    load_cmap.wait()
    order = cmap_ref[...] == lax.broadcasted_iota(jnp.int32, (nc, nc), 0)
    order = jnp.where(order, 1.0, 0.0).astype(bf16)

    collect(extra, eb_send, eb_recv)
    blocks = [(a, b) for a in range(gx) for b in range(gy)]
    inverse = jnp.concatenate([extra[a, b, :, 0:nc] for a, b in blocks], axis=0)
    inverse = sum(dot16(piece, order) for piece in reversed(pieces(inverse)))
    gram = jnp.concatenate([extra[a, b, :, nc:] for a, b in blocks], axis=0)
    row = lax.broadcasted_iota(jnp.int32, (src, nc), 0)
    column = lax.broadcasted_iota(jnp.int32, (src, nc), 1)
    repeat = jnp.where(row == column % k, 1.0, 0.0).astype(bf16)
    gram = sum(dot16(piece, repeat) for piece in reversed(pieces(gram)))
    row = lax.broadcasted_iota(jnp.int32, (nc, nc), 0)
    column = lax.broadcasted_iota(jnp.int32, (nc, nc), 1)
    gram = jnp.where(row // k == column // k, gram, 0.0)
    both_ref[0:nc, :] = six(inverse, True)
    both_ref[nc:, :] = six(wide_dot(gram, inverse), True)

    solved, _, projected = solve(0)
    e_ref[...] = projected
    d_ref[...] = q0 + dot16(dt_ref[...], solved_of((me_x, me_y)))
    dh_ref[...] = halo_mapped(0)
    x_ref[...] = jnp.zeros_like(x_ref)
    xh_ref[...] = jnp.zeros_like(xh_ref)
    load_schur.wait()

    def schur(field_ref, margin_ref):
        v_ref[0:rows, :] = field_ref[...].astype(bf16)
        v_ref[rows:, :] = margin_ref[...].astype(bf16)
        return sd_ref[...] * v_ref[0:rows, :].astype(f32) + dot16(sb_ref[...], v_ref[...])

    def iteration(step, carry):
        t = step + 1
        more = t < iters
        rounded = schur(d_ref, dh_ref).astype(bf16)
        start_coarse(t, rounded)
        q = local_prec(rounded)
        sum_a[t, me_y, :, :] = jnp.concatenate(
            [
                jnp.sum(q * d_ref[...], axis=0, keepdims=True),
                jnp.sum(q * q, axis=0, keepdims=True),
                jnp.zeros((k - 2, src), f32),
            ],
            axis=0,
        )
        first = to_lines(sum_a.at[t, me_y], sa_send.at[t], sa_recv.at[t])
        start(first)
        forward_coarse(t)
        wait(first)
        total = sum_a[t, 0, :, :]
        for b in range(1, gy):
            total = total + sum_a[t, b, :, :]
        sum_b[t, me_x, :, :] = total
        second = to_columns(sum_b.at[t, me_x], sb_send.at[t], sb_recv.at[t])
        start(second)
        pl.when(more)(lambda: send_halo(t, q))
        solved, dq_all, projected = solve(t)
        numer = jnp.sum(solved * e_ref[...], axis=0, keepdims=True)
        denom = jnp.sum(solved * (dq_all + projected), axis=0, keepdims=True)
        wait(second)
        total = sum_b[t, 0, :, :]
        for a in range(1, gx):
            total = total + sum_b[t, a, :, :]
        alpha = (total[0:1] + numer) / (total[1:2] + denom)
        x_ref[...] += alpha * d_ref[...]
        xh_ref[...] += alpha * dh_ref[...]

        @pl.when(more)
        def _():
            d_ref[...] -= alpha * (q + dot16(dt_ref[...], solved_of((me_x, me_y))))
            e_ref[...] -= alpha * projected
            dh_ref[...] -= alpha * halo_mapped(t)

        return carry

    lax.fori_loop(0, iters, iteration, 0)
    res_ref[...] = rhs_ref[...].astype(f32) - schur(x_ref, xh_ref)


def hand_on(x_in, res_in, x_out, res_out, held, in_sem, out_sem):
    half = x_in.shape[0] // 2
    parts = [(i, j) for j in range(2) for i in range(2)]
    inward, outward = [], []
    for i, j in parts:
        source, target = (x_in, res_in)[i], (x_out, res_out)[i]
        here = pl.ds(j * half, half)
        inward.append(pltpu.make_async_copy(source.at[here], held.at[i, j], in_sem.at[i, j]))
        outward.append(pltpu.make_async_copy(held.at[i, j], target.at[here], out_sem.at[i, j]))
    for copy in inward:
        copy.start()
    for arrival, copy in zip(inward, outward):
        arrival.wait()
        copy.start()
    for copy in outward:
        copy.wait()


def one_kernel(gx, gy, *args):
    right_side, schur, sdiag, trace, tdiag, couplings, margin, deflation, inverse, coarse_map = args
    rows, src = right_side.shape[2:]
    ov = margin.shape[3]
    k = deflation.shape[2]
    nc = inverse.shape[1]
    f32, bf16 = jnp.float32, jnp.bfloat16
    rounds = ITERS + 1
    vmem, dma = pltpu.VMEM, pltpu.SemaphoreType.DMA
    x, residual = pl.pallas_call(
        functools.partial(kernel, gx, gy),
        out_shape=[jax.ShapeDtypeStruct((rows, src), f32)] * 2,
        in_specs=[pl.BlockSpec(memory_space=pl.ANY)] * 10,
        out_specs=[pl.BlockSpec(memory_space=pltpu.VMEM)] * 2,
        scratch_shapes=[
            vmem((rows, src), bf16),
            vmem((1, rows), f32),
            vmem((rows, rows), bf16),
            vmem((1, rows), f32),
            vmem((4, ov, ov), bf16),
            vmem((4, ov), jnp.int32),
            vmem((k, rows), bf16),
            vmem((1, nc), jnp.int32),
            dma((10,)),
            vmem((rows, rows + 4 * ov), bf16),
            vmem((4 * ov, rows), bf16),
            vmem((rows + 4 * ov, src), bf16),
            vmem((rows, src), f32),
            vmem((rows, src), f32),
            vmem((rows, src), f32),
            vmem((4 * ov, src), f32),
            vmem((4 * ov, src), f32),
            vmem((nc, src), f32),
            vmem((nc, src), f32),
            vmem((rows, 3 * k), bf16),
            vmem((4, ov, 3 * k), bf16),
            vmem((2 * nc, 6 * nc), bf16),
            vmem((4 * k, rows), bf16),
            vmem((rounds, gx, gy, 2 * k, src), f32),
            vmem((rounds, gy, k, src), f32),
            vmem((rounds, gx, k, src), f32),
            vmem((gx, gy, k, nc + src), f32),
            vmem((ITERS, 4, ov, src), f32),
            vmem((4, k, ov), f32),
            vmem((4, k, ov), f32),
            vmem((ITERS, 4, ov, src), f32),
            dma((rounds, gy - 1)),
            dma((rounds, gy - 1)),
            dma((rounds, gx - 1)),
            dma((rounds, gx - 1)),
            dma((rounds, gy - 1)),
            dma((rounds, gy - 1)),
            dma((rounds, gx - 1)),
            dma((rounds, gx - 1)),
            dma((gy - 1,)),
            dma((gy - 1,)),
            dma((gx - 1,)),
            dma((gx - 1,)),
            dma((ITERS, 4)),
            dma((ITERS, 4)),
            dma((4,)),
            dma((4,)),
        ],
        compiler_params=pltpu.CompilerParams(
            collective_id=0, has_side_effects=True, vmem_limit_bytes=60 * 1024 * 1024
        ),
        cost_estimate=pl.CostEstimate(flops=4_000_000_000, bytes_accessed=6_000_000, transcendentals=0),
    )(
        right_side[0, 0],
        schur[0, 0],
        sdiag[0],
        trace[0, 0],
        tdiag[0],
        couplings[0, 0],
        margin[0, 0],
        deflation[0, 0],
        inverse,
        coarse_map[None],
    )
    x, residual = pl.pallas_call(
        hand_on,
        out_shape=[jax.ShapeDtypeStruct((rows, src), f32)] * 2,
        in_specs=[pl.BlockSpec(memory_space=pl.ANY)] * 2,
        out_specs=[pl.BlockSpec(memory_space=pl.ANY)] * 2,
        compiler_params=pltpu.CompilerParams(vmem_limit_bytes=60 * 1024 * 1024),
        scratch_shapes=[vmem((2, 2, rows // 2, src), f32), dma((2, 2)), dma((2, 2))],
        cost_estimate=pl.CostEstimate(flops=0, bytes_accessed=16 * rows * src, transcendentals=0),
    )(x, residual)
    return x[None, None], residual[None, None]


def plan(gx, gy, *args):
    if gx % 2 == 0 and args[8].shape[1] <= REPLICATED_COARSE:
        return one_kernel(gx, gy, *args)
    return shards(*args)


def solution(mesh):
    return jax.shard_map(
        functools.partial(plan, mesh.shape["gx"], mesh.shape["gy"]),
        mesh=mesh,
        in_specs=(
            P("gx", "gy", None, None),
            P("gx", "gy", None, None),
            P("gx", "gy", None),
            P("gx", "gy", None, None),
            P("gx", "gy", None),
            P("gx", "gy", None, None, None),
            P("gx", "gy", None, None),
            P("gx", "gy", None, None),
            P(("gx", "gy"), None),
            P(),
        ),
        out_specs=(P("gx", "gy", None, None), P("gx", "gy", None, None)),
        check_vma=False,
    )
```

```python
import functools

import jax
import jax.numpy as jnp
from jax import lax
from jax.experimental import pallas as pl
from jax.experimental.pallas import tpu as pltpu
from jax.sharding import PartitionSpec as P

ITERS = 3


def from_behind(value, axis, steps):
    count = lax.axis_size(axis)
    leading, last = (max(0, -steps), min(count, count - steps))
    return lax.ppermute(value, axis, [(source, source + steps) for source in range(leading, last)])


def pass_columns(rows, offset):
    return from_behind(rows, "gx", offset)


def pass_lines(rows, offset):
    return from_behind(rows, "gy", offset)


def shards(
    right_side,
    schur_offdiag,
    schur_diag,
    trace_offdiag,
    trace_diag,
    couplings,
    margin_rows,
    deflation,
    coarse_inverse,
    coarse_map,
):
    rhs_wide = right_side[0, 0].astype(jnp.float32)
    schur_mat = schur_offdiag[0, 0]
    schur_scale = schur_diag[0, 0][:, None]
    trace_mat = trace_offdiag[0, 0]
    trace_scale = trace_diag[0, 0][:, None]
    coupling_blocks = couplings[0, 0]
    rows_lists = margin_rows[0, 0]
    flat_rows = rows_lists.reshape(-1)
    vectors = deflation[0, 0]
    vectors_wide = vectors.astype(jnp.float32).T
    coarse_cols = jnp.take(coarse_inverse, coarse_map, axis=1)

    def apply_schur(field):
        rounded = lax.optimization_barrier(field.astype(jnp.bfloat16))
        result = schur_scale * rounded.astype(jnp.float32) + jnp.dot(
            schur_mat, rounded, preferred_element_type=jnp.float32
        )
        sent_rows = rounded[rows_lists]
        received = jnp.stack(
            [
                pass_columns(sent_rows[1], 1),
                pass_columns(sent_rows[0], -1),
                pass_lines(sent_rows[3], 1),
                pass_lines(sent_rows[2], -1),
            ]
        )
        coupled = jnp.einsum(
            "dab,dbs->das", coupling_blocks, received, preferred_element_type=jnp.float32
        )
        return result.at[flat_rows].add(-coupled.reshape(-1, coupled.shape[-1]))

    def apply_prec(field):
        rounded = lax.optimization_barrier(field.astype(jnp.bfloat16))
        result = trace_scale * rounded.astype(jnp.float32) + jnp.dot(
            trace_mat, rounded, preferred_element_type=jnp.float32
        )
        coarse = jnp.dot(vectors, rounded, preferred_element_type=jnp.float32)
        stacked = lax.all_gather(coarse, ("gx", "gy"), axis=0, tiled=True)
        solved = jnp.dot(coarse_cols, stacked, precision=lax.Precision.HIGHEST)
        return result + jnp.dot(vectors_wide, solved, precision=lax.Precision.HIGHEST)

    solution = jnp.zeros(rhs_wide.shape, jnp.float32)
    direction = apply_prec(rhs_wide)
    for iteration in range(ITERS):
        image = apply_schur(direction)
        mapped = apply_prec(image)
        numer, denom = lax.psum(
            (jnp.sum(mapped * direction, axis=0), jnp.sum(mapped * mapped, axis=0)), ("gx", "gy")
        )
        alpha = numer / denom
        solution = solution + alpha * direction
        direction = direction - alpha * mapped
    residual = rhs_wide - apply_schur(solution)
    return (solution[None, None], residual[None, None])


MESH = pl.DeviceIdType.MESH
REPLICATED_COARSE = 512


def wide_dot(left, right):
    return jnp.dot(left, right, precision=lax.Precision.HIGHEST, preferred_element_type=jnp.float32)


def dot16(left, right):
    return jnp.dot(left, right, preferred_element_type=jnp.float32)


def pieces(value):
    high = value.astype(jnp.bfloat16)
    rest = value - high.astype(jnp.float32)
    middle = rest.astype(jnp.bfloat16)
    low = (rest - middle.astype(jnp.float32)).astype(jnp.bfloat16)
    return high, middle, low


def exact_dot(left, value):
    cols = value.shape[1]
    out = dot16(left, jnp.concatenate(pieces(value), axis=1))
    return out[:, :cols] + (out[:, cols : 2 * cols] + out[:, 2 * cols :])


def six(value, left):
    high, middle, low = pieces(value)
    if left:
        return jnp.concatenate([high, high, high, middle, middle, low], axis=1)
    return jnp.concatenate([high, middle, low, high, middle, high], axis=0)


def kernel(
    gx,
    gy,
    rhs_hbm,
    schur_hbm,
    sdiag_hbm,
    trace_hbm,
    tdiag_hbm,
    coup_hbm,
    rows_hbm,
    defl_hbm,
    cinv_hbm,
    cmap_hbm,
    x_ref,
    res_ref,
    rhs_ref,
    sdiag_ref,
    trace_ref,
    tdiag_ref,
    coup_ref,
    rows_ref,
    defl_ref,
    cmap_ref,
    load_sem,
    sb_ref,
    pick_ref,
    v_ref,
    sd_ref,
    td_ref,
    d_ref,
    dh_ref,
    xh_ref,
    e_ref,
    last_ref,
    alpha_ref,
    solved_ref,
    dt_ref,
    dht_ref,
    both_ref,
    small_ref,
    main,
    sum_a,
    sum_b,
    extra,
    halo,
    halo_d,
    halo_d_out,
    halo_out,
    a_send,
    a_recv,
    b_send,
    b_recv,
    sa_send,
    sa_recv,
    sb_send,
    sb_recv,
    ea_send,
    ea_recv,
    eb_send,
    eb_recv,
    h_send,
    h_recv,
    hd_send,
    hd_recv,
):
    f32, bf16 = jnp.float32, jnp.bfloat16
    rows, src = rhs_ref.shape
    ov = rows_ref.shape[1]
    k = defl_ref.shape[0]
    nc = cmap_ref.shape[1]
    me_x, me_y = lax.axis_index("gx"), lax.axis_index("gy")
    iters = ITERS

    def load(i, source, target):
        copy = pltpu.make_async_copy(source, target, load_sem.at[i])
        copy.start()
        return copy

    load_defl = load(0, defl_hbm, defl_ref)
    load_cinv = load(1, cinv_hbm, extra.at[me_x, me_y, :, pl.ds(0, nc)])
    load_tdiag = load(2, tdiag_hbm, tdiag_ref)
    load_rhs = load(3, rhs_hbm, rhs_ref)
    load_trace = load(4, trace_hbm, trace_ref)
    load_rows = load(5, rows_hbm, rows_ref)
    load_cmap = load(6, cmap_hbm, cmap_ref)
    load_sdiag = load(7, sdiag_hbm, sdiag_ref)
    load_coup = load(8, coup_hbm, coup_ref)
    load_schur = load(9, schur_hbm, sb_ref.at[:, pl.ds(0, rows)])

    along_x = [lax.rem(me_x + step, gx) for step in range(1, gx)]
    along_y = [lax.rem(me_y + step, gy) for step in range(1, gy)]
    near = [
        (me_x > 0, (jnp.maximum(me_x - 1, 0), me_y)),
        (me_x < gx - 1, (jnp.minimum(me_x + 1, gx - 1), me_y)),
        (me_y > 0, (me_x, jnp.maximum(me_y - 1, 0))),
        (me_y < gy - 1, (me_x, jnp.minimum(me_y + 1, gy - 1))),
    ]

    for d in range(4):

        @pl.when(jnp.logical_not(near[d][0]))
        def _():
            halo[:, d, :, :] = jnp.zeros((iters, ov, src), f32)
            halo_d[d, :, :] = jnp.zeros((k, ov), f32)

    barrier = pltpu.get_barrier_semaphore()
    for other in along_x:
        pl.semaphore_signal(barrier, inc=1, device_id=(other, me_y), device_id_type=MESH)
    for other in along_y:
        pl.semaphore_signal(barrier, inc=1, device_id=(me_x, other), device_id_type=MESH)

    def remote(source, target, send, recv, device):
        return pltpu.make_async_remote_copy(
            src_ref=source, dst_ref=target, send_sem=send, recv_sem=recv, device_id=device, device_id_type=MESH
        )

    def to_lines(ref, send, recv):
        return [remote(ref, ref, send.at[i], recv.at[i], (me_x, other)) for i, other in enumerate(along_y)]

    def to_columns(ref, send, recv):
        return [remote(ref, ref, send.at[i], recv.at[i], (other, me_y)) for i, other in enumerate(along_x)]

    sibling = me_x + 1 - 2 * lax.rem(me_x, 2)
    ahead = [lax.rem(me_x + 2 * step, gx) for step in range(1, gx // 2)]
    behind = [lax.rem(me_x + gx - 2 * step, gx) for step in range(1, gx // 2)]

    def to_chips(ref, send, recv):
        return [
            remote(ref.at[me_x], ref.at[me_x], send.at[i], recv.at[i], (other, me_y)) for i, other in enumerate(ahead)
        ]

    def to_sibling_one(ref, send, recv, i):
        at = gx // 2 - 1 + i
        block = ref.at[me_x if i == 0 else behind[i - 1]]
        return remote(block, block, send.at[at], recv.at[at], (sibling, me_y))

    def to_sibling(ref, send, recv):
        return [to_sibling_one(ref, send, recv, i) for i in range(gx // 2)]

    def spread(ref, send, recv):
        start(to_chips(ref, send, recv))
        to_sibling_one(ref, send, recv, 0).start()

    def pass_on(ref, send, recv):
        arrivals = to_chips(ref, send, recv)
        for arrival in arrivals:
            arrival.wait_send()
        for i, arrival in enumerate(arrivals):
            arrival.wait_recv()
            to_sibling_one(ref, send, recv, i + 1).start()

    def collect(ref, send, recv):
        wait(to_sibling(ref, send, recv))

    def start(copies):
        for copy in copies:
            copy.start()

    def wait(copies):
        for copy in copies:
            copy.wait_send()
        for copy in copies:
            copy.wait_recv()

    load_defl.wait()
    defl = defl_ref[...]
    defl_wide = defl.astype(f32)
    padded = jnp.concatenate([defl_wide, jnp.zeros((src - k, rows), f32)], axis=0).astype(bf16)
    extra[me_x, me_y, :, nc:] = lax.dot_general(
        defl, padded, (((1,), (1,)), ((), ())), preferred_element_type=f32
    )
    load_cinv.wait()
    pl.semaphore_wait(barrier, gx + gy - 2)

    extra_a = to_lines(extra.at[me_x, me_y], ea_send, ea_recv)
    start(extra_a)

    load_tdiag.wait()
    load_trace.wait()
    with_trace = defl_wide * tdiag_ref[...] + dot16(defl, trace_ref[...])
    small_ref[...] = jnp.concatenate(
        [defl_wide] + [piece.astype(f32) for piece in pieces(with_trace)], axis=0
    ).astype(bf16)

    def coarse_lines(t):
        return to_lines(main.at[t, me_x, me_y], a_send.at[t], a_recv.at[t])

    def start_coarse(t, rounded):
        out = dot16(small_ref[...], rounded)
        main[t, me_x, me_y, 0:k, :] = out[0:k]
        main[t, me_x, me_y, k : 2 * k, :] = out[k : 2 * k] + (out[2 * k : 3 * k] + out[3 * k : 4 * k])
        start(coarse_lines(t))

    def forward_coarse(t):
        wait(coarse_lines(t))
        spread(main.at[t], b_send.at[t], b_recv.at[t])

    def local_prec(rounded):
        return td_ref[...] * rounded.astype(f32) + dot16(trace_ref[...], rounded)

    def halo_copies(t, arriving):
        return [
            remote(
                halo_out.at[t, d],
                halo.at[t, d if arriving else d ^ 1],
                h_send.at[t, d],
                h_recv.at[t, d if arriving else d ^ 1],
                near[d][1],
            )
            for d in range(4)
        ]

    def send_halo(t, q):
        picked = exact_dot(pick_ref[...], q)
        for d in range(4):
            halo_out[t, d, :, :] = picked[d * ov : (d + 1) * ov]
        for d, copy in enumerate(halo_copies(t, False)):
            pl.when(near[d][0])(copy.start)

    def wait_halo(t):
        for d, copy in enumerate(halo_copies(t, True)):
            pl.when(near[d][0])(copy.wait)

    def solve(t):
        collect(main.at[t], b_send.at[t], b_recv.at[t])
        coarse_all = jnp.concatenate([main[t, a, b, 0:k, :] for a in range(gx) for b in range(gy)], axis=0)
        dq_all = jnp.concatenate([main[t, a, b, k : 2 * k, :] for a in range(gx) for b in range(gy)], axis=0)
        both = dot16(both_ref[...], six(coarse_all, False))
        solved_ref[...] = both[0:nc]
        return both[0:nc], dq_all, dq_all + both[nc:]

    def solved_of(device):
        at = (device[0] * gy + device[1]) * k
        return jnp.concatenate(pieces(solved_ref[pl.ds(pl.multiple_of(at, k), k), :]), axis=0)

    def halo_mapped(t):
        return jnp.concatenate(
            [halo[t, d, :, :] + dot16(dht_ref[d, :, :], solved_of(near[d][1])) for d in range(4)], axis=0
        )

    load_rhs.wait()
    start_coarse(0, rhs_ref[...])
    wait(extra_a)
    spread(extra, eb_send, eb_recv)

    load_rows.wait()
    for d in range(4):
        wanted = jnp.transpose(jnp.broadcast_to(rows_ref[d : d + 1, :].astype(f32), (ov, ov)))
        wanted = jnp.concatenate([wanted] * (rows // ov), axis=1).astype(jnp.int32)
        hot = wanted == lax.broadcasted_iota(jnp.int32, (ov, rows), 1)
        pick_ref[d * ov : (d + 1) * ov, :] = jnp.where(hot, 1.0, 0.0).astype(bf16)
    for d in range(4):
        halo_d_out[d, :, :] = lax.dot_general(
            defl, pick_ref[d * ov : (d + 1) * ov, :], (((1,), (1,)), ((), ())), preferred_element_type=f32
        )
        copy = remote(halo_d_out.at[d], halo_d.at[d ^ 1], hd_send.at[d], hd_recv.at[d ^ 1], near[d][1])
        pl.when(near[d][0])(copy.start)

    forward_coarse(0)

    def column_of(ref):
        return jnp.transpose(jnp.broadcast_to(ref[...], (src, rows)))

    td_ref[...] = column_of(tdiag_ref)
    q0 = local_prec(rhs_ref[...])
    send_halo(0, q0)
    pass_on(extra, eb_send, eb_recv)

    load_sdiag.wait()
    sd_ref[...] = column_of(sdiag_ref)
    load_coup.wait()
    for d in range(4):
        hot = rows_ref[d : d + 1, :] == lax.broadcasted_iota(jnp.int32, (rows, ov), 0)
        scattered = dot16(jnp.where(hot, -1.0, 0.0).astype(bf16), coup_ref[d, :, :])
        sb_ref[:, rows + d * ov : rows + (d + 1) * ov] = scattered.astype(bf16)
    dt_ref[...] = jnp.transpose(jnp.concatenate([defl_wide] * 3, axis=0)).astype(bf16)
    for d in range(4):
        arrival = remote(halo_d_out.at[d], halo_d.at[d], hd_send.at[d], hd_recv.at[d], near[d][1])
        pl.when(near[d][0])(arrival.wait)
        dht_ref[d, :, :] = jnp.transpose(jnp.concatenate([halo_d[d, :, :]] * 3, axis=0)).astype(bf16)
    pass_on(main.at[0], b_send.at[0], b_recv.at[0])
    load_cmap.wait()
    order = cmap_ref[...] == lax.broadcasted_iota(jnp.int32, (nc, nc), 0)
    order = jnp.where(order, 1.0, 0.0).astype(bf16)

    collect(extra, eb_send, eb_recv)
    blocks = [(a, b) for a in range(gx) for b in range(gy)]
    inverse = jnp.concatenate([extra[a, b, :, 0:nc] for a, b in blocks], axis=0)
    inverse = sum(dot16(piece, order) for piece in reversed(pieces(inverse)))
    gram = jnp.concatenate([extra[a, b, :, nc:] for a, b in blocks], axis=0)
    row = lax.broadcasted_iota(jnp.int32, (src, nc), 0)
    column = lax.broadcasted_iota(jnp.int32, (src, nc), 1)
    repeat = jnp.where(row == column % k, 1.0, 0.0).astype(bf16)
    gram = sum(dot16(piece, repeat) for piece in reversed(pieces(gram)))
    row = lax.broadcasted_iota(jnp.int32, (nc, nc), 0)
    column = lax.broadcasted_iota(jnp.int32, (nc, nc), 1)
    gram = jnp.where(row // k == column // k, gram, 0.0)
    both_ref[0:nc, :] = six(inverse, True)
    both_ref[nc:, :] = six(wide_dot(gram, inverse), True)

    x_ref[...] = jnp.zeros_like(x_ref)
    xh_ref[...] = jnp.zeros_like(xh_ref)
    d_ref[0, :, :] = jnp.zeros((rows, src), f32)
    dh_ref[0, :, :] = jnp.zeros((4 * ov, src), f32)
    alpha_ref[...] = jnp.zeros_like(alpha_ref)
    last_ref[...] = jnp.zeros_like(last_ref)
    load_schur.wait()
    wait_halo(0)
    solved, _, projected = solve(0)
    e_ref[...] = projected
    d_ref[1, :, :] = q0 + dot16(dt_ref[...], solved_of((me_x, me_y)))
    dh_ref[1, :, :] = halo_mapped(0)

    def schur(field, margin):
        v_ref[0:rows, :] = field.astype(bf16)
        v_ref[rows:, :] = margin.astype(bf16)
        return sd_ref[...] * v_ref[0:rows, :].astype(f32) + dot16(sb_ref[...], v_ref[...])

    def iteration(step, carry):
        t = step + 1
        now, other = t % 2, (t + 1) % 2
        more = t < iters
        rounded = schur(d_ref[now], dh_ref[now]).astype(bf16)
        start_coarse(t, rounded)
        q = local_prec(rounded)
        sum_a[t, me_y, :, :] = jnp.concatenate(
            [
                jnp.sum(q * d_ref[now], axis=0, keepdims=True),
                jnp.sum(q * q, axis=0, keepdims=True),
                jnp.zeros((k - 2, src), f32),
            ],
            axis=0,
        )
        first = to_lines(sum_a.at[t, me_y], sa_send.at[t], sa_recv.at[t])
        start(first)
        x_ref[...] += alpha_ref[0:1, :] * d_ref[other]
        xh_ref[...] += alpha_ref[0:1, :] * dh_ref[other]
        e_ref[...] -= alpha_ref[0:1, :] * last_ref[...]
        forward_coarse(t)
        wait(first)
        total = sum_a[t, 0, :, :]
        for b in range(1, gy):
            total = total + sum_a[t, b, :, :]
        sum_b[t, me_x, :, :] = total
        second = to_columns(sum_b.at[t, me_x], sb_send.at[t], sb_recv.at[t])
        start(second)
        pl.when(more)(lambda: send_halo(t, q))
        pass_on(main.at[t], b_send.at[t], b_recv.at[t])
        pl.when(more)(lambda: wait_halo(t))
        solved, dq_all, projected = solve(t)
        numer = jnp.sum(solved * e_ref[...], axis=0, keepdims=True)
        denom = jnp.sum(solved * (dq_all + projected), axis=0, keepdims=True)
        wait(second)
        total = sum_b[t, 0, :, :]
        for a in range(1, gx):
            total = total + sum_b[t, a, :, :]
        alpha = (total[0:1] + numer) / (total[1:2] + denom)
        alpha_ref[...] = jnp.broadcast_to(alpha, alpha_ref.shape)
        last_ref[...] = projected

        @pl.when(more)
        def _():
            d_ref[other, :, :] = d_ref[now] - alpha * (q + dot16(dt_ref[...], solved_of((me_x, me_y))))
            dh_ref[other, :, :] = dh_ref[now] - alpha * halo_mapped(t)

        return carry

    lax.fori_loop(0, iters, iteration, 0)
    x = x_ref[...] + alpha_ref[0:1, :] * d_ref[iters % 2]
    xh = xh_ref[...] + alpha_ref[0:1, :] * dh_ref[iters % 2]
    x_ref[...] = x
    res_ref[...] = rhs_ref[...].astype(f32) - schur(x, xh)


def hand_on(x_in, res_in, x_out, res_out, held, in_sem, out_sem):
    half = x_in.shape[0] // 2
    parts = [(i, j) for j in range(2) for i in range(2)]
    inward, outward = [], []
    for i, j in parts:
        source, target = (x_in, res_in)[i], (x_out, res_out)[i]
        here = pl.ds(j * half, half)
        inward.append(pltpu.make_async_copy(source.at[here], held.at[i, j], in_sem.at[i, j]))
        outward.append(pltpu.make_async_copy(held.at[i, j], target.at[here], out_sem.at[i, j]))
    for copy in inward:
        copy.start()
    for arrival, copy in zip(inward, outward):
        arrival.wait()
        copy.start()
    for copy in outward:
        copy.wait()


def one_kernel(gx, gy, *args):
    right_side, schur, sdiag, trace, tdiag, couplings, margin, deflation, inverse, coarse_map = args
    rows, src = right_side.shape[2:]
    ov = margin.shape[3]
    k = deflation.shape[2]
    nc = inverse.shape[1]
    f32, bf16 = jnp.float32, jnp.bfloat16
    rounds = ITERS + 1
    vmem, dma = pltpu.VMEM, pltpu.SemaphoreType.DMA
    x, residual = pl.pallas_call(
        functools.partial(kernel, gx, gy),
        out_shape=[jax.ShapeDtypeStruct((rows, src), f32)] * 2,
        in_specs=[pl.BlockSpec(memory_space=pl.ANY)] * 10,
        out_specs=[pl.BlockSpec(memory_space=pltpu.VMEM)] * 2,
        scratch_shapes=[
            vmem((rows, src), bf16),
            vmem((1, rows), f32),
            vmem((rows, rows), bf16),
            vmem((1, rows), f32),
            vmem((4, ov, ov), bf16),
            vmem((4, ov), jnp.int32),
            vmem((k, rows), bf16),
            vmem((1, nc), jnp.int32),
            dma((10,)),
            vmem((rows, rows + 4 * ov), bf16),
            vmem((4 * ov, rows), bf16),
            vmem((rows + 4 * ov, src), bf16),
            vmem((rows, src), f32),
            vmem((rows, src), f32),
            vmem((2, rows, src), f32),
            vmem((2, 4 * ov, src), f32),
            vmem((4 * ov, src), f32),
            vmem((nc, src), f32),
            vmem((nc, src), f32),
            vmem((8, src), f32),
            vmem((nc, src), f32),
            vmem((rows, 3 * k), bf16),
            vmem((4, ov, 3 * k), bf16),
            vmem((2 * nc, 6 * nc), bf16),
            vmem((4 * k, rows), bf16),
            vmem((rounds, gx, gy, 2 * k, src), f32),
            vmem((rounds, gy, k, src), f32),
            vmem((rounds, gx, k, src), f32),
            vmem((gx, gy, k, nc + src), f32),
            vmem((ITERS, 4, ov, src), f32),
            vmem((4, k, ov), f32),
            vmem((4, k, ov), f32),
            vmem((ITERS, 4, ov, src), f32),
            dma((rounds, gy - 1)),
            dma((rounds, gy - 1)),
            dma((rounds, gx - 1)),
            dma((rounds, gx - 1)),
            dma((rounds, gy - 1)),
            dma((rounds, gy - 1)),
            dma((rounds, gx - 1)),
            dma((rounds, gx - 1)),
            dma((gy - 1,)),
            dma((gy - 1,)),
            dma((gx - 1,)),
            dma((gx - 1,)),
            dma((ITERS, 4)),
            dma((ITERS, 4)),
            dma((4,)),
            dma((4,)),
        ],
        compiler_params=pltpu.CompilerParams(
            collective_id=0, has_side_effects=True, vmem_limit_bytes=60 * 1024 * 1024
        ),
        cost_estimate=pl.CostEstimate(flops=4_000_000_000, bytes_accessed=6_000_000, transcendentals=0),
    )(
        right_side[0, 0],
        schur[0, 0],
        sdiag[0],
        trace[0, 0],
        tdiag[0],
        couplings[0, 0],
        margin[0, 0],
        deflation[0, 0],
        inverse,
        coarse_map[None],
    )
    x, residual = pl.pallas_call(
        hand_on,
        out_shape=[jax.ShapeDtypeStruct((rows, src), f32)] * 2,
        in_specs=[pl.BlockSpec(memory_space=pl.ANY)] * 2,
        out_specs=[pl.BlockSpec(memory_space=pl.ANY)] * 2,
        compiler_params=pltpu.CompilerParams(vmem_limit_bytes=60 * 1024 * 1024),
        scratch_shapes=[vmem((2, 2, rows // 2, src), f32), dma((2, 2)), dma((2, 2))],
        cost_estimate=pl.CostEstimate(flops=0, bytes_accessed=16 * rows * src, transcendentals=0),
    )(x, residual)
    return x[None, None], residual[None, None]


def plan(gx, gy, *args):
    if gx % 2 == 0 and args[8].shape[1] <= REPLICATED_COARSE:
        return one_kernel(gx, gy, *args)
    return shards(*args)


def solution(mesh):
    return jax.shard_map(
        functools.partial(plan, mesh.shape["gx"], mesh.shape["gy"]),
        mesh=mesh,
        in_specs=(
            P("gx", "gy", None, None),
            P("gx", "gy", None, None),
            P("gx", "gy", None),
            P("gx", "gy", None, None),
            P("gx", "gy", None),
            P("gx", "gy", None, None, None),
            P("gx", "gy", None, None),
            P("gx", "gy", None, None),
            P(("gx", "gy"), None),
            P(),
        ),
        out_specs=(P("gx", "gy", None, None), P("gx", "gy", None, None)),
        check_vma=False,
    )
```

```python
import functools

import jax
import jax.numpy as jnp
from jax import lax
from jax.experimental import pallas as pl
from jax.experimental.pallas import tpu as pltpu
from jax.sharding import PartitionSpec as P

ITERS = 3


def from_behind(value, axis, steps):
    count = lax.axis_size(axis)
    leading, last = (max(0, -steps), min(count, count - steps))
    return lax.ppermute(value, axis, [(source, source + steps) for source in range(leading, last)])


def pass_columns(rows, offset):
    return from_behind(rows, "gx", offset)


def pass_lines(rows, offset):
    return from_behind(rows, "gy", offset)


def shards(
    right_side,
    schur_offdiag,
    schur_diag,
    trace_offdiag,
    trace_diag,
    couplings,
    margin_rows,
    deflation,
    coarse_inverse,
    coarse_map,
):
    rhs_wide = right_side[0, 0].astype(jnp.float32)
    schur_mat = schur_offdiag[0, 0]
    schur_scale = schur_diag[0, 0][:, None]
    trace_mat = trace_offdiag[0, 0]
    trace_scale = trace_diag[0, 0][:, None]
    coupling_blocks = couplings[0, 0]
    rows_lists = margin_rows[0, 0]
    flat_rows = rows_lists.reshape(-1)
    vectors = deflation[0, 0]
    vectors_wide = vectors.astype(jnp.float32).T
    coarse_cols = jnp.take(coarse_inverse, coarse_map, axis=1)

    def apply_schur(field):
        rounded = lax.optimization_barrier(field.astype(jnp.bfloat16))
        result = schur_scale * rounded.astype(jnp.float32) + jnp.dot(
            schur_mat, rounded, preferred_element_type=jnp.float32
        )
        sent_rows = rounded[rows_lists]
        received = jnp.stack(
            [
                pass_columns(sent_rows[1], 1),
                pass_columns(sent_rows[0], -1),
                pass_lines(sent_rows[3], 1),
                pass_lines(sent_rows[2], -1),
            ]
        )
        coupled = jnp.einsum(
            "dab,dbs->das", coupling_blocks, received, preferred_element_type=jnp.float32
        )
        return result.at[flat_rows].add(-coupled.reshape(-1, coupled.shape[-1]))

    def apply_prec(field):
        rounded = lax.optimization_barrier(field.astype(jnp.bfloat16))
        result = trace_scale * rounded.astype(jnp.float32) + jnp.dot(
            trace_mat, rounded, preferred_element_type=jnp.float32
        )
        coarse = jnp.dot(vectors, rounded, preferred_element_type=jnp.float32)
        stacked = lax.all_gather(coarse, ("gx", "gy"), axis=0, tiled=True)
        solved = jnp.dot(coarse_cols, stacked, precision=lax.Precision.HIGHEST)
        return result + jnp.dot(vectors_wide, solved, precision=lax.Precision.HIGHEST)

    solution = jnp.zeros(rhs_wide.shape, jnp.float32)
    direction = apply_prec(rhs_wide)
    for iteration in range(ITERS):
        image = apply_schur(direction)
        mapped = apply_prec(image)
        numer, denom = lax.psum(
            (jnp.sum(mapped * direction, axis=0), jnp.sum(mapped * mapped, axis=0)), ("gx", "gy")
        )
        alpha = numer / denom
        solution = solution + alpha * direction
        direction = direction - alpha * mapped
    residual = rhs_wide - apply_schur(solution)
    return (solution[None, None], residual[None, None])


MESH = pl.DeviceIdType.MESH
LARGEST_COARSE = 512


def wide_dot(left, right):
    return jnp.dot(left, right, precision=lax.Precision.HIGHEST, preferred_element_type=jnp.float32)


def dot16(left, right):
    return jnp.dot(left, right, preferred_element_type=jnp.float32)


def pieces(value):
    high = value.astype(jnp.bfloat16)
    rest = value - high.astype(jnp.float32)
    middle = rest.astype(jnp.bfloat16)
    low = (rest - middle.astype(jnp.float32)).astype(jnp.bfloat16)
    return high, middle, low


def exact_dot(left, value):
    cols = value.shape[1]
    out = dot16(left, jnp.concatenate(pieces(value), axis=1))
    return out[:, :cols] + (out[:, cols : 2 * cols] + out[:, 2 * cols :])


def six(value, left):
    high, middle, low = pieces(value)
    if left:
        return jnp.concatenate([high, high, high, middle, middle, low], axis=1)
    return jnp.concatenate([high, middle, low, high, middle, high], axis=0)


def kernel(
    gx,
    gy,
    rhs_hbm,
    schur_hbm,
    sdiag_hbm,
    trace_hbm,
    tdiag_hbm,
    coup_hbm,
    rows_hbm,
    defl_hbm,
    cinv_hbm,
    cmap_hbm,
    x_ref,
    res_ref,
    rhs_ref,
    sdiag_ref,
    trace_ref,
    tdiag_ref,
    coup_ref,
    rows_ref,
    defl_ref,
    cmap_ref,
    load_sem,
    sb_ref,
    pick_ref,
    v_ref,
    sd_ref,
    td_ref,
    d_ref,
    dh_ref,
    xh_ref,
    e_ref,
    last_ref,
    alpha_ref,
    solved_ref,
    dt_ref,
    dht_ref,
    both_ref,
    small_ref,
    mapped_ref,
    main,
    tail,
    sum_b,
    extra,
    halo,
    halo_d,
    halo_d_out,
    halo_out,
    a_send,
    a_recv,
    b_send,
    b_recv,
    sa_send,
    sa_recv,
    sb_send,
    sb_recv,
    ea_send,
    ea_recv,
    en_send,
    en_recv,
    h_send,
    h_recv,
    hd_send,
    hd_recv,
):
    f32, bf16 = jnp.float32, jnp.bfloat16
    rows, src = rhs_ref.shape
    ov = rows_ref.shape[1]
    k = defl_ref.shape[0]
    nc = cmap_ref.shape[1]
    me_x, me_y = lax.axis_index("gx"), lax.axis_index("gy")
    iters = ITERS

    def load(i, source, target):
        copy = pltpu.make_async_copy(source, target, load_sem.at[i])
        copy.start()
        return copy

    load_defl = load(0, defl_hbm, defl_ref)
    load_cinv = load(1, cinv_hbm, extra.at[me_y, :, pl.ds(0, nc)])
    load_tdiag = load(2, tdiag_hbm, tdiag_ref)
    load_rhs = load(3, rhs_hbm, rhs_ref)
    load_trace = load(4, trace_hbm, trace_ref)
    load_rows = load(5, rows_hbm, rows_ref)
    load_cmap = load(6, cmap_hbm, cmap_ref)
    load_sdiag = load(7, sdiag_hbm, sdiag_ref)
    load_coup = load(8, coup_hbm, coup_ref)
    load_schur = load(9, schur_hbm, sb_ref.at[:, pl.ds(0, rows)])

    along_x = [lax.rem(me_x + step, gx) for step in range(1, gx)]
    along_y = [lax.rem(me_y + step, gy) for step in range(1, gy)]
    near = [
        (me_x > 0, (jnp.maximum(me_x - 1, 0), me_y)),
        (me_x < gx - 1, (jnp.minimum(me_x + 1, gx - 1), me_y)),
        (me_y > 0, (me_x, jnp.maximum(me_y - 1, 0))),
        (me_y < gy - 1, (me_x, jnp.minimum(me_y + 1, gy - 1))),
    ]

    for d in range(4):

        @pl.when(jnp.logical_not(near[d][0]))
        def _():
            halo[:, d, :, :] = jnp.zeros((iters, ov, src), f32)
            halo_d[d, :, :] = jnp.zeros((k, ov), f32)
            if d < 2:
                extra[gy + d, :, :] = jnp.zeros((k, nc + src), f32)

    barrier = pltpu.get_barrier_semaphore()
    for other in along_x:
        pl.semaphore_signal(barrier, inc=1, device_id=(other, me_y), device_id_type=MESH)
    for other in along_y:
        pl.semaphore_signal(barrier, inc=1, device_id=(me_x, other), device_id_type=MESH)

    def remote(source, target, send, recv, device):
        return pltpu.make_async_remote_copy(
            src_ref=source, dst_ref=target, send_sem=send, recv_sem=recv, device_id=device, device_id_type=MESH
        )

    def to_lines(ref, send, recv):
        return [remote(ref, ref, send.at[i], recv.at[i], (me_x, other)) for i, other in enumerate(along_y)]

    def to_columns(ref, send, recv):
        return [remote(ref, ref, send.at[i], recv.at[i], (other, me_y)) for i, other in enumerate(along_x)]

    def start(copies):
        for copy in copies:
            copy.start()

    def wait(copies):
        for copy in copies:
            copy.wait_send()
        for copy in copies:
            copy.wait_recv()

    load_defl.wait()
    defl = defl_ref[...]
    defl_wide = defl.astype(f32)
    padded = jnp.concatenate([defl_wide, jnp.zeros((src - k, rows), f32)], axis=0).astype(bf16)
    extra[me_y, :, nc:] = lax.dot_general(
        defl, padded, (((1,), (1,)), ((), ())), preferred_element_type=f32
    )
    load_cinv.wait()
    pl.semaphore_wait(barrier, gx + gy - 2)

    extra_a = to_lines(extra.at[me_y], ea_send, ea_recv)
    start(extra_a)

    def extra_near(d, arriving):
        slot = d if arriving else d ^ 1
        return remote(extra.at[me_y], extra.at[gy + slot], en_send.at[d], en_recv.at[slot], near[d][1])

    for d in range(2):
        pl.when(near[d][0])(extra_near(d, False).start)

    load_tdiag.wait()
    load_trace.wait()
    with_trace = defl_wide * tdiag_ref[...] + dot16(defl, trace_ref[...])
    small_ref[...] = jnp.concatenate(
        [defl_wide] + [piece.astype(f32) for piece in pieces(with_trace)], axis=0
    ).astype(bf16)

    def coarse_lines(t):
        return to_lines(main.at[t, me_x, me_y], a_send.at[t], a_recv.at[t])

    def start_coarse(t, rounded):
        out = dot16(small_ref[...], rounded)
        main[t, me_x, me_y, :, :] = out[0:k]
        start(coarse_lines(t))
        tail[t, me_y, 0:k, :] = out[k : 2 * k] + (out[2 * k : 3 * k] + out[3 * k : 4 * k])

    def coarse_columns(t):
        return to_columns(main.at[t, me_x], b_send.at[t], b_recv.at[t])

    def forward_coarse(t):
        wait(coarse_lines(t))
        start(coarse_columns(t))

    def tail_lines(t):
        return to_lines(tail.at[t, me_y], sa_send.at[t], sa_recv.at[t])

    def local_prec(rounded):
        return td_ref[...] * rounded.astype(f32) + dot16(trace_ref[...], rounded)

    def halo_copies(t, arriving):
        return [
            remote(
                halo_out.at[t, d],
                halo.at[t, d if arriving else d ^ 1],
                h_send.at[t, d],
                h_recv.at[t, d if arriving else d ^ 1],
                near[d][1],
            )
            for d in range(4)
        ]

    def send_halo(t, q):
        picked = exact_dot(pick_ref[...], q)
        for d in range(4):
            halo_out[t, d, :, :] = picked[d * ov : (d + 1) * ov]
        for d, copy in enumerate(halo_copies(t, False)):
            pl.when(near[d][0])(copy.start)

    def wait_halo(t):
        for d, copy in enumerate(halo_copies(t, True)):
            pl.when(near[d][0])(copy.wait)

    line = gy * k
    blocks = line + 2 * k

    def solve(t):
        wait(coarse_columns(t))
        coarse_all = jnp.concatenate([main[t, a, b, :, :] for a in range(gx) for b in range(gy)], axis=0)
        both = dot16(both_ref[...], six(coarse_all, False))
        solved_ref[...] = both[0:blocks]
        dq = jnp.concatenate([tail[t, b, 0:k, :] for b in range(gy)], axis=0)
        return both[0:line], dq, dq + both[blocks:]

    solved_at = [line, line + k, near[2][1][1] * k, near[3][1][1] * k]

    def solved_of(at):
        return jnp.concatenate(pieces(solved_ref[pl.ds(pl.multiple_of(at, k), k), :]), axis=0)

    def halo_mapped(t):
        return jnp.concatenate(
            [halo[t, d, :, :] + dot16(dht_ref[d, :, :], solved_of(solved_at[d])) for d in range(4)], axis=0
        )

    load_rhs.wait()
    start_coarse(0, rhs_ref[...])
    tail[0, me_y, k:, :] = jnp.zeros((k, src), f32)
    start(tail_lines(0))

    load_rows.wait()
    for d in range(4):
        wanted = jnp.transpose(jnp.broadcast_to(rows_ref[d : d + 1, :].astype(f32), (ov, ov)))
        wanted = jnp.concatenate([wanted] * (rows // ov), axis=1).astype(jnp.int32)
        hot = wanted == lax.broadcasted_iota(jnp.int32, (ov, rows), 1)
        pick_ref[d * ov : (d + 1) * ov, :] = jnp.where(hot, 1.0, 0.0).astype(bf16)
    for d in range(4):
        halo_d_out[d, :, :] = lax.dot_general(
            defl, pick_ref[d * ov : (d + 1) * ov, :], (((1,), (1,)), ((), ())), preferred_element_type=f32
        )
        copy = remote(halo_d_out.at[d], halo_d.at[d ^ 1], hd_send.at[d], hd_recv.at[d ^ 1], near[d][1])
        pl.when(near[d][0])(copy.start)

    forward_coarse(0)

    def column_of(ref):
        return jnp.transpose(jnp.broadcast_to(ref[...], (src, rows)))

    td_ref[...] = column_of(tdiag_ref)
    q0 = local_prec(rhs_ref[...])
    send_halo(0, q0)

    load_sdiag.wait()
    sd_ref[...] = column_of(sdiag_ref)
    load_coup.wait()
    for d in range(4):
        hot = rows_ref[d : d + 1, :] == lax.broadcasted_iota(jnp.int32, (rows, ov), 0)
        scattered = dot16(jnp.where(hot, -1.0, 0.0).astype(bf16), coup_ref[d, :, :])
        sb_ref[:, rows + d * ov : rows + (d + 1) * ov] = scattered.astype(bf16)
    dt_ref[...] = jnp.transpose(jnp.concatenate([defl_wide] * 3, axis=0)).astype(bf16)
    for d in range(4):
        arrival = remote(halo_d_out.at[d], halo_d.at[d], hd_send.at[d], hd_recv.at[d], near[d][1])
        pl.when(near[d][0])(arrival.wait)
        dht_ref[d, :, :] = jnp.transpose(jnp.concatenate([halo_d[d, :, :]] * 3, axis=0)).astype(bf16)
    load_cmap.wait()
    order = cmap_ref[...] == lax.broadcasted_iota(jnp.int32, (nc, nc), 0)
    order = jnp.where(order, 1.0, 0.0).astype(bf16)

    wait(extra_a)
    for d in range(2):
        pl.when(near[d][0])(extra_near(d, True).wait)
    inverse = jnp.concatenate([extra[b, :, 0:nc] for b in range(gy + 2)], axis=0)
    inverse = sum(dot16(piece, order) for piece in reversed(pieces(inverse)))
    gram = jnp.concatenate([extra[b, :, nc:] for b in range(gy)], axis=0)
    row = lax.broadcasted_iota(jnp.int32, (src, src), 0)
    column = lax.broadcasted_iota(jnp.int32, (src, src), 1)
    repeat = jnp.where((row == column % k) & (column < line), 1.0, 0.0).astype(bf16)
    gram = sum(dot16(piece, repeat) for piece in reversed(pieces(gram)))
    row = lax.broadcasted_iota(jnp.int32, (line, src), 0)
    column = lax.broadcasted_iota(jnp.int32, (line, src), 1)
    gram = jnp.where(row // k == column // k, gram, 0.0)
    lined = jnp.concatenate([inverse[0:line], jnp.zeros((src - line, nc), f32)], axis=0)
    both_ref[0:blocks, :] = six(inverse, True)
    both_ref[blocks:, :] = six(wide_dot(gram, lined), True)

    x_ref[...] = jnp.zeros_like(x_ref)
    xh_ref[...] = jnp.zeros_like(xh_ref)
    d_ref[0, :, :] = jnp.zeros((rows, src), f32)
    dh_ref[0, :, :] = jnp.zeros((4 * ov, src), f32)
    alpha_ref[...] = jnp.zeros_like(alpha_ref)
    last_ref[...] = jnp.zeros_like(last_ref)
    load_schur.wait()
    wait_halo(0)
    wait(tail_lines(0))
    solved, _, projected = solve(0)
    e_ref[...] = projected
    d_ref[1, :, :] = q0 + dot16(dt_ref[...], solved_of(me_y * k))
    dh_ref[1, :, :] = halo_mapped(0)

    def schur(field, margin):
        v_ref[0:rows, :] = field.astype(bf16)
        v_ref[rows:, :] = margin.astype(bf16)
        return sd_ref[...] * v_ref[0:rows, :].astype(f32) + dot16(sb_ref[...], v_ref[...])

    def iteration(step, carry):
        t = step + 1
        now, other = t % 2, (t + 1) % 2
        more = t < iters
        rounded = schur(d_ref[now], dh_ref[now]).astype(bf16)
        start_coarse(t, rounded)
        q = local_prec(rounded)
        tail[t, me_y, k:, :] = jnp.concatenate(
            [
                jnp.sum(q * d_ref[now], axis=0, keepdims=True),
                jnp.sum(q * q, axis=0, keepdims=True),
                jnp.zeros((k - 2, src), f32),
            ],
            axis=0,
        )
        start(tail_lines(t))
        x_ref[...] += alpha_ref[0:1, :] * d_ref[other]
        xh_ref[...] += alpha_ref[0:1, :] * dh_ref[other]
        e_ref[...] -= alpha_ref[0:1, :] * last_ref[...]
        forward_coarse(t)
        pl.when(more)(lambda: send_halo(t, q))
        wait(tail_lines(t))
        pl.when(more)(lambda: wait_halo(t))
        solved, dq, projected = solve(t)
        total = tail[t, 0, k:, :]
        for b in range(1, gy):
            total = total + tail[t, b, k:, :]
        numer = total[0:1] + jnp.sum(solved * e_ref[...], axis=0, keepdims=True)
        denom = total[1:2] + jnp.sum(solved * (dq + projected), axis=0, keepdims=True)
        sum_b[t, me_x, :, :] = jnp.concatenate([numer, denom, jnp.zeros((k - 2, src), f32)], axis=0)
        second = to_columns(sum_b.at[t, me_x], sb_send.at[t], sb_recv.at[t])
        start(second)
        last_ref[...] = projected

        @pl.when(more)
        def _():
            mapped_ref[0:rows, :] = q + dot16(dt_ref[...], solved_of(me_y * k))
            mapped_ref[rows:, :] = halo_mapped(t)

        wait(second)
        total = sum_b[t, 0, :, :]
        for a in range(1, gx):
            total = total + sum_b[t, a, :, :]
        alpha = total[0:1] / total[1:2]
        alpha_ref[...] = jnp.broadcast_to(alpha, alpha_ref.shape)

        @pl.when(more)
        def _():
            d_ref[other, :, :] = d_ref[now] - alpha * mapped_ref[0:rows, :]
            dh_ref[other, :, :] = dh_ref[now] - alpha * mapped_ref[rows:, :]

        return carry

    lax.fori_loop(0, iters, iteration, 0)
    x = x_ref[...] + alpha_ref[0:1, :] * d_ref[iters % 2]
    xh = xh_ref[...] + alpha_ref[0:1, :] * dh_ref[iters % 2]
    x_ref[...] = x
    res_ref[...] = rhs_ref[...].astype(f32) - schur(x, xh)


def hand_on(x_in, res_in, x_out, res_out, held, in_sem, out_sem):
    half = x_in.shape[0] // 2
    parts = [(i, j) for j in range(2) for i in range(2)]
    inward, outward = [], []
    for i, j in parts:
        source, target = (x_in, res_in)[i], (x_out, res_out)[i]
        here = pl.ds(j * half, half)
        inward.append(pltpu.make_async_copy(source.at[here], held.at[i, j], in_sem.at[i, j]))
        outward.append(pltpu.make_async_copy(held.at[i, j], target.at[here], out_sem.at[i, j]))
    for copy in inward:
        copy.start()
    for arrival, copy in zip(inward, outward):
        arrival.wait()
        copy.start()
    for copy in outward:
        copy.wait()


def one_kernel(gx, gy, *args):
    right_side, schur, sdiag, trace, tdiag, couplings, margin, deflation, inverse, coarse_map = args
    rows, src = right_side.shape[2:]
    ov = margin.shape[3]
    k = deflation.shape[2]
    nc = inverse.shape[1]
    f32, bf16 = jnp.float32, jnp.bfloat16
    rounds = ITERS + 1
    vmem, dma = pltpu.VMEM, pltpu.SemaphoreType.DMA
    x, residual = pl.pallas_call(
        functools.partial(kernel, gx, gy),
        out_shape=[jax.ShapeDtypeStruct((rows, src), f32)] * 2,
        in_specs=[pl.BlockSpec(memory_space=pl.ANY)] * 10,
        out_specs=[pl.BlockSpec(memory_space=pltpu.VMEM)] * 2,
        scratch_shapes=[
            vmem((rows, src), bf16),
            vmem((1, rows), f32),
            vmem((rows, rows), bf16),
            vmem((1, rows), f32),
            vmem((4, ov, ov), bf16),
            vmem((4, ov), jnp.int32),
            vmem((k, rows), bf16),
            vmem((1, nc), jnp.int32),
            dma((10,)),
            vmem((rows, rows + 4 * ov), bf16),
            vmem((4 * ov, rows), bf16),
            vmem((rows + 4 * ov, src), bf16),
            vmem((rows, src), f32),
            vmem((rows, src), f32),
            vmem((2, rows, src), f32),
            vmem((2, 4 * ov, src), f32),
            vmem((4 * ov, src), f32),
            vmem((gy * k, src), f32),
            vmem((gy * k, src), f32),
            vmem((8, src), f32),
            vmem(((gy + 2) * k, src), f32),
            vmem((rows, 3 * k), bf16),
            vmem((4, ov, 3 * k), bf16),
            vmem(((2 * gy + 2) * k, 6 * nc), bf16),
            vmem((4 * k, rows), bf16),
            vmem((rows + 4 * ov, src), f32),
            vmem((rounds, gx, gy, k, src), f32),
            vmem((rounds, gy, 2 * k, src), f32),
            vmem((rounds, gx, k, src), f32),
            vmem((gy + 2, k, nc + src), f32),
            vmem((ITERS, 4, ov, src), f32),
            vmem((4, k, ov), f32),
            vmem((4, k, ov), f32),
            vmem((ITERS, 4, ov, src), f32),
            dma((rounds, gy - 1)),
            dma((rounds, gy - 1)),
            dma((rounds, gx - 1)),
            dma((rounds, gx - 1)),
            dma((rounds, gy - 1)),
            dma((rounds, gy - 1)),
            dma((rounds, gx - 1)),
            dma((rounds, gx - 1)),
            dma((gy - 1,)),
            dma((gy - 1,)),
            dma((2,)),
            dma((2,)),
            dma((ITERS, 4)),
            dma((ITERS, 4)),
            dma((4,)),
            dma((4,)),
        ],
        compiler_params=pltpu.CompilerParams(
            collective_id=0, has_side_effects=True, vmem_limit_bytes=60 * 1024 * 1024
        ),
        cost_estimate=pl.CostEstimate(flops=4_000_000_000, bytes_accessed=6_000_000, transcendentals=0),
    )(
        right_side[0, 0],
        schur[0, 0],
        sdiag[0],
        trace[0, 0],
        tdiag[0],
        couplings[0, 0],
        margin[0, 0],
        deflation[0, 0],
        inverse,
        coarse_map[None],
    )
    x, residual = pl.pallas_call(
        hand_on,
        out_shape=[jax.ShapeDtypeStruct((rows, src), f32)] * 2,
        in_specs=[pl.BlockSpec(memory_space=pl.ANY)] * 2,
        out_specs=[pl.BlockSpec(memory_space=pl.ANY)] * 2,
        compiler_params=pltpu.CompilerParams(vmem_limit_bytes=60 * 1024 * 1024),
        scratch_shapes=[vmem((2, 2, rows // 2, src), f32), dma((2, 2)), dma((2, 2))],
        cost_estimate=pl.CostEstimate(flops=0, bytes_accessed=16 * rows * src, transcendentals=0),
    )(x, residual)
    return x[None, None], residual[None, None]


def plan(gx, gy, *args):
    if args[8].shape[1] <= LARGEST_COARSE:
        return one_kernel(gx, gy, *args)
    return shards(*args)


def solution(mesh):
    return jax.shard_map(
        functools.partial(plan, mesh.shape["gx"], mesh.shape["gy"]),
        mesh=mesh,
        in_specs=(
            P("gx", "gy", None, None),
            P("gx", "gy", None, None),
            P("gx", "gy", None),
            P("gx", "gy", None, None),
            P("gx", "gy", None),
            P("gx", "gy", None, None, None),
            P("gx", "gy", None, None),
            P("gx", "gy", None, None),
            P(("gx", "gy"), None),
            P(),
        ),
        out_specs=(P("gx", "gy", None, None), P("gx", "gy", None, None)),
        check_vma=False,
    )
```

```python
import functools

import jax
import jax.numpy as jnp
from jax import lax
from jax.experimental import pallas as pl
from jax.experimental.pallas import tpu as pltpu
from jax.sharding import PartitionSpec as P

ITERS = 3


def from_behind(value, axis, steps):
    count = lax.axis_size(axis)
    leading, last = (max(0, -steps), min(count, count - steps))
    return lax.ppermute(value, axis, [(source, source + steps) for source in range(leading, last)])


def pass_columns(rows, offset):
    return from_behind(rows, "gx", offset)


def pass_lines(rows, offset):
    return from_behind(rows, "gy", offset)


def shards(
    right_side,
    schur_offdiag,
    schur_diag,
    trace_offdiag,
    trace_diag,
    couplings,
    margin_rows,
    deflation,
    coarse_inverse,
    coarse_map,
):
    rhs_wide = right_side[0, 0].astype(jnp.float32)
    schur_mat = schur_offdiag[0, 0]
    schur_scale = schur_diag[0, 0][:, None]
    trace_mat = trace_offdiag[0, 0]
    trace_scale = trace_diag[0, 0][:, None]
    coupling_blocks = couplings[0, 0]
    rows_lists = margin_rows[0, 0]
    flat_rows = rows_lists.reshape(-1)
    vectors = deflation[0, 0]
    vectors_wide = vectors.astype(jnp.float32).T
    coarse_cols = jnp.take(coarse_inverse, coarse_map, axis=1)

    def apply_schur(field):
        rounded = lax.optimization_barrier(field.astype(jnp.bfloat16))
        result = schur_scale * rounded.astype(jnp.float32) + jnp.dot(
            schur_mat, rounded, preferred_element_type=jnp.float32
        )
        sent_rows = rounded[rows_lists]
        received = jnp.stack(
            [
                pass_columns(sent_rows[1], 1),
                pass_columns(sent_rows[0], -1),
                pass_lines(sent_rows[3], 1),
                pass_lines(sent_rows[2], -1),
            ]
        )
        coupled = jnp.einsum(
            "dab,dbs->das", coupling_blocks, received, preferred_element_type=jnp.float32
        )
        return result.at[flat_rows].add(-coupled.reshape(-1, coupled.shape[-1]))

    def apply_prec(field):
        rounded = lax.optimization_barrier(field.astype(jnp.bfloat16))
        result = trace_scale * rounded.astype(jnp.float32) + jnp.dot(
            trace_mat, rounded, preferred_element_type=jnp.float32
        )
        coarse = jnp.dot(vectors, rounded, preferred_element_type=jnp.float32)
        stacked = lax.all_gather(coarse, ("gx", "gy"), axis=0, tiled=True)
        solved = jnp.dot(coarse_cols, stacked, precision=lax.Precision.HIGHEST)
        return result + jnp.dot(vectors_wide, solved, precision=lax.Precision.HIGHEST)

    solution = jnp.zeros(rhs_wide.shape, jnp.float32)
    direction = apply_prec(rhs_wide)
    for iteration in range(ITERS):
        image = apply_schur(direction)
        mapped = apply_prec(image)
        numer, denom = lax.psum(
            (jnp.sum(mapped * direction, axis=0), jnp.sum(mapped * mapped, axis=0)), ("gx", "gy")
        )
        alpha = numer / denom
        solution = solution + alpha * direction
        direction = direction - alpha * mapped
    residual = rhs_wide - apply_schur(solution)
    return (solution[None, None], residual[None, None])


MESH = pl.DeviceIdType.MESH
REPLICATED_COARSE = 512


def wide_dot(left, right):
    return jnp.dot(left, right, precision=lax.Precision.HIGHEST, preferred_element_type=jnp.float32)


def dot16(left, right):
    return jnp.dot(left, right, preferred_element_type=jnp.float32)


def pieces(value):
    high = value.astype(jnp.bfloat16)
    rest = value - high.astype(jnp.float32)
    middle = rest.astype(jnp.bfloat16)
    low = (rest - middle.astype(jnp.float32)).astype(jnp.bfloat16)
    return high, middle, low


def exact_dot(left, value):
    cols = value.shape[1]
    out = dot16(left, jnp.concatenate(pieces(value), axis=1))
    return out[:, :cols] + (out[:, cols : 2 * cols] + out[:, 2 * cols :])


def six(value, left):
    high, middle, low = pieces(value)
    if left:
        return jnp.concatenate([high, high, high, middle, middle, low], axis=1)
    return jnp.concatenate([high, middle, low, high, middle, high], axis=0)


def kernel(
    gx,
    gy,
    rhs_hbm,
    schur_hbm,
    sdiag_hbm,
    trace_hbm,
    tdiag_hbm,
    coup_hbm,
    rows_hbm,
    defl_hbm,
    cinv_hbm,
    cmap_hbm,
    x_ref,
    res_ref,
    rhs_ref,
    sdiag_ref,
    trace_ref,
    tdiag_ref,
    coup_ref,
    rows_ref,
    defl_ref,
    cmap_ref,
    load_sem,
    sb_ref,
    pick_ref,
    v_ref,
    sd_ref,
    td_ref,
    d_ref,
    dh_ref,
    xh_ref,
    e_ref,
    last_ref,
    alpha_ref,
    solved_ref,
    dt_ref,
    dht_ref,
    both_ref,
    small_ref,
    main,
    sum_a,
    sum_b,
    extra,
    halo,
    halo_d,
    halo_d_out,
    halo_out,
    a_send,
    a_recv,
    b_send,
    b_recv,
    sa_send,
    sa_recv,
    sb_send,
    sb_recv,
    ea_send,
    ea_recv,
    eb_send,
    eb_recv,
    h_send,
    h_recv,
    hd_send,
    hd_recv,
):
    f32, bf16 = jnp.float32, jnp.bfloat16
    rows, src = rhs_ref.shape
    ov = rows_ref.shape[1]
    k = defl_ref.shape[0]
    nc = cmap_ref.shape[1]
    me_x, me_y = lax.axis_index("gx"), lax.axis_index("gy")
    iters = ITERS

    def load(i, source, target):
        copy = pltpu.make_async_copy(source, target, load_sem.at[i])
        copy.start()
        return copy

    load_defl = load(0, defl_hbm, defl_ref)
    load_cinv = load(1, cinv_hbm, extra.at[me_x, me_y, :, pl.ds(0, nc)])
    load_tdiag = load(2, tdiag_hbm, tdiag_ref)
    load_rhs = load(3, rhs_hbm, rhs_ref)
    load_trace = load(4, trace_hbm, trace_ref)
    load_rows = load(5, rows_hbm, rows_ref)
    load_cmap = load(6, cmap_hbm, cmap_ref)
    load_sdiag = load(7, sdiag_hbm, sdiag_ref)
    load_coup = load(8, coup_hbm, coup_ref)
    load_schur = load(9, schur_hbm, sb_ref.at[:, pl.ds(0, rows)])

    chips = gx // 2 * gy
    core = lax.rem(me_x, 2)
    sibling = me_x + 1 - 2 * core
    chip = lax.div(me_x, 2) * gy + me_y
    others = [lax.rem(chip + step, chips) for step in range(1, chips)]
    others = [(2 * lax.div(other, gy) + core, lax.rem(other, gy)) for other in others]
    beside = lax.rem(me_x + gx - 1 + 2 * core, gx)
    along_y = [lax.rem(me_y + step, gy) for step in range(1, gy)]
    near = [
        (me_x > 0, (jnp.maximum(me_x - 1, 0), me_y)),
        (me_x < gx - 1, (jnp.minimum(me_x + 1, gx - 1), me_y)),
        (me_y > 0, (me_x, jnp.maximum(me_y - 1, 0))),
        (me_y < gy - 1, (me_x, jnp.minimum(me_y + 1, gy - 1))),
    ]

    for d in range(4):

        @pl.when(jnp.logical_not(near[d][0]))
        def _():
            halo[:, d, :, :] = jnp.zeros((iters, ov, src), f32)
            halo_d[d, :, :] = jnp.zeros((k, ov), f32)

    barrier = pltpu.get_barrier_semaphore()
    for device in others + [(sibling, me_y), (beside, me_y)]:
        pl.semaphore_signal(barrier, inc=1, device_id=device, device_id_type=MESH)

    def remote(source, target, send, recv, device):
        return pltpu.make_async_remote_copy(
            src_ref=source, dst_ref=target, send_sem=send, recv_sem=recv, device_id=device, device_id_type=MESH
        )

    def to_lines(ref, send, recv):
        return [remote(ref, ref, send.at[i], recv.at[i], (me_x, other)) for i, other in enumerate(along_y)]

    def to_others(ref, send, recv):
        return [remote(ref.at[chip], ref.at[chip], send, recv, device) for device in others]

    def all_others(ref, send, recv):
        blocks = ref.at[pl.ds(0, chips - 1)]
        return remote(blocks, blocks, send, recv, others[0])

    ahead = [lax.rem(me_x + 2 * step, gx) for step in range(1, gx // 2)]
    behind = [lax.rem(me_x + gx - 2 * step, gx) for step in range(1, gx // 2)]

    def to_chips(ref, send, recv):
        return [
            remote(ref.at[me_x], ref.at[me_x], send.at[i], recv.at[i], (other, me_y)) for i, other in enumerate(ahead)
        ]

    def to_sibling_one(ref, send, recv, i):
        at = gx // 2 - 1 + i
        block = ref.at[me_x if i == 0 else behind[i - 1]]
        return remote(block, block, send.at[at], recv.at[at], (sibling, me_y))

    def to_sibling(ref, send, recv):
        return [to_sibling_one(ref, send, recv, i) for i in range(gx // 2)]

    def spread(ref, send, recv):
        start(to_chips(ref, send, recv))
        to_sibling_one(ref, send, recv, 0).start()

    def pass_on(ref, send, recv):
        arrivals = to_chips(ref, send, recv)
        for arrival in arrivals:
            arrival.wait_send()
        for i, arrival in enumerate(arrivals):
            arrival.wait_recv()
            to_sibling_one(ref, send, recv, i + 1).start()

    def collect(ref, send, recv):
        wait(to_sibling(ref, send, recv))

    def start(copies):
        for copy in copies:
            copy.start()

    def wait(copies):
        for copy in copies:
            copy.wait_send()
        for copy in copies:
            copy.wait_recv()

    load_defl.wait()
    defl = defl_ref[...]
    defl_wide = defl.astype(f32)
    padded = jnp.concatenate([defl_wide, jnp.zeros((src - k, rows), f32)], axis=0).astype(bf16)
    extra[me_x, me_y, :, nc:] = lax.dot_general(
        defl, padded, (((1,), (1,)), ((), ())), preferred_element_type=f32
    )
    load_cinv.wait()
    pl.semaphore_wait(barrier, chips + 1)

    extra_a = to_lines(extra.at[me_x, me_y], ea_send, ea_recv)
    start(extra_a)

    load_tdiag.wait()
    load_trace.wait()
    with_trace = defl_wide * tdiag_ref[...] + dot16(defl, trace_ref[...])
    small_ref[...] = jnp.concatenate(
        [defl_wide] + [piece.astype(f32) for piece in pieces(with_trace)], axis=0
    ).astype(bf16)

    def start_coarse(t, rounded):
        out = dot16(small_ref[...], rounded)
        main[t, core, chip, 0:k, :] = out[0:k]
        main[t, core, chip, k : 2 * k, :] = out[k : 2 * k] + (out[2 * k : 3 * k] + out[3 * k : 4 * k])
        start(to_others(main.at[t, core], a_send.at[t], a_recv.at[t]))

    def swap_coarse(t):
        return remote(main.at[t, core], main.at[t, core], b_send.at[t], b_recv.at[t], (sibling, me_y))

    def forward_coarse(t):
        arrived = all_others(main.at[t, core], a_send.at[t], a_recv.at[t])
        arrived.wait_send()
        arrived.wait_recv()
        swap_coarse(t).start()

    def local_prec(rounded):
        return td_ref[...] * rounded.astype(f32) + dot16(trace_ref[...], rounded)

    def halo_copies(t, arriving):
        return [
            remote(
                halo_out.at[t, d],
                halo.at[t, d if arriving else d ^ 1],
                h_send.at[t, d],
                h_recv.at[t, d if arriving else d ^ 1],
                near[d][1],
            )
            for d in range(4)
        ]

    def send_halo(t, q):
        picked = exact_dot(pick_ref[...], q)
        for d in range(4):
            halo_out[t, d, :, :] = picked[d * ov : (d + 1) * ov]
        for d, copy in enumerate(halo_copies(t, False)):
            pl.when(near[d][0])(copy.start)

    def wait_halo(t):
        for d, copy in enumerate(halo_copies(t, True)):
            pl.when(near[d][0])(copy.wait)

    blocks = [(a, b) for a in range(gx) for b in range(gy)]

    def solve(t):
        swap_coarse(t).wait()
        coarse_all = jnp.concatenate([main[t, a % 2, a // 2 * gy + b, 0:k, :] for a, b in blocks], axis=0)
        dq_all = jnp.concatenate([main[t, a % 2, a // 2 * gy + b, k : 2 * k, :] for a, b in blocks], axis=0)
        both = dot16(both_ref[...], six(coarse_all, False))
        solved_ref[...] = both[0:nc]
        return both[0:nc], dq_all, dq_all + both[nc:]

    def solved_of(device):
        at = (device[0] * gy + device[1]) * k
        return jnp.concatenate(pieces(solved_ref[pl.ds(pl.multiple_of(at, k), k), :]), axis=0)

    def halo_mapped(t):
        return jnp.concatenate(
            [halo[t, d, :, :] + dot16(dht_ref[d, :, :], solved_of(near[d][1])) for d in range(4)], axis=0
        )

    load_rhs.wait()
    start_coarse(0, rhs_ref[...])
    wait(extra_a)
    spread(extra, eb_send, eb_recv)

    load_rows.wait()
    for d in range(4):
        wanted = jnp.transpose(jnp.broadcast_to(rows_ref[d : d + 1, :].astype(f32), (ov, ov)))
        wanted = jnp.concatenate([wanted] * (rows // ov), axis=1).astype(jnp.int32)
        hot = wanted == lax.broadcasted_iota(jnp.int32, (ov, rows), 1)
        pick_ref[d * ov : (d + 1) * ov, :] = jnp.where(hot, 1.0, 0.0).astype(bf16)
    for d in range(4):
        halo_d_out[d, :, :] = lax.dot_general(
            defl, pick_ref[d * ov : (d + 1) * ov, :], (((1,), (1,)), ((), ())), preferred_element_type=f32
        )
        copy = remote(halo_d_out.at[d], halo_d.at[d ^ 1], hd_send.at[d], hd_recv.at[d ^ 1], near[d][1])
        pl.when(near[d][0])(copy.start)

    def column_of(ref):
        return jnp.transpose(jnp.broadcast_to(ref[...], (src, rows)))

    td_ref[...] = column_of(tdiag_ref)
    q0 = local_prec(rhs_ref[...])
    send_halo(0, q0)
    pass_on(extra, eb_send, eb_recv)

    load_sdiag.wait()
    sd_ref[...] = column_of(sdiag_ref)
    load_coup.wait()
    for d in range(4):
        hot = rows_ref[d : d + 1, :] == lax.broadcasted_iota(jnp.int32, (rows, ov), 0)
        scattered = dot16(jnp.where(hot, -1.0, 0.0).astype(bf16), coup_ref[d, :, :])
        sb_ref[:, rows + d * ov : rows + (d + 1) * ov] = scattered.astype(bf16)
    dt_ref[...] = jnp.transpose(jnp.concatenate([defl_wide] * 3, axis=0)).astype(bf16)
    for d in range(4):
        arrival = remote(halo_d_out.at[d], halo_d.at[d], hd_send.at[d], hd_recv.at[d], near[d][1])
        pl.when(near[d][0])(arrival.wait)
        dht_ref[d, :, :] = jnp.transpose(jnp.concatenate([halo_d[d, :, :]] * 3, axis=0)).astype(bf16)
    forward_coarse(0)
    load_cmap.wait()
    order = cmap_ref[...] == lax.broadcasted_iota(jnp.int32, (nc, nc), 0)
    order = jnp.where(order, 1.0, 0.0).astype(bf16)

    collect(extra, eb_send, eb_recv)
    inverse = jnp.concatenate([extra[a, b, :, 0:nc] for a, b in blocks], axis=0)
    inverse = sum(dot16(piece, order) for piece in reversed(pieces(inverse)))
    gram = jnp.concatenate([extra[a, b, :, nc:] for a, b in blocks], axis=0)
    row = lax.broadcasted_iota(jnp.int32, (src, nc), 0)
    column = lax.broadcasted_iota(jnp.int32, (src, nc), 1)
    repeat = jnp.where(row == column % k, 1.0, 0.0).astype(bf16)
    gram = sum(dot16(piece, repeat) for piece in reversed(pieces(gram)))
    row = lax.broadcasted_iota(jnp.int32, (nc, nc), 0)
    column = lax.broadcasted_iota(jnp.int32, (nc, nc), 1)
    gram = jnp.where(row // k == column // k, gram, 0.0)
    both_ref[0:nc, :] = six(inverse, True)
    both_ref[nc:, :] = six(wide_dot(gram, inverse), True)

    x_ref[...] = jnp.zeros_like(x_ref)
    xh_ref[...] = jnp.zeros_like(xh_ref)
    d_ref[0, :, :] = jnp.zeros((rows, src), f32)
    dh_ref[0, :, :] = jnp.zeros((4 * ov, src), f32)
    alpha_ref[...] = jnp.zeros_like(alpha_ref)
    last_ref[...] = jnp.zeros_like(last_ref)
    load_schur.wait()
    wait_halo(0)
    solved, _, projected = solve(0)
    e_ref[...] = projected
    d_ref[1, :, :] = q0 + dot16(dt_ref[...], solved_of((me_x, me_y)))
    dh_ref[1, :, :] = halo_mapped(0)

    def schur(field, margin):
        v_ref[0:rows, :] = field.astype(bf16)
        v_ref[rows:, :] = margin.astype(bf16)
        return sd_ref[...] * v_ref[0:rows, :].astype(f32) + dot16(sb_ref[...], v_ref[...])

    def iteration(step, carry):
        t = step + 1
        now, other = t % 2, (t + 1) % 2
        more = t < iters
        rounded = schur(d_ref[now], dh_ref[now]).astype(bf16)
        start_coarse(t, rounded)
        q = local_prec(rounded)
        sum_a[t, chip, :, :] = jnp.concatenate(
            [
                jnp.sum(q * d_ref[now], axis=0, keepdims=True),
                jnp.sum(q * q, axis=0, keepdims=True),
                jnp.zeros((k - 2, src), f32),
            ],
            axis=0,
        )
        start(to_others(sum_a.at[t], sa_send.at[t], sa_recv.at[t]))
        x_ref[...] += alpha_ref[0:1, :] * d_ref[other]
        xh_ref[...] += alpha_ref[0:1, :] * dh_ref[other]
        e_ref[...] -= alpha_ref[0:1, :] * last_ref[...]
        pl.when(more)(lambda: send_halo(t, q))
        forward_coarse(t)
        arrived = all_others(sum_a.at[t], sa_send.at[t], sa_recv.at[t])
        arrived.wait_send()
        arrived.wait_recv()
        total = sum_a[t, 0, :, :]
        for i in range(1, chips):
            total = total + sum_a[t, i, :, :]
        sum_b[t, core, :, :] = total
        swap = remote(sum_b.at[t, core], sum_b.at[t, core], sb_send.at[t], sb_recv.at[t], (sibling, me_y))
        swap.start()
        pl.when(more)(lambda: wait_halo(t))
        solved, dq_all, projected = solve(t)
        numer = jnp.sum(solved * e_ref[...], axis=0, keepdims=True)
        denom = jnp.sum(solved * (dq_all + projected), axis=0, keepdims=True)
        swap.wait()
        total = sum_b[t, 0, :, :] + sum_b[t, 1, :, :]
        alpha = (total[0:1] + numer) / (total[1:2] + denom)
        alpha_ref[...] = jnp.broadcast_to(alpha, alpha_ref.shape)
        last_ref[...] = projected

        @pl.when(more)
        def _():
            d_ref[other, :, :] = d_ref[now] - alpha * (q + dot16(dt_ref[...], solved_of((me_x, me_y))))
            dh_ref[other, :, :] = dh_ref[now] - alpha * halo_mapped(t)

        return carry

    lax.fori_loop(0, iters, iteration, 0)
    x = x_ref[...] + alpha_ref[0:1, :] * d_ref[iters % 2]
    xh = xh_ref[...] + alpha_ref[0:1, :] * dh_ref[iters % 2]
    x_ref[...] = x
    res_ref[...] = rhs_ref[...].astype(f32) - schur(x, xh)


def hand_on(x_in, res_in, x_out, res_out, held, in_sem, out_sem):
    half = x_in.shape[0] // 2
    parts = [(i, j) for j in range(2) for i in range(2)]
    inward, outward = [], []
    for i, j in parts:
        source, target = (x_in, res_in)[i], (x_out, res_out)[i]
        here = pl.ds(j * half, half)
        inward.append(pltpu.make_async_copy(source.at[here], held.at[i, j], in_sem.at[i, j]))
        outward.append(pltpu.make_async_copy(held.at[i, j], target.at[here], out_sem.at[i, j]))
    for copy in inward:
        copy.start()
    for arrival, copy in zip(inward, outward):
        arrival.wait()
        copy.start()
    for copy in outward:
        copy.wait()


def one_kernel(gx, gy, *args):
    right_side, schur, sdiag, trace, tdiag, couplings, margin, deflation, inverse, coarse_map = args
    rows, src = right_side.shape[2:]
    ov = margin.shape[3]
    k = deflation.shape[2]
    nc = inverse.shape[1]
    f32, bf16 = jnp.float32, jnp.bfloat16
    rounds = ITERS + 1
    vmem, dma = pltpu.VMEM, pltpu.SemaphoreType.DMA
    x, residual = pl.pallas_call(
        functools.partial(kernel, gx, gy),
        out_shape=[jax.ShapeDtypeStruct((rows, src), f32)] * 2,
        in_specs=[pl.BlockSpec(memory_space=pl.ANY)] * 10,
        out_specs=[pl.BlockSpec(memory_space=pltpu.VMEM)] * 2,
        scratch_shapes=[
            vmem((rows, src), bf16),
            vmem((1, rows), f32),
            vmem((rows, rows), bf16),
            vmem((1, rows), f32),
            vmem((4, ov, ov), bf16),
            vmem((4, ov), jnp.int32),
            vmem((k, rows), bf16),
            vmem((1, nc), jnp.int32),
            dma((10,)),
            vmem((rows, rows + 4 * ov), bf16),
            vmem((4 * ov, rows), bf16),
            vmem((rows + 4 * ov, src), bf16),
            vmem((rows, src), f32),
            vmem((rows, src), f32),
            vmem((2, rows, src), f32),
            vmem((2, 4 * ov, src), f32),
            vmem((4 * ov, src), f32),
            vmem((nc, src), f32),
            vmem((nc, src), f32),
            vmem((8, src), f32),
            vmem((nc, src), f32),
            vmem((rows, 3 * k), bf16),
            vmem((4, ov, 3 * k), bf16),
            vmem((2 * nc, 6 * nc), bf16),
            vmem((4 * k, rows), bf16),
            vmem((rounds, 2, gx // 2 * gy, 2 * k, src), f32),
            vmem((rounds, gx // 2 * gy, k, src), f32),
            vmem((rounds, 2, k, src), f32),
            vmem((gx, gy, k, nc + src), f32),
            vmem((ITERS, 4, ov, src), f32),
            vmem((4, k, ov), f32),
            vmem((4, k, ov), f32),
            vmem((ITERS, 4, ov, src), f32),
            dma((rounds,)),
            dma((rounds,)),
            dma((rounds,)),
            dma((rounds,)),
            dma((rounds,)),
            dma((rounds,)),
            dma((rounds,)),
            dma((rounds,)),
            dma((gy - 1,)),
            dma((gy - 1,)),
            dma((gx - 1,)),
            dma((gx - 1,)),
            dma((ITERS, 4)),
            dma((ITERS, 4)),
            dma((4,)),
            dma((4,)),
        ],
        compiler_params=pltpu.CompilerParams(
            collective_id=0, has_side_effects=True, vmem_limit_bytes=60 * 1024 * 1024
        ),
        cost_estimate=pl.CostEstimate(flops=4_000_000_000, bytes_accessed=6_000_000, transcendentals=0),
    )(
        right_side[0, 0],
        schur[0, 0],
        sdiag[0],
        trace[0, 0],
        tdiag[0],
        couplings[0, 0],
        margin[0, 0],
        deflation[0, 0],
        inverse,
        coarse_map[None],
    )
    x, residual = pl.pallas_call(
        hand_on,
        out_shape=[jax.ShapeDtypeStruct((rows, src), f32)] * 2,
        in_specs=[pl.BlockSpec(memory_space=pl.ANY)] * 2,
        out_specs=[pl.BlockSpec(memory_space=pl.ANY)] * 2,
        compiler_params=pltpu.CompilerParams(vmem_limit_bytes=60 * 1024 * 1024),
        scratch_shapes=[vmem((2, 2, rows // 2, src), f32), dma((2, 2)), dma((2, 2))],
        cost_estimate=pl.CostEstimate(flops=0, bytes_accessed=16 * rows * src, transcendentals=0),
    )(x, residual)
    return x[None, None], residual[None, None]


def plan(gx, gy, *args):
    if gx % 2 == 0 and args[8].shape[1] <= REPLICATED_COARSE:
        return one_kernel(gx, gy, *args)
    return shards(*args)


def solution(mesh):
    return jax.shard_map(
        functools.partial(plan, mesh.shape["gx"], mesh.shape["gy"]),
        mesh=mesh,
        in_specs=(
            P("gx", "gy", None, None),
            P("gx", "gy", None, None),
            P("gx", "gy", None),
            P("gx", "gy", None, None),
            P("gx", "gy", None),
            P("gx", "gy", None, None, None),
            P("gx", "gy", None, None),
            P("gx", "gy", None, None),
            P(("gx", "gy"), None),
            P(),
        ),
        out_specs=(P("gx", "gy", None, None), P("gx", "gy", None, None)),
        check_vma=False,
    )
```

```python
import functools

import jax
import jax.numpy as jnp
from jax import lax
from jax.experimental import pallas as pl
from jax.experimental.pallas import tpu as pltpu
from jax.sharding import PartitionSpec as P

ITERS = 3


def from_behind(value, axis, steps):
    count = lax.axis_size(axis)
    leading, last = (max(0, -steps), min(count, count - steps))
    return lax.ppermute(value, axis, [(source, source + steps) for source in range(leading, last)])


def pass_columns(rows, offset):
    return from_behind(rows, "gx", offset)


def pass_lines(rows, offset):
    return from_behind(rows, "gy", offset)


def shards(
    right_side,
    schur_offdiag,
    schur_diag,
    trace_offdiag,
    trace_diag,
    couplings,
    margin_rows,
    deflation,
    coarse_inverse,
    coarse_map,
):
    rhs_wide = right_side[0, 0].astype(jnp.float32)
    schur_mat = schur_offdiag[0, 0]
    schur_scale = schur_diag[0, 0][:, None]
    trace_mat = trace_offdiag[0, 0]
    trace_scale = trace_diag[0, 0][:, None]
    coupling_blocks = couplings[0, 0]
    rows_lists = margin_rows[0, 0]
    flat_rows = rows_lists.reshape(-1)
    vectors = deflation[0, 0]
    vectors_wide = vectors.astype(jnp.float32).T
    coarse_cols = jnp.take(coarse_inverse, coarse_map, axis=1)

    def apply_schur(field):
        rounded = lax.optimization_barrier(field.astype(jnp.bfloat16))
        result = schur_scale * rounded.astype(jnp.float32) + jnp.dot(
            schur_mat, rounded, preferred_element_type=jnp.float32
        )
        sent_rows = rounded[rows_lists]
        received = jnp.stack(
            [
                pass_columns(sent_rows[1], 1),
                pass_columns(sent_rows[0], -1),
                pass_lines(sent_rows[3], 1),
                pass_lines(sent_rows[2], -1),
            ]
        )
        coupled = jnp.einsum(
            "dab,dbs->das", coupling_blocks, received, preferred_element_type=jnp.float32
        )
        return result.at[flat_rows].add(-coupled.reshape(-1, coupled.shape[-1]))

    def apply_prec(field):
        rounded = lax.optimization_barrier(field.astype(jnp.bfloat16))
        result = trace_scale * rounded.astype(jnp.float32) + jnp.dot(
            trace_mat, rounded, preferred_element_type=jnp.float32
        )
        coarse = jnp.dot(vectors, rounded, preferred_element_type=jnp.float32)
        stacked = lax.all_gather(coarse, ("gx", "gy"), axis=0, tiled=True)
        solved = jnp.dot(coarse_cols, stacked, precision=lax.Precision.HIGHEST)
        return result + jnp.dot(vectors_wide, solved, precision=lax.Precision.HIGHEST)

    solution = jnp.zeros(rhs_wide.shape, jnp.float32)
    direction = apply_prec(rhs_wide)
    for iteration in range(ITERS):
        image = apply_schur(direction)
        mapped = apply_prec(image)
        numer, denom = lax.psum(
            (jnp.sum(mapped * direction, axis=0), jnp.sum(mapped * mapped, axis=0)), ("gx", "gy")
        )
        alpha = numer / denom
        solution = solution + alpha * direction
        direction = direction - alpha * mapped
    residual = rhs_wide - apply_schur(solution)
    return (solution[None, None], residual[None, None])


MESH = pl.DeviceIdType.MESH
REPLICATED_COARSE = 512


def wide_dot(left, right):
    return jnp.dot(left, right, precision=lax.Precision.HIGHEST, preferred_element_type=jnp.float32)


def dot16(left, right):
    return jnp.dot(left, right, preferred_element_type=jnp.float32)


def pieces(value):
    high = value.astype(jnp.bfloat16)
    rest = value - high.astype(jnp.float32)
    middle = rest.astype(jnp.bfloat16)
    low = (rest - middle.astype(jnp.float32)).astype(jnp.bfloat16)
    return high, middle, low


def exact_dot(left, value):
    cols = value.shape[1]
    out = dot16(left, jnp.concatenate(pieces(value), axis=1))
    return out[:, :cols] + (out[:, cols : 2 * cols] + out[:, 2 * cols :])


def six(value, left):
    high, middle, low = pieces(value)
    if left:
        return jnp.concatenate([high, high, high, middle, middle, low], axis=1)
    return jnp.concatenate([high, middle, low, high, middle, high], axis=0)


def kernel(
    gx,
    gy,
    rhs_hbm,
    schur_hbm,
    sdiag_hbm,
    trace_hbm,
    tdiag_hbm,
    coup_hbm,
    rows_hbm,
    defl_hbm,
    cinv_hbm,
    cmap_hbm,
    x_ref,
    res_ref,
    rhs_ref,
    sdiag_ref,
    trace_ref,
    tdiag_ref,
    coup_ref,
    rows_ref,
    defl_ref,
    cmap_ref,
    load_sem,
    sb_ref,
    pick_ref,
    v_ref,
    sd_ref,
    td_ref,
    d_ref,
    dh_ref,
    xh_ref,
    e_ref,
    last_ref,
    alpha_ref,
    solved_ref,
    dt_ref,
    dht_ref,
    both_ref,
    small_ref,
    main,
    tail,
    extra,
    halo,
    halo_d,
    halo_d_out,
    halo_out,
    a_send,
    a_recv,
    b_send,
    b_recv,
    sa_send,
    sa_recv,
    sb_send,
    sb_recv,
    ea_send,
    ea_recv,
    eb_send,
    eb_recv,
    h_send,
    h_recv,
    hd_send,
    hd_recv,
):
    f32, bf16 = jnp.float32, jnp.bfloat16
    rows, src = rhs_ref.shape
    ov = rows_ref.shape[1]
    k = defl_ref.shape[0]
    nc = cmap_ref.shape[1]
    me_x, me_y = lax.axis_index("gx"), lax.axis_index("gy")
    iters = ITERS

    def load(i, source, target):
        copy = pltpu.make_async_copy(source, target, load_sem.at[i])
        copy.start()
        return copy

    load_defl = load(0, defl_hbm, defl_ref)
    load_cinv = load(1, cinv_hbm, extra.at[me_x, me_y, :, pl.ds(0, nc)])
    load_tdiag = load(2, tdiag_hbm, tdiag_ref)
    load_rhs = load(3, rhs_hbm, rhs_ref)
    load_trace = load(4, trace_hbm, trace_ref)
    load_rows = load(5, rows_hbm, rows_ref)
    load_cmap = load(6, cmap_hbm, cmap_ref)
    load_sdiag = load(7, sdiag_hbm, sdiag_ref)
    load_coup = load(8, coup_hbm, coup_ref)
    load_schur = load(9, schur_hbm, sb_ref.at[:, pl.ds(0, rows)])

    chips = gx // 2 * gy
    core = lax.rem(me_x, 2)
    sibling = me_x + 1 - 2 * core
    chip = lax.div(me_x, 2) * gy + me_y
    others = [lax.rem(chip + step, chips) for step in range(1, chips)]
    others = [(2 * lax.div(other, gy) + core, lax.rem(other, gy)) for other in others]
    beside = lax.rem(me_x + gx - 1 + 2 * core, gx)
    along_y = [lax.rem(me_y + step, gy) for step in range(1, gy)]
    near = [
        (me_x > 0, (jnp.maximum(me_x - 1, 0), me_y)),
        (me_x < gx - 1, (jnp.minimum(me_x + 1, gx - 1), me_y)),
        (me_y > 0, (me_x, jnp.maximum(me_y - 1, 0))),
        (me_y < gy - 1, (me_x, jnp.minimum(me_y + 1, gy - 1))),
    ]

    for d in range(4):

        @pl.when(jnp.logical_not(near[d][0]))
        def _():
            halo[:, d, :, :] = jnp.zeros((iters, ov, src), f32)
            halo_d[d, :, :] = jnp.zeros((k, ov), f32)

    barrier = pltpu.get_barrier_semaphore()
    for device in others + [(sibling, me_y), (beside, me_y)]:
        pl.semaphore_signal(barrier, inc=1, device_id=device, device_id_type=MESH)

    def remote(source, target, send, recv, device):
        return pltpu.make_async_remote_copy(
            src_ref=source, dst_ref=target, send_sem=send, recv_sem=recv, device_id=device, device_id_type=MESH
        )

    def to_lines(ref, send, recv):
        return [remote(ref, ref, send.at[i], recv.at[i], (me_x, other)) for i, other in enumerate(along_y)]

    def to_others(ref, send, recv):
        return [remote(ref.at[chip], ref.at[chip], send, recv, device) for device in others]

    def all_others(ref, send, recv):
        blocks = ref.at[pl.ds(0, chips - 1)]
        return remote(blocks, blocks, send, recv, others[0])

    ahead = [lax.rem(me_x + 2 * step, gx) for step in range(1, gx // 2)]
    behind = [lax.rem(me_x + gx - 2 * step, gx) for step in range(1, gx // 2)]

    def to_chips(ref, send, recv):
        return [
            remote(ref.at[me_x], ref.at[me_x], send.at[i], recv.at[i], (other, me_y)) for i, other in enumerate(ahead)
        ]

    def to_sibling_one(ref, send, recv, i):
        at = gx // 2 - 1 + i
        block = ref.at[me_x if i == 0 else behind[i - 1]]
        return remote(block, block, send.at[at], recv.at[at], (sibling, me_y))

    def to_sibling(ref, send, recv):
        return [to_sibling_one(ref, send, recv, i) for i in range(gx // 2)]

    def spread(ref, send, recv):
        start(to_chips(ref, send, recv))
        to_sibling_one(ref, send, recv, 0).start()

    def pass_on(ref, send, recv):
        arrivals = to_chips(ref, send, recv)
        for arrival in arrivals:
            arrival.wait_send()
        for i, arrival in enumerate(arrivals):
            arrival.wait_recv()
            to_sibling_one(ref, send, recv, i + 1).start()

    def collect(ref, send, recv):
        wait(to_sibling(ref, send, recv))

    def start(copies):
        for copy in copies:
            copy.start()

    def wait(copies):
        for copy in copies:
            copy.wait_send()
        for copy in copies:
            copy.wait_recv()

    load_defl.wait()
    defl = defl_ref[...]
    defl_wide = defl.astype(f32)
    padded = jnp.concatenate([defl_wide, jnp.zeros((src - k, rows), f32)], axis=0).astype(bf16)
    extra[me_x, me_y, :, nc:] = lax.dot_general(
        defl, padded, (((1,), (1,)), ((), ())), preferred_element_type=f32
    )
    load_cinv.wait()
    pl.semaphore_wait(barrier, chips + 1)

    extra_a = to_lines(extra.at[me_x, me_y], ea_send, ea_recv)
    start(extra_a)

    load_tdiag.wait()
    load_trace.wait()
    with_trace = defl_wide * tdiag_ref[...] + dot16(defl, trace_ref[...])
    small_ref[...] = jnp.concatenate(
        [defl_wide] + [piece.astype(f32) for piece in pieces(with_trace)], axis=0
    ).astype(bf16)

    def start_coarse(t, rounded):
        out = dot16(small_ref[...], rounded)
        main[t, core, chip, :, :] = out[0:k]
        tail[t, core, chip, 0:k, :] = out[k : 2 * k] + (out[2 * k : 3 * k] + out[3 * k : 4 * k])
        start(to_others(main.at[t, core], a_send.at[t], a_recv.at[t]))

    def start_tail(t, numer, denom):
        tail[t, core, chip, k : k + 1, :] = numer
        tail[t, core, chip, k + 1 : k + 2, :] = denom
        start(to_others(tail.at[t, core], sa_send.at[t], sa_recv.at[t]))

    def swap_coarse(t):
        return remote(main.at[t, core], main.at[t, core], b_send.at[t], b_recv.at[t], (sibling, me_y))

    def swap_tail(t):
        return remote(tail.at[t, core], tail.at[t, core], sb_send.at[t], sb_recv.at[t], (sibling, me_y))

    def forward(ref, send, recv, swap):
        arrived = all_others(ref, send, recv)
        arrived.wait_send()
        arrived.wait_recv()
        swap.start()

    def forward_coarse(t):
        forward(main.at[t, core], a_send.at[t], a_recv.at[t], swap_coarse(t))

    def forward_tail(t):
        forward(tail.at[t, core], sa_send.at[t], sa_recv.at[t], swap_tail(t))

    def local_prec(rounded):
        return td_ref[...] * rounded.astype(f32) + dot16(trace_ref[...], rounded)

    def halo_copies(t, arriving):
        return [
            remote(
                halo_out.at[t, d],
                halo.at[t, d if arriving else d ^ 1],
                h_send.at[t, d],
                h_recv.at[t, d if arriving else d ^ 1],
                near[d][1],
            )
            for d in range(4)
        ]

    def send_halo(t, q):
        picked = exact_dot(pick_ref[...], q)
        for d in range(4):
            halo_out[t, d, :, :] = picked[d * ov : (d + 1) * ov]
        for d, copy in enumerate(halo_copies(t, False)):
            pl.when(near[d][0])(copy.start)

    def wait_halo(t):
        for d, copy in enumerate(halo_copies(t, True)):
            pl.when(near[d][0])(copy.wait)

    blocks = [(a, b) for a in range(gx) for b in range(gy)]

    def solve(t):
        swap_coarse(t).wait()
        coarse_all = jnp.concatenate([main[t, a % 2, a // 2 * gy + b, :, :] for a, b in blocks], axis=0)
        both = dot16(both_ref[...], six(coarse_all, False))
        solved_ref[...] = both[0:nc]
        return both[0:nc], both[nc:]

    def tail_of(t, gram_solved):
        swap_tail(t).wait()
        dq_all = jnp.concatenate([tail[t, a % 2, a // 2 * gy + b, 0:k, :] for a, b in blocks], axis=0)
        return dq_all, dq_all + gram_solved

    def solved_of(device):
        at = (device[0] * gy + device[1]) * k
        return jnp.concatenate(pieces(solved_ref[pl.ds(pl.multiple_of(at, k), k), :]), axis=0)

    def halo_mapped(t):
        return jnp.concatenate(
            [halo[t, d, :, :] + dot16(dht_ref[d, :, :], solved_of(near[d][1])) for d in range(4)], axis=0
        )

    load_rhs.wait()
    start_coarse(0, rhs_ref[...])
    start_tail(0, jnp.zeros((1, src), f32), jnp.zeros((1, src), f32))
    wait(extra_a)
    spread(extra, eb_send, eb_recv)

    load_rows.wait()
    for d in range(4):
        wanted = jnp.transpose(jnp.broadcast_to(rows_ref[d : d + 1, :].astype(f32), (ov, ov)))
        wanted = jnp.concatenate([wanted] * (rows // ov), axis=1).astype(jnp.int32)
        hot = wanted == lax.broadcasted_iota(jnp.int32, (ov, rows), 1)
        pick_ref[d * ov : (d + 1) * ov, :] = jnp.where(hot, 1.0, 0.0).astype(bf16)
    for d in range(4):
        halo_d_out[d, :, :] = lax.dot_general(
            defl, pick_ref[d * ov : (d + 1) * ov, :], (((1,), (1,)), ((), ())), preferred_element_type=f32
        )
        copy = remote(halo_d_out.at[d], halo_d.at[d ^ 1], hd_send.at[d], hd_recv.at[d ^ 1], near[d][1])
        pl.when(near[d][0])(copy.start)

    def column_of(ref):
        return jnp.transpose(jnp.broadcast_to(ref[...], (src, rows)))

    td_ref[...] = column_of(tdiag_ref)
    q0 = local_prec(rhs_ref[...])
    send_halo(0, q0)
    pass_on(extra, eb_send, eb_recv)

    load_sdiag.wait()
    sd_ref[...] = column_of(sdiag_ref)
    load_coup.wait()
    for d in range(4):
        hot = rows_ref[d : d + 1, :] == lax.broadcasted_iota(jnp.int32, (rows, ov), 0)
        scattered = dot16(jnp.where(hot, -1.0, 0.0).astype(bf16), coup_ref[d, :, :])
        sb_ref[:, rows + d * ov : rows + (d + 1) * ov] = scattered.astype(bf16)
    dt_ref[...] = jnp.transpose(jnp.concatenate([defl_wide] * 3, axis=0)).astype(bf16)
    for d in range(4):
        arrival = remote(halo_d_out.at[d], halo_d.at[d], hd_send.at[d], hd_recv.at[d], near[d][1])
        pl.when(near[d][0])(arrival.wait)
        dht_ref[d, :, :] = jnp.transpose(jnp.concatenate([halo_d[d, :, :]] * 3, axis=0)).astype(bf16)
    forward_coarse(0)
    forward_tail(0)
    load_cmap.wait()
    order = cmap_ref[...] == lax.broadcasted_iota(jnp.int32, (nc, nc), 0)
    order = jnp.where(order, 1.0, 0.0).astype(bf16)

    collect(extra, eb_send, eb_recv)
    inverse = jnp.concatenate([extra[a, b, :, 0:nc] for a, b in blocks], axis=0)
    inverse = sum(dot16(piece, order) for piece in reversed(pieces(inverse)))
    gram = jnp.concatenate([extra[a, b, :, nc:] for a, b in blocks], axis=0)
    row = lax.broadcasted_iota(jnp.int32, (src, nc), 0)
    column = lax.broadcasted_iota(jnp.int32, (src, nc), 1)
    repeat = jnp.where(row == column % k, 1.0, 0.0).astype(bf16)
    gram = sum(dot16(piece, repeat) for piece in reversed(pieces(gram)))
    row = lax.broadcasted_iota(jnp.int32, (nc, nc), 0)
    column = lax.broadcasted_iota(jnp.int32, (nc, nc), 1)
    gram = jnp.where(row // k == column // k, gram, 0.0)
    both_ref[0:nc, :] = six(inverse, True)
    both_ref[nc:, :] = six(wide_dot(gram, inverse), True)

    x_ref[...] = jnp.zeros_like(x_ref)
    xh_ref[...] = jnp.zeros_like(xh_ref)
    d_ref[0, :, :] = jnp.zeros((rows, src), f32)
    dh_ref[0, :, :] = jnp.zeros((4 * ov, src), f32)
    alpha_ref[...] = jnp.zeros_like(alpha_ref)
    last_ref[...] = jnp.zeros_like(last_ref)
    load_schur.wait()
    wait_halo(0)
    _, projected = solve(0)
    e_ref[...] = tail_of(0, projected)[1]
    d_ref[1, :, :] = q0 + dot16(dt_ref[...], solved_of((me_x, me_y)))
    dh_ref[1, :, :] = halo_mapped(0)

    def schur(field, margin):
        v_ref[0:rows, :] = field.astype(bf16)
        v_ref[rows:, :] = margin.astype(bf16)
        return sd_ref[...] * v_ref[0:rows, :].astype(f32) + dot16(sb_ref[...], v_ref[...])

    def iteration(step, carry):
        t = step + 1
        now, other = t % 2, (t + 1) % 2
        more = t < iters
        rounded = schur(d_ref[now], dh_ref[now]).astype(bf16)
        start_coarse(t, rounded)
        q = local_prec(rounded)
        start_tail(t, jnp.sum(q * d_ref[now], axis=0, keepdims=True), jnp.sum(q * q, axis=0, keepdims=True))
        x_ref[...] += alpha_ref[0:1, :] * d_ref[other]
        xh_ref[...] += alpha_ref[0:1, :] * dh_ref[other]
        e_ref[...] -= alpha_ref[0:1, :] * last_ref[...]
        pl.when(more)(lambda: send_halo(t, q))
        forward_coarse(t)
        forward_tail(t)
        solved, gram_solved = solve(t)
        pl.when(more)(lambda: wait_halo(t))
        numer = jnp.sum(solved * e_ref[...], axis=0, keepdims=True)
        dq_all, projected = tail_of(t, gram_solved)
        denom = jnp.sum(solved * (dq_all + projected), axis=0, keepdims=True)
        total = tail[t, 0, 0, k:, :]
        for i in range(1, 2 * chips):
            total = total + tail[t, i // chips, i % chips, k:, :]
        alpha = (total[0:1] + numer) / (total[1:2] + denom)
        alpha_ref[...] = jnp.broadcast_to(alpha, alpha_ref.shape)
        last_ref[...] = projected

        @pl.when(more)
        def _():
            d_ref[other, :, :] = d_ref[now] - alpha * (q + dot16(dt_ref[...], solved_of((me_x, me_y))))
            dh_ref[other, :, :] = dh_ref[now] - alpha * halo_mapped(t)

        return carry

    lax.fori_loop(0, iters, iteration, 0)
    x = x_ref[...] + alpha_ref[0:1, :] * d_ref[iters % 2]
    xh = xh_ref[...] + alpha_ref[0:1, :] * dh_ref[iters % 2]
    x_ref[...] = x
    res_ref[...] = rhs_ref[...].astype(f32) - schur(x, xh)


def hand_on(x_in, res_in, x_out, res_out, sem):
    copies = [
        pltpu.make_async_copy(source, target, sem.at[i])
        for i, (source, target) in enumerate([(x_in, x_out), (res_in, res_out)])
    ]
    for copy in copies:
        copy.start()
    for copy in copies:
        copy.wait()


def one_kernel(gx, gy, *args):
    right_side, schur, sdiag, trace, tdiag, couplings, margin, deflation, inverse, coarse_map = args
    rows, src = right_side.shape[2:]
    ov = margin.shape[3]
    k = deflation.shape[2]
    nc = inverse.shape[1]
    f32, bf16 = jnp.float32, jnp.bfloat16
    rounds = ITERS + 1
    vmem, dma = pltpu.VMEM, pltpu.SemaphoreType.DMA
    x, residual = pl.pallas_call(
        functools.partial(kernel, gx, gy),
        out_shape=[jax.ShapeDtypeStruct((rows, src), f32)] * 2,
        in_specs=[pl.BlockSpec(memory_space=pl.ANY)] * 10,
        out_specs=[pl.BlockSpec(memory_space=pltpu.VMEM)] * 2,
        scratch_shapes=[
            vmem((rows, src), bf16),
            vmem((1, rows), f32),
            vmem((rows, rows), bf16),
            vmem((1, rows), f32),
            vmem((4, ov, ov), bf16),
            vmem((4, ov), jnp.int32),
            vmem((k, rows), bf16),
            vmem((1, nc), jnp.int32),
            dma((10,)),
            vmem((rows, rows + 4 * ov), bf16),
            vmem((4 * ov, rows), bf16),
            vmem((rows + 4 * ov, src), bf16),
            vmem((rows, src), f32),
            vmem((rows, src), f32),
            vmem((2, rows, src), f32),
            vmem((2, 4 * ov, src), f32),
            vmem((4 * ov, src), f32),
            vmem((nc, src), f32),
            vmem((nc, src), f32),
            vmem((8, src), f32),
            vmem((nc, src), f32),
            vmem((rows, 3 * k), bf16),
            vmem((4, ov, 3 * k), bf16),
            vmem((2 * nc, 6 * nc), bf16),
            vmem((4 * k, rows), bf16),
            vmem((rounds, 2, gx // 2 * gy, k, src), f32),
            vmem((rounds, 2, gx // 2 * gy, k + 2, src), f32),
            vmem((gx, gy, k, nc + src), f32),
            vmem((ITERS, 4, ov, src), f32),
            vmem((4, k, ov), f32),
            vmem((4, k, ov), f32),
            vmem((ITERS, 4, ov, src), f32),
            dma((rounds,)),
            dma((rounds,)),
            dma((rounds,)),
            dma((rounds,)),
            dma((rounds,)),
            dma((rounds,)),
            dma((rounds,)),
            dma((rounds,)),
            dma((gy - 1,)),
            dma((gy - 1,)),
            dma((gx - 1,)),
            dma((gx - 1,)),
            dma((ITERS, 4)),
            dma((ITERS, 4)),
            dma((4,)),
            dma((4,)),
        ],
        compiler_params=pltpu.CompilerParams(
            collective_id=0, has_side_effects=True, vmem_limit_bytes=60 * 1024 * 1024
        ),
        cost_estimate=pl.CostEstimate(flops=4_000_000_000, bytes_accessed=6_000_000, transcendentals=0),
    )(
        right_side[0, 0],
        schur[0, 0],
        sdiag[0],
        trace[0, 0],
        tdiag[0],
        couplings[0, 0],
        margin[0, 0],
        deflation[0, 0],
        inverse,
        coarse_map[None],
    )
    x, residual = pl.pallas_call(
        hand_on,
        out_shape=[jax.ShapeDtypeStruct((rows, src), f32)] * 2,
        in_specs=[pl.BlockSpec(memory_space=pl.ANY)] * 2,
        out_specs=[pl.BlockSpec(memory_space=pl.ANY)] * 2,
        compiler_params=pltpu.CompilerParams(vmem_limit_bytes=60 * 1024 * 1024),
        scratch_shapes=[dma((2,))],
        cost_estimate=pl.CostEstimate(flops=0, bytes_accessed=16 * rows * src, transcendentals=0),
    )(x, residual)
    return x[None, None], residual[None, None]


def plan(gx, gy, *args):
    if gx % 2 == 0 and args[8].shape[1] <= REPLICATED_COARSE:
        return one_kernel(gx, gy, *args)
    return shards(*args)


def solution(mesh):
    return jax.shard_map(
        functools.partial(plan, mesh.shape["gx"], mesh.shape["gy"]),
        mesh=mesh,
        in_specs=(
            P("gx", "gy", None, None),
            P("gx", "gy", None, None),
            P("gx", "gy", None),
            P("gx", "gy", None, None),
            P("gx", "gy", None),
            P("gx", "gy", None, None, None),
            P("gx", "gy", None, None),
            P("gx", "gy", None, None),
            P(("gx", "gy"), None),
            P(),
        ),
        out_specs=(P("gx", "gy", None, None), P("gx", "gy", None, None)),
        check_vma=False,
    )
```

```python
import functools

import jax
import jax.numpy as jnp
from jax import lax
from jax.experimental import pallas as pl
from jax.experimental.pallas import tpu as pltpu
from jax.sharding import PartitionSpec as P

ITERS = 3


def from_behind(value, axis, steps):
    count = lax.axis_size(axis)
    leading, last = (max(0, -steps), min(count, count - steps))
    return lax.ppermute(value, axis, [(source, source + steps) for source in range(leading, last)])


def pass_columns(rows, offset):
    return from_behind(rows, "gx", offset)


def pass_lines(rows, offset):
    return from_behind(rows, "gy", offset)


def shards(
    right_side,
    schur_offdiag,
    schur_diag,
    trace_offdiag,
    trace_diag,
    couplings,
    margin_rows,
    deflation,
    coarse_inverse,
    coarse_map,
):
    rhs_wide = right_side[0, 0].astype(jnp.float32)
    schur_mat = schur_offdiag[0, 0]
    schur_scale = schur_diag[0, 0][:, None]
    trace_mat = trace_offdiag[0, 0]
    trace_scale = trace_diag[0, 0][:, None]
    coupling_blocks = couplings[0, 0]
    rows_lists = margin_rows[0, 0]
    flat_rows = rows_lists.reshape(-1)
    vectors = deflation[0, 0]
    vectors_wide = vectors.astype(jnp.float32).T
    coarse_cols = jnp.take(coarse_inverse, coarse_map, axis=1)

    def apply_schur(field):
        rounded = lax.optimization_barrier(field.astype(jnp.bfloat16))
        result = schur_scale * rounded.astype(jnp.float32) + jnp.dot(
            schur_mat, rounded, preferred_element_type=jnp.float32
        )
        sent_rows = rounded[rows_lists]
        received = jnp.stack(
            [
                pass_columns(sent_rows[1], 1),
                pass_columns(sent_rows[0], -1),
                pass_lines(sent_rows[3], 1),
                pass_lines(sent_rows[2], -1),
            ]
        )
        coupled = jnp.einsum(
            "dab,dbs->das", coupling_blocks, received, preferred_element_type=jnp.float32
        )
        return result.at[flat_rows].add(-coupled.reshape(-1, coupled.shape[-1]))

    def apply_prec(field):
        rounded = lax.optimization_barrier(field.astype(jnp.bfloat16))
        result = trace_scale * rounded.astype(jnp.float32) + jnp.dot(
            trace_mat, rounded, preferred_element_type=jnp.float32
        )
        coarse = jnp.dot(vectors, rounded, preferred_element_type=jnp.float32)
        stacked = lax.all_gather(coarse, ("gx", "gy"), axis=0, tiled=True)
        solved = jnp.dot(coarse_cols, stacked, precision=lax.Precision.HIGHEST)
        return result + jnp.dot(vectors_wide, solved, precision=lax.Precision.HIGHEST)

    solution = jnp.zeros(rhs_wide.shape, jnp.float32)
    direction = apply_prec(rhs_wide)
    for iteration in range(ITERS):
        image = apply_schur(direction)
        mapped = apply_prec(image)
        numer, denom = lax.psum(
            (jnp.sum(mapped * direction, axis=0), jnp.sum(mapped * mapped, axis=0)), ("gx", "gy")
        )
        alpha = numer / denom
        solution = solution + alpha * direction
        direction = direction - alpha * mapped
    residual = rhs_wide - apply_schur(solution)
    return (solution[None, None], residual[None, None])


MESH = pl.DeviceIdType.MESH
REPLICATED_COARSE = 512


def wide_dot(left, right):
    return jnp.dot(left, right, precision=lax.Precision.HIGHEST, preferred_element_type=jnp.float32)


def dot16(left, right):
    return jnp.dot(left, right, preferred_element_type=jnp.float32)


def pieces(value):
    high = value.astype(jnp.bfloat16)
    rest = value - high.astype(jnp.float32)
    middle = rest.astype(jnp.bfloat16)
    low = (rest - middle.astype(jnp.float32)).astype(jnp.bfloat16)
    return high, middle, low


def exact_dot(left, value):
    cols = value.shape[1]
    out = dot16(left, jnp.concatenate(pieces(value), axis=1))
    return out[:, :cols] + (out[:, cols : 2 * cols] + out[:, 2 * cols :])


def six(value, left):
    high, middle, low = pieces(value)
    if left:
        return jnp.concatenate([high, high, high, middle, middle, low], axis=1)
    return jnp.concatenate([high, middle, low, high, middle, high], axis=0)


def kernel(
    gx,
    gy,
    rhs_hbm,
    schur_hbm,
    sdiag_hbm,
    trace_hbm,
    tdiag_hbm,
    coup_hbm,
    rows_hbm,
    defl_hbm,
    cinv_hbm,
    cmap_hbm,
    x_ref,
    res_ref,
    rhs_ref,
    sdiag_ref,
    trace_ref,
    tdiag_ref,
    coup_ref,
    rows_ref,
    defl_ref,
    cmap_ref,
    load_sem,
    sb_ref,
    pick_ref,
    v_ref,
    sd_ref,
    td_ref,
    d_ref,
    dh_ref,
    xh_ref,
    e_ref,
    last_ref,
    alpha_ref,
    solved_ref,
    dt_ref,
    dht_ref,
    both_ref,
    small_ref,
    main,
    tail,
    extra,
    halo,
    halo_d,
    halo_d_out,
    halo_out,
    a_send,
    a_recv,
    b_send,
    b_recv,
    sa_send,
    sa_recv,
    sb_send,
    sb_recv,
    ea_send,
    ea_recv,
    eb_send,
    eb_recv,
    h_send,
    h_recv,
    hd_send,
    hd_recv,
):
    f32, bf16 = jnp.float32, jnp.bfloat16
    rows, src = rhs_ref.shape
    ov = rows_ref.shape[1]
    k = defl_ref.shape[0]
    nc = cmap_ref.shape[1]
    me_x, me_y = lax.axis_index("gx"), lax.axis_index("gy")
    iters = ITERS

    def load(i, source, target):
        copy = pltpu.make_async_copy(source, target, load_sem.at[i])
        copy.start()
        return copy

    load_defl = load(0, defl_hbm, defl_ref)
    load_cinv = load(1, cinv_hbm, extra.at[me_x, me_y, :, pl.ds(0, nc)])
    load_tdiag = load(2, tdiag_hbm, tdiag_ref)
    load_rhs = load(3, rhs_hbm, rhs_ref)
    load_trace = load(4, trace_hbm, trace_ref)
    load_rows = load(5, rows_hbm, rows_ref)
    load_cmap = load(6, cmap_hbm, cmap_ref)
    load_sdiag = load(7, sdiag_hbm, sdiag_ref)
    load_coup = load(8, coup_hbm, coup_ref)
    load_schur = load(9, schur_hbm, sb_ref.at[:, pl.ds(0, rows)])

    chips = gx // 2 * gy
    core = lax.rem(me_x, 2)
    sibling = me_x + 1 - 2 * core
    chip = lax.div(me_x, 2) * gy + me_y
    others = [lax.rem(chip + step, chips) for step in range(1, chips)]
    others = [(2 * lax.div(other, gy) + core, lax.rem(other, gy)) for other in others]
    beside = lax.rem(me_x + gx - 1 + 2 * core, gx)
    along_y = [lax.rem(me_y + step, gy) for step in range(1, gy)]
    near = [
        (me_x > 0, (jnp.maximum(me_x - 1, 0), me_y)),
        (me_x < gx - 1, (jnp.minimum(me_x + 1, gx - 1), me_y)),
        (me_y > 0, (me_x, jnp.maximum(me_y - 1, 0))),
        (me_y < gy - 1, (me_x, jnp.minimum(me_y + 1, gy - 1))),
    ]

    for d in range(4):

        @pl.when(jnp.logical_not(near[d][0]))
        def _():
            halo[:, d, :, :] = jnp.zeros((iters, ov, src), f32)
            halo_d[d, :, :] = jnp.zeros((k, ov), f32)

    barrier = pltpu.get_barrier_semaphore()
    for device in others + [(sibling, me_y), (beside, me_y)]:
        pl.semaphore_signal(barrier, inc=1, device_id=device, device_id_type=MESH)

    def remote(source, target, send, recv, device):
        return pltpu.make_async_remote_copy(
            src_ref=source, dst_ref=target, send_sem=send, recv_sem=recv, device_id=device, device_id_type=MESH
        )

    def to_lines(ref, send, recv):
        return [remote(ref, ref, send.at[i], recv.at[i], (me_x, other)) for i, other in enumerate(along_y)]

    def to_others(ref, send, recv):
        return [remote(ref.at[chip], ref.at[chip], send, recv, device) for device in others]

    def all_others(ref, send, recv):
        blocks = ref.at[pl.ds(0, chips - 1)]
        return remote(blocks, blocks, send, recv, others[0])

    ahead = [lax.rem(me_x + 2 * step, gx) for step in range(1, gx // 2)]
    behind = [lax.rem(me_x + gx - 2 * step, gx) for step in range(1, gx // 2)]

    def to_chips(ref, send, recv):
        return [
            remote(ref.at[me_x], ref.at[me_x], send.at[i], recv.at[i], (other, me_y)) for i, other in enumerate(ahead)
        ]

    def to_sibling_one(ref, send, recv, i):
        at = gx // 2 - 1 + i
        block = ref.at[me_x if i == 0 else behind[i - 1]]
        return remote(block, block, send.at[at], recv.at[at], (sibling, me_y))

    def to_sibling(ref, send, recv):
        return [to_sibling_one(ref, send, recv, i) for i in range(gx // 2)]

    def spread(ref, send, recv):
        start(to_chips(ref, send, recv))
        to_sibling_one(ref, send, recv, 0).start()

    def pass_on(ref, send, recv):
        arrivals = to_chips(ref, send, recv)
        for arrival in arrivals:
            arrival.wait_send()
        for i, arrival in enumerate(arrivals):
            arrival.wait_recv()
            to_sibling_one(ref, send, recv, i + 1).start()

    def collect(ref, send, recv):
        wait(to_sibling(ref, send, recv))

    def start(copies):
        for copy in copies:
            copy.start()

    def wait(copies):
        for copy in copies:
            copy.wait_send()
        for copy in copies:
            copy.wait_recv()

    load_defl.wait()
    defl = defl_ref[...]
    defl_wide = defl.astype(f32)
    padded = jnp.concatenate([defl_wide, jnp.zeros((src - k, rows), f32)], axis=0).astype(bf16)
    extra[me_x, me_y, :, nc:] = lax.dot_general(
        defl, padded, (((1,), (1,)), ((), ())), preferred_element_type=f32
    )
    load_cinv.wait()
    pl.semaphore_wait(barrier, chips + 1)

    extra_a = to_lines(extra.at[me_x, me_y], ea_send, ea_recv)
    start(extra_a)

    load_tdiag.wait()
    load_trace.wait()
    with_trace = defl_wide * tdiag_ref[...] + dot16(defl, trace_ref[...])
    small_ref[...] = jnp.concatenate(
        [defl_wide] + [piece.astype(f32) for piece in pieces(with_trace)], axis=0
    ).astype(bf16)

    def start_coarse(t, rounded):
        out = dot16(small_ref[...], rounded)
        main[t, core, chip, :, :] = out[0:k]
        tail[t, core, chip, 0:k, :] = out[k : 2 * k] + (out[2 * k : 3 * k] + out[3 * k : 4 * k])
        start(to_others(main.at[t, core], a_send.at[t], a_recv.at[t]))

    def start_tail(t, numer, denom):
        tail[t, core, chip, k : k + 1, :] = numer
        tail[t, core, chip, k + 1 : k + 2, :] = denom
        start(to_others(tail.at[t, core], sa_send.at[t], sa_recv.at[t]))

    def swap_coarse(t):
        return remote(main.at[t, core], main.at[t, core], b_send.at[t], b_recv.at[t], (sibling, me_y))

    def swap_tail(t):
        return remote(tail.at[t, core], tail.at[t, core], sb_send.at[t], sb_recv.at[t], (sibling, me_y))

    def forward(ref, send, recv, swap):
        arrived = all_others(ref, send, recv)
        arrived.wait_send()
        arrived.wait_recv()
        swap.start()

    def forward_coarse(t):
        forward(main.at[t, core], a_send.at[t], a_recv.at[t], swap_coarse(t))

    def forward_tail(t):
        forward(tail.at[t, core], sa_send.at[t], sa_recv.at[t], swap_tail(t))

    def local_prec(rounded):
        return td_ref[...] * rounded.astype(f32) + dot16(trace_ref[...], rounded)

    def halo_copies(t, arriving):
        return [
            remote(
                halo_out.at[t, d],
                halo.at[t, d if arriving else d ^ 1],
                h_send.at[t, d],
                h_recv.at[t, d if arriving else d ^ 1],
                near[d][1],
            )
            for d in range(4)
        ]

    def send_halo(t, q):
        picked = exact_dot(pick_ref[...], q)
        for d in range(4):
            halo_out[t, d, :, :] = picked[d * ov : (d + 1) * ov]
        for d, copy in enumerate(halo_copies(t, False)):
            pl.when(near[d][0])(copy.start)

    def wait_halo(t):
        for d, copy in enumerate(halo_copies(t, True)):
            pl.when(near[d][0])(copy.wait)

    blocks = [(a, b) for a in range(gx) for b in range(gy)]

    def solve(t):
        swap_coarse(t).wait()
        coarse_all = jnp.concatenate([main[t, a % 2, a // 2 * gy + b, :, :] for a, b in blocks], axis=0)
        both = dot16(both_ref[...], six(coarse_all, False))
        solved_ref[...] = both[0:nc]
        return both[0:nc], both[nc:]

    def tail_of(t, gram_solved):
        swap_tail(t).wait()
        dq_all = jnp.concatenate([tail[t, a % 2, a // 2 * gy + b, 0:k, :] for a, b in blocks], axis=0)
        return dq_all, dq_all + gram_solved

    def solved_of(device):
        at = (device[0] * gy + device[1]) * k
        return jnp.concatenate(pieces(solved_ref[pl.ds(pl.multiple_of(at, k), k), :]), axis=0)

    def halo_mapped(t):
        return jnp.concatenate(
            [halo[t, d, :, :] + dot16(dht_ref[d, :, :], solved_of(near[d][1])) for d in range(4)], axis=0
        )

    load_rhs.wait()
    start_coarse(0, rhs_ref[...])
    start_tail(0, jnp.zeros((1, src), f32), jnp.zeros((1, src), f32))
    wait(extra_a)
    spread(extra, eb_send, eb_recv)

    load_rows.wait()
    for d in range(4):
        wanted = jnp.transpose(jnp.broadcast_to(rows_ref[d : d + 1, :].astype(f32), (ov, ov)))
        wanted = jnp.concatenate([wanted] * (rows // ov), axis=1).astype(jnp.int32)
        hot = wanted == lax.broadcasted_iota(jnp.int32, (ov, rows), 1)
        pick_ref[d * ov : (d + 1) * ov, :] = jnp.where(hot, 1.0, 0.0).astype(bf16)
    for d in range(4):
        halo_d_out[d, :, :] = lax.dot_general(
            defl, pick_ref[d * ov : (d + 1) * ov, :], (((1,), (1,)), ((), ())), preferred_element_type=f32
        )
        copy = remote(halo_d_out.at[d], halo_d.at[d ^ 1], hd_send.at[d], hd_recv.at[d ^ 1], near[d][1])
        pl.when(near[d][0])(copy.start)

    def column_of(ref):
        return jnp.transpose(jnp.broadcast_to(ref[...], (src, rows)))

    td_ref[...] = column_of(tdiag_ref)
    q0 = local_prec(rhs_ref[...])
    send_halo(0, q0)
    pass_on(extra, eb_send, eb_recv)

    load_sdiag.wait()
    sd_ref[...] = column_of(sdiag_ref)
    load_coup.wait()
    for d in range(4):
        hot = rows_ref[d : d + 1, :] == lax.broadcasted_iota(jnp.int32, (rows, ov), 0)
        scattered = dot16(jnp.where(hot, -1.0, 0.0).astype(bf16), coup_ref[d, :, :])
        sb_ref[:, rows + d * ov : rows + (d + 1) * ov] = scattered.astype(bf16)
    dt_ref[...] = jnp.transpose(jnp.concatenate([defl_wide] * 3, axis=0)).astype(bf16)
    for d in range(4):
        arrival = remote(halo_d_out.at[d], halo_d.at[d], hd_send.at[d], hd_recv.at[d], near[d][1])
        pl.when(near[d][0])(arrival.wait)
        dht_ref[d, :, :] = jnp.transpose(jnp.concatenate([halo_d[d, :, :]] * 3, axis=0)).astype(bf16)
    forward_coarse(0)
    forward_tail(0)
    load_cmap.wait()
    order = cmap_ref[...] == lax.broadcasted_iota(jnp.int32, (nc, nc), 0)
    order = jnp.where(order, 1.0, 0.0).astype(bf16)

    collect(extra, eb_send, eb_recv)
    inverse = jnp.concatenate([extra[a, b, :, 0:nc] for a, b in blocks], axis=0)
    inverse = sum(dot16(piece, order) for piece in reversed(pieces(inverse)))
    gram = jnp.concatenate([extra[a, b, :, nc:] for a, b in blocks], axis=0)
    row = lax.broadcasted_iota(jnp.int32, (src, nc), 0)
    column = lax.broadcasted_iota(jnp.int32, (src, nc), 1)
    repeat = jnp.where(row == column % k, 1.0, 0.0).astype(bf16)
    gram = sum(dot16(piece, repeat) for piece in reversed(pieces(gram)))
    row = lax.broadcasted_iota(jnp.int32, (nc, nc), 0)
    column = lax.broadcasted_iota(jnp.int32, (nc, nc), 1)
    gram = jnp.where(row // k == column // k, gram, 0.0)
    both_ref[0:nc, :] = six(inverse, True)
    both_ref[nc:, :] = six(wide_dot(gram, inverse), True)

    x_ref[...] = jnp.zeros_like(x_ref)
    xh_ref[...] = jnp.zeros_like(xh_ref)
    d_ref[0, :, :] = jnp.zeros((rows, src), f32)
    dh_ref[0, :, :] = jnp.zeros((4 * ov, src), f32)
    alpha_ref[...] = jnp.zeros_like(alpha_ref)
    last_ref[...] = jnp.zeros_like(last_ref)
    load_schur.wait()
    wait_halo(0)
    _, projected = solve(0)
    e_ref[...] = tail_of(0, projected)[1]
    d_ref[1, :, :] = q0 + dot16(dt_ref[...], solved_of((me_x, me_y)))
    dh_ref[1, :, :] = halo_mapped(0)

    def schur(field, margin):
        v_ref[0:rows, :] = field.astype(bf16)
        v_ref[rows:, :] = margin.astype(bf16)
        return sd_ref[...] * v_ref[0:rows, :].astype(f32) + dot16(sb_ref[...], v_ref[...])

    def iteration(step, carry):
        t = step + 1
        now, other = t % 2, (t + 1) % 2
        more = t < iters
        rounded = schur(d_ref[now], dh_ref[now]).astype(bf16)
        start_coarse(t, rounded)
        q = local_prec(rounded)
        start_tail(t, jnp.sum(q * d_ref[now], axis=0, keepdims=True), jnp.sum(q * q, axis=0, keepdims=True))
        x_ref[...] += alpha_ref[0:1, :] * d_ref[other]
        xh_ref[...] += alpha_ref[0:1, :] * dh_ref[other]
        e_ref[...] -= alpha_ref[0:1, :] * last_ref[...]
        pl.when(more)(lambda: send_halo(t, q))
        forward_coarse(t)
        forward_tail(t)
        solved, gram_solved = solve(t)
        pl.when(more)(lambda: wait_halo(t))
        numer = jnp.sum(solved * e_ref[...], axis=0, keepdims=True)
        dq_all, projected = tail_of(t, gram_solved)
        denom = jnp.sum(solved * (dq_all + projected), axis=0, keepdims=True)
        total = tail[t, 0, 0, k:, :]
        for i in range(1, 2 * chips):
            total = total + tail[t, i // chips, i % chips, k:, :]
        alpha = (total[0:1] + numer) / (total[1:2] + denom)
        alpha_ref[...] = jnp.broadcast_to(alpha, alpha_ref.shape)
        last_ref[...] = projected

        @pl.when(more)
        def _():
            d_ref[other, :, :] = d_ref[now] - alpha * (q + dot16(dt_ref[...], solved_of((me_x, me_y))))
            dh_ref[other, :, :] = dh_ref[now] - alpha * halo_mapped(t)

        return carry

    lax.fori_loop(0, iters, iteration, 0)
    x = x_ref[...] + alpha_ref[0:1, :] * d_ref[iters % 2]
    xh = xh_ref[...] + alpha_ref[0:1, :] * dh_ref[iters % 2]
    x_ref[...] = x
    res_ref[...] = rhs_ref[...].astype(f32) - schur(x, xh)


def hand_on(x_in, res_in, x_out, res_out, held, in_sem, out_sem):
    half = x_in.shape[0] // 2
    parts = [(i, j) for j in range(2) for i in range(2)]
    inward, outward = [], []
    for i, j in parts:
        source, target = (x_in, res_in)[i], (x_out, res_out)[i]
        here = pl.ds(j * half, half)
        inward.append(pltpu.make_async_copy(source.at[here], held.at[i, j], in_sem.at[i, j]))
        outward.append(pltpu.make_async_copy(held.at[i, j], target.at[here], out_sem.at[i, j]))
    for copy in inward:
        copy.start()
    for arrival, copy in zip(inward, outward):
        arrival.wait()
        copy.start()
    for copy in outward:
        copy.wait()


def one_kernel(gx, gy, *args):
    right_side, schur, sdiag, trace, tdiag, couplings, margin, deflation, inverse, coarse_map = args
    rows, src = right_side.shape[2:]
    ov = margin.shape[3]
    k = deflation.shape[2]
    nc = inverse.shape[1]
    f32, bf16 = jnp.float32, jnp.bfloat16
    rounds = ITERS + 1
    vmem, dma = pltpu.VMEM, pltpu.SemaphoreType.DMA
    x, residual = pl.pallas_call(
        functools.partial(kernel, gx, gy),
        out_shape=[jax.ShapeDtypeStruct((rows, src), f32)] * 2,
        in_specs=[pl.BlockSpec(memory_space=pl.ANY)] * 10,
        out_specs=[pl.BlockSpec(memory_space=pltpu.VMEM)] * 2,
        scratch_shapes=[
            vmem((rows, src), bf16),
            vmem((1, rows), f32),
            vmem((rows, rows), bf16),
            vmem((1, rows), f32),
            vmem((4, ov, ov), bf16),
            vmem((4, ov), jnp.int32),
            vmem((k, rows), bf16),
            vmem((1, nc), jnp.int32),
            dma((10,)),
            vmem((rows, rows + 4 * ov), bf16),
            vmem((4 * ov, rows), bf16),
            vmem((rows + 4 * ov, src), bf16),
            vmem((rows, src), f32),
            vmem((rows, src), f32),
            vmem((2, rows, src), f32),
            vmem((2, 4 * ov, src), f32),
            vmem((4 * ov, src), f32),
            vmem((nc, src), f32),
            vmem((nc, src), f32),
            vmem((8, src), f32),
            vmem((nc, src), f32),
            vmem((rows, 3 * k), bf16),
            vmem((4, ov, 3 * k), bf16),
            vmem((2 * nc, 6 * nc), bf16),
            vmem((4 * k, rows), bf16),
            vmem((rounds, 2, gx // 2 * gy, k, src), f32),
            vmem((rounds, 2, gx // 2 * gy, k + 2, src), f32),
            vmem((gx, gy, k, nc + src), f32),
            vmem((ITERS, 4, ov, src), f32),
            vmem((4, k, ov), f32),
            vmem((4, k, ov), f32),
            vmem((ITERS, 4, ov, src), f32),
            dma((rounds,)),
            dma((rounds,)),
            dma((rounds,)),
            dma((rounds,)),
            dma((rounds,)),
            dma((rounds,)),
            dma((rounds,)),
            dma((rounds,)),
            dma((gy - 1,)),
            dma((gy - 1,)),
            dma((gx - 1,)),
            dma((gx - 1,)),
            dma((ITERS, 4)),
            dma((ITERS, 4)),
            dma((4,)),
            dma((4,)),
        ],
        compiler_params=pltpu.CompilerParams(
            collective_id=0, has_side_effects=True, vmem_limit_bytes=60 * 1024 * 1024
        ),
        cost_estimate=pl.CostEstimate(flops=4_000_000_000, bytes_accessed=6_000_000, transcendentals=0),
    )(
        right_side[0, 0],
        schur[0, 0],
        sdiag[0],
        trace[0, 0],
        tdiag[0],
        couplings[0, 0],
        margin[0, 0],
        deflation[0, 0],
        inverse,
        coarse_map[None],
    )
    x, residual = pl.pallas_call(
        hand_on,
        out_shape=[jax.ShapeDtypeStruct((rows, src), f32)] * 2,
        in_specs=[pl.BlockSpec(memory_space=pl.ANY)] * 2,
        out_specs=[pl.BlockSpec(memory_space=pl.ANY)] * 2,
        compiler_params=pltpu.CompilerParams(vmem_limit_bytes=60 * 1024 * 1024),
        scratch_shapes=[vmem((2, 2, rows // 2, src), f32), dma((2, 2)), dma((2, 2))],
        cost_estimate=pl.CostEstimate(flops=0, bytes_accessed=16 * rows * src, transcendentals=0),
    )(x, residual)
    return x[None, None], residual[None, None]


def plan(gx, gy, *args):
    if gx % 2 == 0 and args[8].shape[1] <= REPLICATED_COARSE:
        return one_kernel(gx, gy, *args)
    return shards(*args)


def solution(mesh):
    return jax.shard_map(
        functools.partial(plan, mesh.shape["gx"], mesh.shape["gy"]),
        mesh=mesh,
        in_specs=(
            P("gx", "gy", None, None),
            P("gx", "gy", None, None),
            P("gx", "gy", None),
            P("gx", "gy", None, None),
            P("gx", "gy", None),
            P("gx", "gy", None, None, None),
            P("gx", "gy", None, None),
            P("gx", "gy", None, None),
            P(("gx", "gy"), None),
            P(),
        ),
        out_specs=(P("gx", "gy", None, None), P("gx", "gy", None, None)),
        check_vma=False,
    )
```
